32 devices in a mesh: dp: 4 (over x, core), ctx: 8 (over z, y).
Axes of the slice: x: 2, y: 2, z: 4, core: 2. Of those that a mesh axis runs over, the one named last changes fastest.
Arguments:
- hidden_in: bfloat16 [4, 4, 512, 1024], P(None, 'dp', 'ctx'), may hold values from -6 to 6
- segments: int32 [4, 4, 512], P(None, 'dp', 'ctx'), may hold values from 0 to 5, as said below
- attention_gain: bfloat16 [1024], P(('dp', 'ctx')), may hold values from 0.099609375 to 1.8984375
- query_gain: bfloat16 [128], P(('dp', 'ctx')), may hold values from 0.59765625 to 2
- key_gain: bfloat16 [128], P(('dp', 'ctx')), may hold values from 0.59765625 to 2
- query_weight: bfloat16 [1024, 2048], P(('dp', 'ctx')), may hold values from -0.1875 to 0.1875
- key_weight: bfloat16 [1024, 1024], P(('dp', 'ctx')), may hold values from -0.1875 to 0.1875
- value_weight: bfloat16 [1024, 1024], P(('dp', 'ctx')), may hold values from -0.1875 to 0.1875
- out_weight: bfloat16 [2048, 1024], P(None, ('dp', 'ctx')), may hold values from -0.75 to 0.75
- feedforward_gain: bfloat16 [1024], P(('dp', 'ctx')), may hold values from 0.099609375 to 1.8984375
- gate_weight: bfloat16 [1024, 3072], P(('dp', 'ctx')), may hold values from -0.1875 to 0.1875
- up_weight: bfloat16 [1024, 3072], P(('dp', 'ctx')), may hold values from -0.1875 to 0.1875
- down_weight: bfloat16 [3072, 1024], P(None, ('dp', 'ctx')), may hold values from -0.109375 to 0.109375
- cotangent: bfloat16 [4, 4, 512, 1024], P(None, 'dp', 'ctx'), may hold values from -6 to 6
Outputs:
- block_out: bfloat16 [4, 4, 512, 1024], P(None, 'dp', 'ctx')
- input_grad: float32 [4, 4, 512, 1024], P(None, 'dp', 'ctx')
- attention_gain_grad: float32 [1024], P(('dp', 'ctx'))
- query_gain_grad: float32 [128], P(('dp', 'ctx'))
- key_gain_grad: float32 [128], P(('dp', 'ctx'))
- query_weight_grad: float32 [1024, 2048], P(('dp', 'ctx'))
- key_weight_grad: float32 [1024, 1024], P(('dp', 'ctx'))
- value_weight_grad: float32 [1024, 1024], P(('dp', 'ctx'))
- out_weight_grad: float32 [2048, 1024], P(None, ('dp', 'ctx'))
- feedforward_gain_grad: float32 [1024], P(('dp', 'ctx'))
- gate_weight_grad: float32 [1024, 3072], P(('dp', 'ctx'))
- up_weight_grad: float32 [1024, 3072], P(('dp', 'ctx'))
- down_weight_grad: float32 [3072, 1024], P(None, ('dp', 'ctx'))
The draws below stay inside these ranges and needn't reach their ends.
Inputs may be any that keep to these rules, and one draw needn't show every extreme that they name: `segments`: along every sequence the segment number starts at 0 and rises by 0 or 1 from one token to the next. Of the 4 sequences that share an index of dp, one is a single document; each of the others holds exactly six documents.
All inputs are finite; a program needn't handle non-finite values.
Results may differ from the reference program's by a relative error of at most 0.019.
Values may be sent and summed in bfloat16 or wider, within the bound.
A program may use at most 256 MiB of HBM per device.

```python
import math
import jax
import jax.numpy as jnp
from jax import lax

D = 1024
HQ = 16
HK = 8
HD = 128
FF = 3072
MB = 4
SEQS_MB = 4
LENGTH = 512


def draw_segments(key, part):
    key = jax.random.fold_in(key, 11)
    order_key, pick_key = jax.random.split(key)
    count = MB * SEQS_MB
    row_keys = jax.random.split(order_key, count)
    chosen = jax.vmap(lambda row_key: jax.random.permutation(row_key, LENGTH - 1))(row_keys)[:, :5] + 1
    rows = jnp.arange(count, dtype=jnp.int32)[:, None]
    starts = jnp.zeros((count, LENGTH), jnp.int32).at[rows, chosen].set(1)
    numbers = jnp.cumsum(starts, axis=-1).reshape(MB, SEQS_MB, LENGTH)
    whole = jax.random.randint(pick_key, (1, SEQS_MB, 1), 0, MB)
    batch = jnp.arange(MB, dtype=jnp.int32).reshape(MB, 1, 1)
    return jnp.where(batch == whole, 0, numbers).astype(jnp.int32)


def spiked(drawn, stream_key, source, target, shards_of, factor):
    owner, partner = [(jnp.arange(drawn.shape[dim]) // (drawn.shape[dim] // shards_of)).reshape([-1 if axis == dim else 1 for axis in range(drawn.ndim)]) for dim in (source, target)]
    chosen = jax.random.permutation(stream_key, shards_of)[partner]
    strong = (owner == chosen) | (owner == (partner + shards_of // 2) % shards_of)
    return jnp.where(strong, factor * drawn, drawn)


def levels(own_key, dims, shards, smallest, largest):
    gain = 1.0
    for axis_at, parts in shards:
        steps = jax.random.uniform(jax.random.fold_in(jax.random.fold_in(own_key, 6), axis_at), (parts,), jnp.float32, smallest / len(shards), largest / len(shards))
        gain = gain * jnp.repeat(jnp.exp(steps), dims[axis_at] // parts).reshape((-1,) + (1,) * (len(dims) - 1 - axis_at))
    return gain


def bell_draw(own_key, dims, deviation, bound, shards=(), held_as=jnp.bfloat16):
    values = deviation * jax.random.normal(own_key, dims, jnp.float32)
    if shards:
        values = values * levels(own_key, dims, shards, -0.22, 0.18)
    return jnp.clip(values, -bound, bound).astype(held_as)


def bell_draw_with(stream_key, shape, deviation, bound, cuts, heavy, held_as=jnp.bfloat16):
    array = deviation * jax.random.normal(stream_key, shape, jnp.float32)
    if cuts:
        array = array * levels(stream_key, shape, cuts, -0.22, 0.18)
    return jnp.clip(spiked(array, jax.random.fold_in(stream_key, 3), *heavy), -bound, bound).astype(held_as)


def setup_inputs(seed: int = 0) -> dict:
    arg_keys = jax.random.split(jax.random.key(seed), 15)
    hidden_in = bell_draw(arg_keys[0], (MB, SEQS_MB, LENGTH, D), 1.0, 6.0, ((1, 4), (2, 8)))
    segments = draw_segments(jax.random.fold_in(arg_keys[14], 71), 0)
    attention_gain = jnp.clip(1.0 + 0.18 * jax.random.normal(arg_keys[2], (D,), jnp.float32), 0.099609375, 1.8984375).astype(jnp.bfloat16)
    query_gain = jnp.clip(0.59765625 + 1.4023438 * jax.random.uniform(arg_keys[3], (HD,), jnp.float32) ** levels(arg_keys[3], (HD,), ((0, 32),), -0.2, 0.2), 0.59765625, 2.0).astype(jnp.bfloat16)
    key_gain = jnp.clip(0.59765625 + 1.4023438 * jax.random.uniform(arg_keys[4], (HD,), jnp.float32) ** levels(arg_keys[4], (HD,), ((0, 32),), -0.2, 0.2), 0.59765625, 2.0).astype(jnp.bfloat16)
    query_weight = bell_draw(arg_keys[5], (D, HQ * HD), D ** -0.5, 0.1875, ((0, 32),))
    key_weight = bell_draw(arg_keys[6], (D, HK * HD), D ** -0.5, 0.1875, ((0, 32),))
    value_weight = bell_draw(arg_keys[7], (D, HK * HD), D ** -0.5, 0.1875, ((0, 32),))
    out_weight = bell_draw(arg_keys[8], (HQ * HD, D), (HQ * HD // 32) ** -0.5, 0.75, ((1, 32),))
    feedforward_gain = jnp.clip(1.0 + 0.18 * jax.random.normal(arg_keys[9], (D,), jnp.float32), 0.099609375, 1.8984375).astype(jnp.bfloat16)
    gate_weight = bell_draw(arg_keys[10], (D, FF), D ** -0.5, 0.1875, ((0, 32),))
    up_weight = bell_draw(arg_keys[11], (D, FF), D ** -0.5, 0.1875, ((0, 32),))
    down_weight = bell_draw(arg_keys[12], (FF, D), FF ** -0.5, 0.109375, ((1, 32),))
    cotangent = bell_draw_with(arg_keys[13], (MB, SEQS_MB, LENGTH, D), 1.0, 6.0, ((1, 4), (2, 8)), (2, 3, 8, 2.0))
    return {"hidden_in": hidden_in, "segments": segments, "attention_gain": attention_gain, "query_gain": query_gain, "key_gain": key_gain, "query_weight": query_weight, "key_weight": key_weight, "value_weight": value_weight, "out_weight": out_weight, "feedforward_gain": feedforward_gain, "gate_weight": gate_weight, "up_weight": up_weight, "down_weight": down_weight, "cotangent": cotangent}


@jax.custom_vjp
def low(v):
    return lax.optimization_barrier(v.astype(jnp.bfloat16)).astype(jnp.float32)

@jax.custom_vjp
def low_back(v):
    return v

def low_keep(v):
    return (low(v), None)

def low_pass(kept, grad):
    return (grad,)

def back_keep(v):
    return (v, None)

def back_low(kept, grad):
    return (low(grad),)
low.defvjp(low_keep, low_pass)
low_back.defvjp(back_keep, back_low)
NORM_EPS = 1e-06
ROPE_BASE = 1000000.0
MASKED = -1e+30
HIGHEST = lax.Precision.HIGHEST

def normalize(value):
    return value * lax.rsqrt(lax.optimization_barrier(jnp.mean(value * value, axis=-1, keepdims=True)) + NORM_EPS)

def product(left, right):
    return jnp.dot(left, right, precision=HIGHEST, preferred_element_type=jnp.float32)

def rope_tables():
    positions = jnp.arange(LENGTH, dtype=jnp.int32).astype(jnp.float32)
    frequency = ROPE_BASE ** (-(jnp.arange(HD // 2, dtype=jnp.float32) * 2.0) / HD)
    angles = positions[:, None] * frequency[None, :]
    cosine = jnp.concatenate([jnp.cos(angles), jnp.cos(angles)], axis=-1)
    sine = jnp.concatenate([jnp.sin(angles), jnp.sin(angles)], axis=-1)
    return (cosine[:, None, :], sine[:, None, :])

def rotate(value, cosine, sine):
    half = value.shape[-1] // 2
    turned = jnp.concatenate([-value[..., half:], value[..., :half]], axis=-1)
    return value * cosine + turned * sine

def attend_block(keys, values, segments, item):
    query_block, query_pos, query_seg = item
    size = query_block.shape[0]
    grouped = query_block.reshape(size, HK, HQ // HK, HD)
    raw = low_back(jnp.einsum('qkgd,skd->kgqs', grouped, keys, precision=HIGHEST) * HD ** (-0.5))
    key_pos = jnp.arange(LENGTH, dtype=jnp.int32)
    visible = (key_pos[None, :] <= query_pos[:, None]) & (segments[None, :] == query_seg[:, None])
    masked = jnp.where(visible, raw, MASKED)
    top = lax.optimization_barrier(jnp.max(masked, axis=-1, keepdims=True))
    lse = top + jnp.log(lax.optimization_barrier(jnp.sum(jnp.exp(masked - top), axis=-1, keepdims=True)))
    probs = low(jnp.exp(masked - lse))
    mixed = jnp.einsum('kgqs,skd->qkgd', probs, values, precision=HIGHEST)
    return mixed.reshape(size, HQ * HD)

def attend(queries, keys, values, segments):
    size = math.gcd(LENGTH, 512)
    count = LENGTH // size
    positions = jnp.arange(LENGTH, dtype=jnp.int32)
    items = (queries.reshape(count, size, HQ, HD), positions.reshape(count, size), segments.reshape(count, size))
    checked = jax.checkpoint(attend_block)
    mixed = lax.map(lambda item: checked(keys, values, segments, item), items)
    return mixed.reshape(LENGTH, HQ * HD)

def layer(hidden, segments, weights):
    attention_gain, query_gain, key_gain, query_weight, key_weight, value_weight, out_weight, feedforward_gain, gate_weight, up_weight, down_weight = weights
    cosine, sine = rope_tables()
    scaled_in = low(normalize(hidden) * attention_gain)
    query_acc = low_back(product(scaled_in, query_weight)).reshape(LENGTH, HQ, HD)
    key_acc = low_back(product(scaled_in, key_weight)).reshape(LENGTH, HK, HD)
    values = low_back(low(product(scaled_in, value_weight))).reshape(LENGTH, HK, HD)
    queries = low(rotate(normalize(query_acc) * query_gain, cosine, sine))
    keys = low(rotate(normalize(key_acc) * key_gain, cosine, sine))
    mixed = low_back(low(attend(queries, keys, values, segments)))
    residual = hidden + low_back(product(mixed, out_weight))
    ff_in = low(normalize(residual) * feedforward_gain)
    gate = low_back(product(ff_in, gate_weight))
    up = low_back(product(ff_in, up_weight))
    hidden_act = low(jax.nn.silu(gate) * up)
    return residual + product(hidden_act, down_weight)

def reference(hidden_in, segments, attention_gain, query_gain, key_gain, query_weight, key_weight, value_weight, out_weight, feedforward_gain, gate_weight, up_weight, down_weight, cotangent):
    weights = tuple((weight.astype(jnp.float32) for weight in (attention_gain, query_gain, key_gain, query_weight, key_weight, value_weight, out_weight, feedforward_gain, gate_weight, up_weight, down_weight)))
    count = MB * SEQS_MB
    inputs = hidden_in.reshape(count, LENGTH, D).astype(jnp.float32)
    documents = segments.reshape(count, LENGTH)
    grads_in = cotangent.reshape(count, LENGTH, D).astype(jnp.float32)

    def step(totals, item):
        hidden, seq_seg, grad_out = item
        result, pull = jax.vjp(lambda value, params: layer(value, seq_seg, params), hidden, weights)
        grad_hidden, grad_weights = pull(grad_out)
        totals = tuple((total + grad for total, grad in zip(totals, grad_weights)))
        return (totals, (result.astype(jnp.bfloat16), grad_hidden))
    zeros = tuple((jnp.zeros_like(weight) for weight in weights))
    totals, (results, grads) = lax.scan(step, zeros, (inputs, documents, grads_in))
    block_out = results.reshape(MB, SEQS_MB, LENGTH, D)
    input_grad = grads.reshape(MB, SEQS_MB, LENGTH, D)
    return (block_out, input_grad, totals[0], totals[1], totals[2], totals[3], totals[4], totals[5], totals[6], totals[7], totals[8], totals[9], totals[10])
```

```python
import functools
import types

import jax
import jax.numpy as jnp
from jax import lax
from jax.experimental import pallas as pl
from jax.experimental.pallas import tpu as pltpu
from jax.sharding import PartitionSpec as P

D = 1024
HQ = 16
HK = 8
HD = 128
FF = 3072
MB = 4

NORM_EPS = 1e-06
ROPE_BASE = 1000000.0
MASKED = -1e30
SCALE = HD ** (-0.5)
BF = jnp.bfloat16
F32 = jnp.float32
MESH = pl.DeviceIdType.MESH


def normalize(value):
    return value * lax.rsqrt(jnp.mean(value * value, axis=-1, keepdims=True) + NORM_EPS)


def norm_back(value, grad):
    scale = lax.rsqrt(jnp.mean(value * value, axis=-1, keepdims=True) + NORM_EPS)
    return scale * grad - value * (scale * scale * scale) * jnp.mean(
        grad * value, axis=-1, keepdims=True
    )


def rope_angles(first, count):
    positions = (first + jnp.arange(count, dtype=jnp.int32)).astype(F32)
    frequency = ROPE_BASE ** (-(jnp.arange(HD // 2, dtype=F32) * 2.0) / HD)
    return positions[:, None] * frequency[None, :]


WIDTHS = dict(
    e=128,
    k=HK * HD // 2,
    v=HK * HD // 2,
    q=HQ * HD // 2,
    o=HQ * HD // 2,
    g=FF // 2,
    u=FF // 2,
    d=FF // 2,
)
ORDER = tuple(WIDTHS)
HALF_HQ, HALF_HK = HQ // 2, HK // 2


def split_columns(name):
    width = WIDTHS[name]
    first = max(128, width // 2)
    return first, width - first


def dot(left, right):
    return jnp.dot(left, right, preferred_element_type=F32)


def dot_nt(left, right):
    return lax.dot_general(left, right, (((1,), (1,)), ((), ())), preferred_element_type=F32)


def dot_tn(left, right):
    return lax.dot_general(left, right, (((0,), (0,)), ((), ())), preferred_element_type=F32)


class Semaphores:
    def __init__(self):
        self.count = 0

    def take(self, number=1):
        first = self.count
        self.count += number
        return first


def layer_kernel(names, tokens, *refs):
    at = types.SimpleNamespace(**dict(zip(names, refs)))
    sends, recvs = at.sends, at.recvs
    places = Semaphores()
    dp, ctx = lax.axis_index("dp"), lax.axis_index("ctx")
    x, c = lax.div(dp, 2), lax.rem(dp, 2)
    z, y = lax.div(ctx, 2), lax.rem(ctx, 2)
    ox, oc, oy = 1 - x, 1 - c, 1 - y
    sibling = (2 * x + oc, ctx)
    x_next = (2 * ox + c, ctx)
    y_next = (dp, 2 * z + oy)
    length = 8 * tokens
    own_rows = 4 * tokens
    half = length // 2

    def z_at(step):
        return lax.rem(z + step, 4)

    def z_device(step):
        return (dp, 2 * z_at(step) + y)

    def remote(src, dst, place, device, recv_place=None):
        return pltpu.make_async_remote_copy(
            src_ref=src,
            dst_ref=dst,
            send_sem=sends.at[place],
            recv_sem=recvs.at[place if recv_place is None else recv_place],
            device_id=device,
            device_id_type=MESH,
        )

    def arrived(region, place, device):
        remote(region, region, place, device).wait_recv()

    barrier = pltpu.get_barrier_semaphore()
    me = c * 8 + ctx
    for other in range(1, 16):
        there = lax.rem(me + other, 16)
        pl.semaphore_signal(
            barrier, inc=1, device_id=(2 * x + lax.div(there, 8), lax.rem(there, 8)), device_id_type=MESH
        )
    pl.semaphore_signal(barrier, inc=1, device_id=x_next, device_id_type=MESH)
    pl.semaphore_wait(barrier, 16)

    weight = {n: getattr(at, "w_" + n) for n in ORDER}
    shard = {n: getattr(at, "in_" + n) for n in ORDER}
    s0 = {n: places.take() for n in ORDER}
    lc = {n: places.take() for n in ORDER}
    sz = {n: places.take(6) for n in ORDER}
    s2 = {n: places.take(2) for n in ORDER}
    s3 = {n: places.take(2) for n in ORDER}
    gather_sends = {n: [] for n in ORDER}

    def part(name, which):
        if name == "e":
            return shard[name]
        width = WIDTHS[name]
        return shard[name].at[:, pl.ds(pl.multiple_of(which * width, width), width)]

    def local(name):
        return pltpu.make_async_copy(part(name, c), weight[name].at[x, c, z, y], recvs.at[lc[name]])

    def begin(name, copy):
        copy.start()
        gather_sends[name].append(copy)

    def gather_core(name):
        begin(name, remote(part(name, oc), weight[name].at[x, c, z, y], s0[name], sibling))
        local(name).start()

    def gather_z_own(name):
        for step in (1, 2, 3):
            begin(
                name,
                remote(
                    part(name, c), weight[name].at[x, c, z, y], sz[name] + step - 1, z_device(step)
                ),
            )

    def gather_z_sibling(name):
        block = weight[name].at[x, oc, z, y]
        arrived(block, s0[name], sibling)
        for step in (1, 2, 3):
            begin(name, remote(block, block, sz[name] + 2 + step, z_device(step)))

    def gather_start(name):
        gather_core(name)
        gather_z_own(name)

    def gather_two(name):
        w = weight[name]
        local(name).wait()
        for step in (1, 2, 3):
            source = lax.rem(z + 4 - step, 4)
            device = (dp, 2 * source + y)
            arrived(w.at[x, c, source, y], sz[name] + step - 1, device)
            arrived(w.at[x, oc, source, y], sz[name] + 2 + step, device)
        first, second = split_columns(name)
        one = w.at[x, :, :, y, :, pl.ds(0, first)]
        begin(name, remote(one, one, s2[name], x_next))
        if second:
            two = w.at[x, :, :, y, :, pl.ds(first, second)]
            begin(name, remote(two, two, s2[name] + 1, y_next))

    def gather_three(name):
        w = weight[name]
        first, second = split_columns(name)
        arrived(w.at[ox, :, :, y, :, pl.ds(0, first)], s2[name], x_next)
        one = w.at[:, :, :, y, :, pl.ds(0, first)]
        begin(name, remote(one, one, s3[name], y_next))
        if second:
            arrived(w.at[x, :, :, oy, :, pl.ds(first, second)], s2[name] + 1, y_next)
            two = w.at[x, :, :, :, :, pl.ds(first, second)]
            begin(name, remote(two, two, s3[name] + 1, x_next))

    def gather_done(name):
        w = weight[name]
        first, second = split_columns(name)
        arrived(w.at[:, :, :, oy, :, pl.ds(0, first)], s3[name], y_next)
        if second:
            arrived(w.at[ox, :, :, :, :, pl.ds(first, second)], s3[name] + 1, x_next)

    def gather_sent(name):
        for copy in gather_sends[name]:
            copy.wait_send()

    slot = 2 * lax.rem(z, 2) + y
    target_core = lax.div(z, 2)

    class Reshard:
        def __init__(self, source, landing):
            self.source, self.landing = source, landing
            self.place, self.recv, self.own = places.take(4), places.take(4), places.take()

        def device(self, m):
            return (2 * x + target_core, 2 * m + c)

        def keeps(self, m):
            return (target_core == c) & (z == m) & (y == c)

        def copy(self, m):
            return remote(
                self.source.at[m], self.landing(target_core, slot), self.place + m, self.device(m), self.recv + slot
            )

        def keep(self, m):
            return pltpu.make_async_copy(
                self.source.at[m], self.landing(target_core, slot), recvs.at[self.own]
            )

        def start(self):
            for m in range(MB):
                pl.when(jnp.logical_not(self.keeps(m)))(lambda m=m: self.copy(m).start())
                pl.when(self.keeps(m))(lambda m=m: self.keep(m).start())

        def wait(self):
            for j in range(4):
                mine = (y == c) & (4 * c + j == ctx)
                region = self.landing(c, j)
                device = (2 * x + y, 4 * c + j)
                pl.when(jnp.logical_not(mine))(
                    lambda j=j, region=region, device=device: arrived(region, self.recv + j, device)
                )
                pl.when(mine)(
                    lambda region=region: pltpu.make_async_copy(
                        region, region, recvs.at[self.own]
                    ).wait()
                )

        def sent(self):
            for m in range(MB):
                pl.when(jnp.logical_not(self.keeps(m)))(lambda m=m: self.copy(m).wait_send())

    class Return:
        def __init__(self, source, landing):
            self.source, self.landing = source, landing
            self.place, self.recv, self.own = places.take(4), places.take(4), places.take()

        def keeps(self, j):
            return (y == c) & (4 * c + j == ctx)

        def copy(self, j):
            return remote(
                self.source.at[j], self.landing.at[z], self.place + j, (2 * x + y, 4 * c + j), self.recv + z
            )

        def keep(self, j):
            return pltpu.make_async_copy(
                self.source.at[j], self.landing.at[z], recvs.at[self.own]
            )

        def start(self, j):
            pl.when(jnp.logical_not(self.keeps(j)))(lambda: self.copy(j).start())
            pl.when(self.keeps(j))(lambda: self.keep(j).start())

        def finish(self):
            for j in range(4):
                pl.when(jnp.logical_not(self.keeps(j)))(lambda j=j: self.copy(j).wait_send())
                pl.when(self.keeps(j))(lambda j=j: self.keep(j).wait())
            for m in range(MB):
                mine = (target_core == c) & (z == m) & (y == c)
                device = (2 * x + target_core, 2 * m + c)
                pl.when(jnp.logical_not(mine))(
                    lambda m=m, device=device: arrived(self.landing.at[m], self.recv + m, device)
                )

    hidden_own, cot_all, seg_all = at.hidden_own, at.cot_all, at.seg_all
    hidden_move = Reshard(at.hidden_in, lambda core, j: hidden_own.at[j])
    cot_move = Reshard(at.cotangent, lambda core, j: cot_all.at[4 * core + j])
    out_move = Return(at.out_own, at.block_out)
    grad_move = Return(at.grad_own, at.input_grad)
    seg_place, seg_recv, seg_own = places.take(8), places.take(8), places.take()

    def seg_cases():
        for m in range(MB):
            for core in range(2):
                keeps = (core == c) & (z == m) & (y == c)
                yield m, core, keeps

    def seg_copy(m, core):
        return remote(
            at.segments.at[m], seg_all.at[ctx], seg_place + 2 * m + core, (2 * x + core, 2 * m + c), seg_recv + ctx
        )

    def seg_start():
        for m, core, keeps in seg_cases():
            pl.when(jnp.logical_not(keeps))(lambda m=m, core=core: seg_copy(m, core).start())
            pl.when(keeps)(
                lambda m=m: pltpu.make_async_copy(
                    at.segments.at[m], seg_all.at[ctx], recvs.at[seg_own]
                ).start()
            )

    def seg_wait():
        for m, core, keeps in seg_cases():
            pl.when(jnp.logical_not(keeps))(lambda m=m, core=core: seg_copy(m, core).wait_send())
        for j in range(8):
            mine = (y == c) & (ctx == j)
            pl.when(jnp.logical_not(mine))(
                lambda j=j: arrived(seg_all.at[j], seg_recv + j, (2 * x + y, j))
            )
            pl.when(mine)(
                lambda j=j: pltpu.make_async_copy(
                    seg_all.at[j], seg_all.at[j], recvs.at[seg_own]
                ).wait()
            )

    class Swap:
        def __init__(self, source, there, here):
            self.place = places.take()
            self.out = remote(source, there, self.place, sibling)
            self.here = here

        def start(self):
            self.out.start()

        def wait(self):
            self.out.wait_send()
            arrived(self.here, self.place, sibling)

    def swap_rows(ref):
        mine, theirs = ref.at[pl.ds(own_at, own_rows)], ref.at[pl.ds(other_at, own_rows)]
        return Swap(mine, mine, theirs)

    own_at = pl.multiple_of(c * own_rows, own_rows)
    other_at = pl.multiple_of(oc * own_rows, own_rows)
    partial_out, partial_in = at.partial_out, at.partial_in

    def swap_partial(index):
        landing = partial_in.at[index]
        return Swap(partial_out.at[index % 2], landing, landing)

    r1 = {n: places.take(2) for n in ORDER}
    r2 = {n: places.take(2) for n in ORDER}
    r3 = {n: places.take(3) for n in ORDER}
    r4 = {n: places.take() for n in ORDER}
    sum_sends = []

    def send(copy):
        copy.start()
        sum_sends.append(copy)

    def sum_one(name):
        w = weight[name]
        first, second = split_columns(name)
        send(remote(w.at[:, :, :, oy, :, pl.ds(0, first)], getattr(at, "r1a_" + name), r1[name], y_next))
        if second:
            send(remote(w.at[ox, :, :, :, :, pl.ds(first, second)], getattr(at, "r1b_" + name), r1[name] + 1, x_next))

    def sum_two(name):
        w = weight[name]
        first, second = split_columns(name)
        arrived(getattr(at, "r1a_" + name), r1[name], y_next)

        @pl.loop(0, 16)
        def _(i):
            xx, cc, zz = lax.div(i, 8), lax.rem(lax.div(i, 4), 2), lax.rem(i, 4)
            w[xx, cc, zz, y, :, pl.ds(0, first)] += getattr(at, "r1a_" + name)[xx, cc, zz]

        send(remote(w.at[ox, :, :, y, :, pl.ds(0, first)], getattr(at, "r2a_" + name), r2[name], x_next))
        if second:
            arrived(getattr(at, "r1b_" + name), r1[name] + 1, x_next)

            @pl.loop(0, 16)
            def _(i):
                cc, zz, yy = lax.div(i, 8), lax.rem(lax.div(i, 2), 4), lax.rem(i, 2)
                w[x, cc, zz, yy, :, pl.ds(first, second)] += getattr(at, "r1b_" + name)[cc, zz, yy]

            send(remote(w.at[x, :, :, oy, :, pl.ds(first, second)], getattr(at, "r2b_" + name), r2[name] + 1, y_next))

    def sum_three(name):
        w = weight[name]
        first, second = split_columns(name)
        arrived(getattr(at, "r2a_" + name), r2[name], x_next)
        if second:
            arrived(getattr(at, "r2b_" + name), r2[name] + 1, y_next)

        @pl.loop(0, 8)
        def _(i):
            cc, zz = lax.div(i, 4), lax.rem(i, 4)
            w[x, cc, zz, y, :, pl.ds(0, first)] += getattr(at, "r2a_" + name)[cc, zz]
            if second:
                w[x, cc, zz, y, :, pl.ds(first, second)] += getattr(at, "r2b_" + name)[cc, zz]

        for step in (1, 2, 3):
            send(
                remote(
                    w.at[x, :, z_at(step), y], getattr(at, "r3_" + name).at[step - 1], r3[name] + step - 1, z_device(step)
                )
            )

    def sum_four(name):
        w, landed = weight[name], getattr(at, "r3_" + name)
        for step in (1, 2, 3):
            arrived(landed.at[step - 1], r3[name] + step - 1, (dp, 2 * lax.rem(z + 4 - step, 4) + y))

        def total(core):
            value = w[x, core, z, y].astype(F32)
            for step in range(3):
                value = value + landed[step, core].astype(F32)
            return value

        width = WIDTHS[name]
        staged, result = getattr(at, "r4_" + name), getattr(at, "out_" + name)
        staged[...] = total(oc)
        if name == "e":
            send(remote(staged, at.r5_e, r4[name], sibling))
            result[...] = total(c)
        else:
            columns = pl.ds(pl.multiple_of(c * width, width), width)
            send(remote(staged, result.at[:, columns], r4[name], sibling))
            result[:, columns] = total(c)

    def sum_done(name):
        if name == "e":
            arrived(at.r5_e, r4[name], sibling)
            at.out_e[...] = at.out_e[...] + at.r5_e[...]
        else:
            width = WIDTHS[name]
            columns = pl.ds(pl.multiple_of(oc * width, width), width)
            arrived(getattr(at, "out_" + name).at[:, columns], r4[name], sibling)

    gains, head_gains = at.gains, at.head_gains
    scaled, ff_in, grad_proj = at.scaled, at.ff_in, at.grad_proj
    residual, grad_residual = at.residual, at.grad_residual
    acc_own = at.acc_own
    scaled_swap, ff_swap, proj_swap = swap_rows(scaled), swap_rows(ff_in), swap_rows(grad_proj)
    cot_swap = Swap(
        cot_all.at[pl.ds(4 * c, 4)], cot_all.at[pl.ds(4 * c, 4)], cot_all.at[pl.ds(4 * oc, 4)]
    )
    partials = [swap_partial(i) for i in range(4)]

    def selector():
        row = lax.broadcasted_iota(jnp.int32, (D, HD), 0)
        column = lax.broadcasted_iota(jnp.int32, (D, HD), 1)
        local_row = row & 31
        hit = ((row >> 5) * 4 + local_row == column) & (local_row < 4)
        return jnp.where(hit, 1.0, 0.0).astype(BF)

    def prepare_gains():
        columns = weight["e"][...].reshape(D, 128).astype(F32)
        for i in range(8):
            gains[:, i * 128 : (i + 1) * 128] = columns[i * 128 : (i + 1) * 128].T[:8]
        head_gains[...] = dot(gains[...].astype(BF), selector())

    def prepare_mask():
        rows = [seg_all[2 * j, 0:1] + seg_all[2 * j + 1, 0:1] for j in range(4)]
        for i in range(4):
            query = jnp.broadcast_to(rows[i], (128, 128)).T
            for j in range(4):
                place = slice(i * 128, (i + 1) * 128), slice(j * 128, (j + 1) * 128)
                if j > i:
                    at.bias[place] = jnp.full((128, 128), MASKED, F32)
                    continue
                seen = query == jnp.broadcast_to(rows[j], (128, 128))
                if i == j:
                    seen = seen & (
                        lax.broadcasted_iota(jnp.int32, (128, 128), 1)
                        <= lax.broadcasted_iota(jnp.int32, (128, 128), 0)
                    )
                at.bias[place] = jnp.where(seen, 0.0, MASKED)

    def own_block(j):
        return pl.ds(pl.multiple_of(c * own_rows + j * tokens, tokens), tokens)

    def here_block(j):
        return pl.ds(pl.multiple_of(j * tokens, tokens), tokens)

    def scale_input():
        @pl.loop(0, 4)
        def _(j):
            value = normalize(hidden_own[j].astype(F32)) * gains[0:1]
            scaled[own_block(j)] = value.astype(BF)

    def columns_of(name, t, size=256):
        return weight[name][:, :, :, :, :, pl.ds(pl.multiple_of(t * size, size), size)].reshape(D, size)

    def rows_of(name, t):
        return weight[name][lax.div(t, 2), lax.rem(t, 2)].reshape(D // 4, WIDTHS[name])

    cosine, sine = at.cosine, at.sine

    def turn(value):
        return value * cosine[...] + pltpu.roll(value, HD // 2, 1) * sine[...]

    def project_heads(name, gain, kept, turned):
        @pl.loop(0, WIDTHS[name] // 256)
        def _(t):
            both = dot(scaled[...], columns_of(name, t))
            for i in range(2):
                value = both[:, i * HD : (i + 1) * HD]
                kept[2 * t + i] = value
                turned[2 * t + i] = turn(normalize(value) * gain).astype(BF)

    def project_values():
        @pl.loop(0, WIDTHS["v"] // 256)
        def _(t):
            both = dot(scaled[...], columns_of("v", t))
            for i in range(2):
                at.values[2 * t + i] = both[:, i * HD : (i + 1) * HD].astype(BF)

    def probabilities(head, pair, block):
        rows = slice(block * half, (block + 1) * half)
        seen = slice(0, (block + 1) * half)
        scores = dot_nt(at.queries[head, rows], at.keys[pair, seen]) * SCALE + at.bias[rows, seen]
        terms = jnp.exp(scores - jnp.max(scores, axis=-1, keepdims=True))
        return terms * (1.0 / jnp.sum(terms, axis=-1, keepdims=True))

    def attend():
        @pl.loop(0, HALF_HQ)
        def _(head):
            pair = lax.div(head, 2)
            for block in range(2):
                seen = slice(0, (block + 1) * half)
                low = probabilities(head, pair, block).astype(BF)
                at.mixed[
                    block * half : (block + 1) * half, pl.ds(pl.multiple_of(head * HD, HD), HD)
                ] = dot(low, at.values[pair, seen]).astype(BF)

    def partial_product(index, terms):
        def rows_times(first, t):
            return sum(dot_nt(left[pl.ds(first, own_rows)], rows_of(name, t)) for left, name in terms)

        @pl.loop(0, 4)
        def _(t):
            columns = pl.ds(pl.multiple_of(t * (D // 4), D // 4), D // 4)
            partial_out[index % 2, :, columns] = rows_times(other_at, t).astype(BF)

        partials[index].start()

        @pl.loop(0, 4)
        def _(t):
            columns = pl.ds(pl.multiple_of(t * (D // 4), D // 4), D // 4)
            acc_own[:, columns] = rows_times(own_at, t)

    def own_sum(index, j):
        return acc_own[here_block(j)] + partial_in[index, here_block(j)].astype(F32)

    def add_residual():
        @pl.loop(0, 4)
        def _(j):
            value = hidden_own[j].astype(F32) + own_sum(0, j)
            residual[here_block(j)] = value
            ff_in[own_block(j)] = (normalize(value) * gains[1:2]).astype(BF)

    gate_part, up_part, hidden_low = at.gate_part, at.up_part, at.hidden_low

    def feed_forward():
        @pl.loop(0, WIDTHS["g"] // 256)
        def _(t):
            columns = pl.ds(pl.multiple_of(t * 256, 256), 256)
            gate = dot(ff_in[...], columns_of("g", t))
            up = dot(ff_in[...], columns_of("u", t))
            sigmoid = 1.0 / (1.0 + jnp.exp(-gate))
            swish = gate * sigmoid
            hidden_low[:, columns] = (swish * up).astype(BF)
            up_part[:, columns] = swish.astype(BF)
            gate_part[:, columns] = (up * sigmoid * (1.0 + gate * (1.0 - sigmoid))).astype(BF)

    def write_out():
        @pl.loop(0, 4)
        def _(j):
            at.out_own[j] = (residual[here_block(j)] + own_sum(1, j)).astype(BF)

        for j in range(4):
            out_move.start(j)

    def cotangent_rows():
        return cot_all[...].reshape(length, D)

    def grad_hidden():
        @pl.loop(0, WIDTHS["d"] // 256)
        def _(t):
            columns = pl.ds(pl.multiple_of(t * 256, 256), 256)
            grad = dot(cotangent_rows(), columns_of("d", t))
            gate_part[:, columns] = (grad * gate_part[:, columns].astype(F32)).astype(BF)
            up_part[:, columns] = (grad * up_part[:, columns].astype(F32)).astype(BF)

    turned_rows = at.turned_rows

    def transpose_rows(load):
        @pl.loop(0, D // 128)
        def _(t):
            turned_rows[pl.ds(pl.multiple_of(t * 128, 128), 128)] = load(
                pl.ds(pl.multiple_of(t * 128, 128), 128)
            ).T

    def weight_grad(name, right, first=0):
        gather_sent(name)

        @pl.loop(0, WIDTHS[name] // 256)
        def _(t):
            grad = dot(turned_rows[...], right[:, pl.ds(pl.multiple_of(first + t * 256, 256), 256)])
            weight[name][:, :, :, :, :, pl.ds(pl.multiple_of(t * 256, 256), 256)] = grad.astype(BF).reshape(
                2, 2, 4, 2, 32, 256
            )

    grad_gains = at.grad_gains

    def back_residual():
        grad_gains[...] = jnp.zeros_like(grad_gains)

        @pl.loop(0, 4)
        def _(j):
            value = residual[here_block(j)]
            grad = own_sum(2, j)
            scale = lax.rsqrt(jnp.mean(value * value, axis=-1, keepdims=True) + NORM_EPS)
            grad_gains[1:2] += jnp.sum(grad * (value * scale), axis=0, keepdims=True)
            total = cot_all[4 * c + j].astype(F32) + norm_back(value, grad * gains[1:2])
            grad_residual[here_block(j)] = total
            grad_proj[own_block(j)] = total.astype(BF)

    grad_mixed = gate_part

    def back_mixed():
        @pl.loop(0, WIDTHS["o"] // 256)
        def _(t):
            columns = pl.ds(pl.multiple_of(t * 256, 256), 256)
            grad_mixed[:, columns] = dot(grad_proj[...], columns_of("o", t)).astype(BF)

    grad_heads, grad_values = hidden_low, at.grad_values
    grad_head_gains = at.grad_head_gains

    def turn_back(value):
        return value * cosine[...] - pltpu.roll(value, HD // 2, 1) * sine[...]

    def back_head(value, grad, row, columns):
        scale = lax.rsqrt(jnp.mean(value * value, axis=-1, keepdims=True) + NORM_EPS)
        turned = turn_back(grad)
        grad_head_gains[row : row + 1] += jnp.sum(turned * (value * scale), axis=0, keepdims=True)
        grad_heads[:, columns] = norm_back(value, turned * head_gains[row : row + 1]).astype(BF)

    grad_key, grad_value, grad_query = at.grad_key, at.grad_value, at.grad_query

    def back_attend():
        grad_head_gains[...] = jnp.zeros_like(grad_head_gains)

        @pl.loop(0, HALF_HK)
        def _(pair):
            for i in range(2):
                head = 2 * pair + i
                lanes = pl.ds(pl.multiple_of(head * HD, HD), HD)
                for block in (1, 0):
                    rows = slice(block * half, (block + 1) * half)
                    seen = slice(0, (block + 1) * half)
                    probs = probabilities(head, pair, block)
                    grad_out = grad_mixed[rows, lanes]
                    grad_probs = dot_nt(grad_out, at.values[pair, seen])
                    delta = jnp.sum(probs * grad_probs, axis=-1, keepdims=True)
                    grad_scores = (probs * (grad_probs - delta)).astype(BF)
                    grad_query[rows] = dot(grad_scores, at.keys[pair, seen]) * SCALE
                    key_part = dot_tn(grad_scores, at.queries[head, rows]) * SCALE
                    value_part = dot_tn(probs.astype(BF), grad_out)
                    if i == 0 and block == 1:
                        grad_key[...] = key_part
                        grad_value[...] = value_part
                    else:
                        grad_key[seen] += key_part
                        grad_value[seen] += value_part
                back_head(at.query_acc[head], grad_query[...], 2, lanes)
            back_head(
                at.key_acc[pair],
                grad_key[...],
                3,
                pl.ds(pl.multiple_of(WIDTHS["q"] + pair * HD, HD), HD),
            )
            grad_values[:, pl.ds(pl.multiple_of(pair * HD, HD), HD)] = grad_value[...].astype(BF)

    def back_input():
        @pl.loop(0, 4)
        def _(j):
            value = hidden_own[j].astype(F32)
            grad = own_sum(3, j)
            scale = lax.rsqrt(jnp.mean(value * value, axis=-1, keepdims=True) + NORM_EPS)
            grad_gains[0:1] += jnp.sum(grad * (value * scale), axis=0, keepdims=True)
            at.grad_own[j] = (
                grad_residual[here_block(j)] + norm_back(value, grad * gains[0:1])
            ).astype(BF)

        for j in range(4):
            grad_move.start(j)

    def gain_grads():
        gather_sent("e")
        grad_gains[...] += dot_nt(grad_head_gains[...].astype(BF), selector())
        for i in range(8):
            block = jnp.concatenate(
                [grad_gains[:, i * 128 : (i + 1) * 128], jnp.zeros((120, 128), F32)], axis=0
            ).T
            weight["e"][i // 4, (i // 2) % 2, 2 * (i % 2) : 2 * (i % 2) + 2] = block.astype(BF).reshape(2, 2, 32, 128)

    for name in ("e", "k", "v"):
        gather_start(name)
    seg_start()
    hidden_move.start()
    for name in ("q", "o"):
        gather_start(name)
    for name in ("e", "k", "v"):
        gather_z_sibling(name)
    gather_two("e")
    gather_two("k")
    gather_three("e")
    gather_z_sibling("q")
    gather_two("v")
    gather_three("k")
    gather_done("e")
    prepare_gains()
    seg_wait()
    prepare_mask()
    hidden_move.wait()
    scale_input()
    scaled_swap.start()
    gather_start("g")
    gather_z_sibling("o")
    gather_two("q")
    gather_three("v")
    cot_move.start()
    gather_start("u")
    gather_z_sibling("g")
    gather_done("k")
    scaled_swap.wait()
    project_heads("k", head_gains[3:4], at.key_acc, at.keys)
    gather_two("o")
    gather_three("q")
    gather_start("d")
    gather_z_sibling("u")
    gather_done("v")
    project_values()
    gather_two("g")
    gather_three("o")
    gather_z_sibling("d")
    gather_done("q")
    project_heads("q", head_gains[2:3], at.query_acc, at.queries)
    cot_move.wait()
    cot_swap.start()
    gather_two("u")
    gather_three("g")
    attend()
    gather_two("d")
    gather_three("u")
    gather_done("o")
    partial_product(0, [(at.mixed, "o")])
    partials[0].wait()
    add_residual()
    ff_swap.start()
    gather_done("g")
    gather_done("u")
    gather_three("d")
    ff_swap.wait()
    feed_forward()
    cot_swap.wait()
    transpose_rows(lambda columns: cot_all[:, :, columns].reshape(length, 128))
    gather_done("d")

    partial_product(1, [(hidden_low, "d")])
    grad_hidden()
    weight_grad("d", hidden_low)
    sum_one("d")
    partials[1].wait()
    write_out()
    partial_product(2, [(gate_part, "g"), (up_part, "u")])
    transpose_rows(lambda columns: ff_in[:, columns])
    weight_grad("g", gate_part)
    sum_one("g")
    weight_grad("u", up_part)
    sum_one("u")
    partials[2].wait()
    back_residual()
    proj_swap.start()
    sum_two("d")
    proj_swap.wait()
    back_mixed()
    transpose_rows(lambda columns: grad_proj[:, columns])
    weight_grad("o", at.mixed)
    sum_one("o")
    back_attend()
    sum_three("d")
    sum_two("g")
    partial_product(3, [(grad_heads.at[:, pl.ds(0, WIDTHS["q"])], "q"),
                        (grad_heads.at[:, pl.ds(WIDTHS["q"], WIDTHS["k"])], "k"),
                        (grad_values, "v")])
    transpose_rows(lambda columns: scaled[:, columns])
    weight_grad("q", grad_heads)
    sum_one("q")
    weight_grad("k", grad_heads, WIDTHS["q"])
    sum_one("k")
    weight_grad("v", grad_values)
    sum_one("v")
    partials[3].wait()
    back_input()
    gain_grads()
    sum_one("e")
    sum_three("g")
    sum_two("u")
    sum_four("d")
    sum_three("u")
    sum_two("o")
    sum_four("g")
    sum_three("o")
    sum_two("q")
    sum_four("u")
    sum_three("q")
    sum_two("k")
    sum_four("o")
    sum_three("k")
    sum_two("v")
    sum_two("e")
    sum_three("v")
    sum_three("e")
    for name in ("q", "k", "v", "e"):
        sum_four(name)
    for name in ("d", "g", "u", "o", "q", "k", "v", "e"):
        sum_done(name)
    for copy in sum_sends:
        copy.wait_send()
    hidden_move.sent()
    cot_move.sent()
    out_move.finish()
    grad_move.finish()
    assert places.count <= SEMAPHORES, places.count


SEMAPHORES = 256


def fused(
    hidden_in,
    segments,
    attention_gain,
    query_gain,
    key_gain,
    query_weight,
    key_weight,
    value_weight,
    out_weight,
    feedforward_gain,
    gate_weight,
    up_weight,
    down_weight,
    cotangent,
):
    tokens = hidden_in.shape[2]
    length = 8 * tokens
    rows = query_weight.shape[0]
    odd = lax.rem(lax.axis_index("ctx"), 2)
    numbers = segments[:, 0].astype(F32)
    blank = jnp.zeros_like(numbers)
    numbers = jnp.where(
        odd == 0, jnp.concatenate([numbers, blank], axis=1), jnp.concatenate([blank, numbers], axis=1)
    )
    numbers = jnp.broadcast_to(numbers[:, None], (MB, 8, 2 * tokens))

    def column(gain):
        return jnp.pad(gain, (0, rows - gain.shape[0]))

    extra = jnp.stack(
        [attention_gain, feedforward_gain, column(query_gain), column(key_gain)], axis=1
    )
    extra = jnp.pad(extra, ((0, 0), (0, 124)))
    angles = rope_angles(0, length)
    cosine = jnp.concatenate([jnp.cos(angles), jnp.cos(angles)], axis=-1)
    sine = jnp.concatenate([-jnp.sin(angles), jnp.sin(angles)], axis=-1)

    vmem, anywhere = pl.BlockSpec(memory_space=pltpu.VMEM), pl.BlockSpec(memory_space=pl.ANY)
    inputs = dict(
        hidden_in=(hidden_in[:, 0], anywhere),
        cotangent=(cotangent[:, 0], anywhere),
        segments=(numbers, vmem),
        cosine=(cosine, vmem),
        sine=(sine, vmem),
        in_e=(extra, anywhere),
        in_k=(key_weight, anywhere),
        in_v=(value_weight, anywhere),
        in_q=(query_weight, anywhere),
        in_o=(out_weight.T, anywhere),
        in_g=(gate_weight, anywhere),
        in_u=(up_weight, anywhere),
        in_d=(down_weight.T, anywhere),
    )
    block = (MB, tokens, D)
    outputs = dict(block_out=(block, BF, anywhere), input_grad=(block, BF, anywhere))
    for name, width in WIDTHS.items():
        outputs["out_" + name] = ((rows, width if name == "e" else 2 * width), F32, vmem)
    own = 4 * tokens
    scratch = dict(
        hidden_own=((4, tokens, D), BF),
        cot_all=((8, tokens, D), BF),
        seg_all=((8, 8, 2 * tokens), F32),
        gains=((8, D), F32),
        head_gains=((8, HD), F32),
        grad_gains=((8, D), F32),
        grad_head_gains=((8, HD), F32),
        bias=((length, length), F32),
        scaled=((length, D), BF),
        query_acc=((HALF_HQ, length, HD), F32),
        key_acc=((HALF_HK, length, HD), F32),
        queries=((HALF_HQ, length, HD), BF),
        keys=((HALF_HK, length, HD), BF),
        values=((HALF_HK, length, HD), BF),
        mixed=((length, HALF_HQ * HD), BF),
        acc_own=((own, D), F32),
        partial_out=((2, own, D), BF),
        partial_in=((4, own, D), BF),
        residual=((own, D), F32),
        grad_residual=((own, D), F32),
        ff_in=((length, D), BF),
        gate_part=((length, FF // 2), BF),
        up_part=((length, FF // 2), BF),
        hidden_low=((length, FF // 2), BF),
        grad_proj=((length, D), BF),
        grad_values=((length, HALF_HK * HD), BF),
        grad_key=((length, HD), F32),
        grad_value=((length, HD), F32),
        grad_query=((length, HD), F32),
        turned_rows=((D, length), BF),
        out_own=((4, tokens, D), BF),
        grad_own=((4, tokens, D), BF),
        r5_e=((rows, 128), F32),
    )
    for name, width in WIDTHS.items():
        first, second = split_columns(name)
        scratch["w_" + name] = ((2, 2, 4, 2, rows, width), BF)
        scratch["r1a_" + name] = ((2, 2, 4, rows, first), BF)
        scratch["r2a_" + name] = ((2, 4, rows, first), BF)
        if second:
            scratch["r1b_" + name] = ((2, 4, 2, rows, second), BF)
            scratch["r2b_" + name] = ((2, 4, rows, second), BF)
        scratch["r3_" + name] = ((3, 2, rows, width), BF)
        scratch["r4_" + name] = ((rows, width), F32)
    names = (*inputs, *outputs, *scratch, "sends", "recvs")
    results = pl.pallas_call(
        functools.partial(layer_kernel, names, tokens),
        out_shape=[jax.ShapeDtypeStruct(shape, dtype) for shape, dtype, _ in outputs.values()],
        in_specs=[spec for _, spec in inputs.values()],
        out_specs=[spec for _, _, spec in outputs.values()],
        scratch_shapes=[pltpu.VMEM(shape, dtype) for shape, dtype in scratch.values()]
        + [pltpu.SemaphoreType.DMA((SEMAPHORES,))] * 2,
        compiler_params=pltpu.CompilerParams(
            collective_id=0, has_side_effects=True, vmem_limit_bytes=64 * 2**20 - 2**16
        ),
        name="layer",
    )(*(value for value, _ in inputs.values()))
    got = types.SimpleNamespace(**dict(zip(outputs, results)))
    gain_grads = got.out_e
    heads = query_gain.shape[0]
    return (
        got.block_out[:, None],
        got.input_grad.astype(F32)[:, None],
        gain_grads[:, 0],
        gain_grads[:heads, 2],
        gain_grads[:heads, 3],
        got.out_q,
        got.out_k,
        got.out_v,
        got.out_o.T,
        gain_grads[:, 1],
        got.out_g,
        got.out_u,
        got.out_d.T,
    )


def rope_tables(first, count):
    angles = rope_angles(first, count)
    cosine = jnp.concatenate([jnp.cos(angles), jnp.cos(angles)], axis=-1)
    sine = jnp.concatenate([jnp.sin(angles), jnp.sin(angles)], axis=-1)
    return (cosine[:, None, :], sine[:, None, :])


def rotate(value, cosine, sine):
    half = value.shape[-1] // 2
    turned = jnp.concatenate([-value[..., half:], value[..., :half]], axis=-1)
    return value * cosine + turned * sine


def rotate_back(grad, cosine, sine):
    half = grad.shape[-1] // 2
    scaled = grad * sine
    return grad * cosine + jnp.concatenate([scaled[..., half:], -scaled[..., :half]], axis=-1)


def contract_last(left, right):
    return lax.dot_general(
        left, right, (((1,), (1,)), ((), ())), preferred_element_type=jnp.float32
    )


def contract_first(left, right):
    return lax.dot_general(
        left, right, (((0,), (0,)), ((), ())), preferred_element_type=jnp.float32
    )


def block_rows(rows):
    size = min(rows, 512)
    while rows % size:
        size -= 1
    return size


def over_blocks(state, pieces, update):
    rows = pieces[0].shape[0]
    size = block_rows(rows)
    count = rows // size
    stacked = tuple((piece.reshape((count, size) + piece.shape[1:]) for piece in pieces))
    offsets = size * jnp.arange(count, dtype=jnp.int32)

    def step(current, item):
        block = item[:-1]
        offset = item[-1]
        current = update(current, block, offset)
        return (current, None)

    final, unused = lax.scan(step, state, stacked + (offsets,))
    return final


def general(
    hidden_in,
    segments,
    attention_gain,
    query_gain,
    key_gain,
    query_weight,
    key_weight,
    value_weight,
    out_weight,
    feedforward_gain,
    gate_weight,
    up_weight,
    down_weight,
    cotangent,
):
    tokens = hidden_in.shape[2]
    groups = HQ // HK
    scale = HD ** (-0.5)
    first = lax.axis_index("ctx") * tokens
    length = lax.axis_size("ctx") * tokens
    query_pos = first + jnp.arange(tokens, dtype=jnp.int32)
    cosine, sine = rope_tables(first, tokens)
    sources = (
        query_weight,
        key_weight,
        value_weight,
        gate_weight,
        up_weight,
        out_weight.T,
        down_weight.T,
    )
    whole = lax.all_gather(jnp.concatenate(sources, axis=1), ("dp", "ctx"), axis=0, tiled=True)
    parts = []
    edge = 0
    for source in sources:
        parts.append(whole[:, edge : edge + source.shape[1]])
        edge = edge + source.shape[1]
    whole_query, whole_key, whole_value, whole_gate, whole_up, whole_out, whole_down = parts
    gain_in, gain_query, gain_key, gain_feed = (
        lax.all_gather(gain, ("dp", "ctx"), axis=0, tiled=True)
        for gain in (attention_gain, query_gain, key_gain, feedforward_gain)
    )
    grad_attention_gain = jnp.zeros((D,), jnp.float32)
    grad_feed_gain = jnp.zeros((D,), jnp.float32)
    grad_query_gain = jnp.zeros((HD,), jnp.float32)
    grad_key_gain = jnp.zeros((HD,), jnp.float32)
    outputs = []
    input_grads = []
    stored = []
    for batch in range(MB):
        hidden = hidden_in[batch, 0].astype(jnp.float32)
        query_seg = segments[batch, 0]
        grad_out = cotangent[batch, 0]
        normed = normalize(hidden)
        scaled_in = (normed * gain_in.astype(jnp.float32)).astype(jnp.bfloat16)
        query_heads = jnp.dot(scaled_in, whole_query, preferred_element_type=jnp.float32).reshape(
            tokens, HQ, HD
        )
        key_heads = jnp.dot(scaled_in, whole_key, preferred_element_type=jnp.float32).reshape(
            tokens, HK, HD
        )
        values = jnp.dot(scaled_in, whole_value, preferred_element_type=jnp.float32).astype(
            jnp.bfloat16
        )
        query_norm = normalize(query_heads)
        key_norm = normalize(key_heads)
        query_scale = gain_query.astype(jnp.float32)
        key_scale = gain_key.astype(jnp.float32)
        queries = rotate(query_norm * query_scale, cosine, sine).astype(jnp.bfloat16)
        keys_low = rotate(key_norm * key_scale, cosine, sine).astype(jnp.bfloat16)
        grouped = queries.reshape(tokens, HK, groups, HD)
        keys_flat = keys_low.reshape(tokens, HK * HD)

        def key_scores(keys, key_seg, offset):
            rows = keys.shape[0]
            shaped = keys.reshape(rows, HK, HD)
            raw = (
                jnp.einsum("qkgd,skd->kgqs", grouped, shaped, preferred_element_type=jnp.float32)
                * scale
            )
            key_pos = offset + jnp.arange(rows, dtype=jnp.int32)
            visible = (key_pos[None, :] <= query_pos[:, None]) & (
                key_seg[None, :] == query_seg[:, None]
            )
            return (jnp.where(visible, raw, MASKED), visible, shaped)

        def fold_with(update, state, pieces):
            return over_blocks(state, pieces, update)

        def add_lse(state, block, offset):
            keys, key_seg = block
            masked, visible, shaped = key_scores(keys, key_seg, offset)
            top, total = state
            new_top = jnp.maximum(top, jnp.max(masked, axis=-1))
            terms = jnp.where(visible, jnp.exp(masked - new_top[..., None]), 0.0)
            return (new_top, total * jnp.exp(top - new_top) + jnp.sum(terms, axis=-1))

        start_state = (
            jnp.full((HK, groups, tokens), MASKED, jnp.float32),
            jnp.zeros((HK, groups, tokens), jnp.float32),
        )
        top, total = fold_with(
            add_lse,
            start_state,
            (
                lax.all_gather(keys_flat, "ctx", axis=0, tiled=True),
                lax.all_gather(query_seg, "ctx", axis=0, tiled=True),
            ),
        )
        lse = top + jnp.log(total)

        def add_mixed(state, block, offset):
            keys, values_block, key_seg = block
            masked, visible, shaped = key_scores(keys, key_seg, offset)
            probs = jnp.exp(masked - lse[..., None]).astype(jnp.bfloat16)
            value_heads = values_block.reshape(values_block.shape[0], HK, HD)
            return state + jnp.einsum(
                "kgqs,skd->qkgd", probs, value_heads, preferred_element_type=jnp.float32
            )

        mixed = fold_with(
            add_mixed,
            jnp.zeros((tokens, HK, groups, HD), jnp.float32),
            (
                lax.all_gather(keys_flat, "ctx", axis=0, tiled=True),
                lax.all_gather(values, "ctx", axis=0, tiled=True),
                lax.all_gather(query_seg, "ctx", axis=0, tiled=True),
            ),
        )
        mixed_low = mixed.reshape(tokens, HQ * HD).astype(jnp.bfloat16)
        residual = hidden + contract_last(mixed_low, whole_out)
        feed_normed = normalize(residual)
        feed_scale = gain_feed.astype(jnp.float32)
        ff_in = (feed_normed * feed_scale).astype(jnp.bfloat16)
        gate = jnp.dot(ff_in, whole_gate, preferred_element_type=jnp.float32)
        up_part = jnp.dot(ff_in, whole_up, preferred_element_type=jnp.float32)
        sigmoid = jax.nn.sigmoid(gate)
        swish = gate * sigmoid
        hidden_low = (swish * up_part).astype(jnp.bfloat16)
        block_out = residual + contract_last(hidden_low, whole_down)
        outputs.append(block_out.astype(jnp.bfloat16))
        grad_hidden = jnp.dot(grad_out, whole_down, preferred_element_type=jnp.float32)
        grad_gate = (grad_hidden * up_part * (sigmoid * (1.0 + gate * (1.0 - sigmoid)))).astype(
            jnp.bfloat16
        )
        grad_up = (grad_hidden * swish).astype(jnp.bfloat16)
        grad_feed_in = contract_last(grad_gate, whole_gate) + contract_last(grad_up, whole_up)
        grad_feed_gain = grad_feed_gain + jnp.sum(grad_feed_in * feed_normed, axis=0)
        grad_residual = grad_out.astype(jnp.float32) + norm_back(
            residual, grad_feed_in * gain_feed.astype(jnp.float32)
        )
        grad_proj = grad_residual.astype(jnp.bfloat16)
        grad_mixed = (
            jnp.dot(grad_proj, whole_out, preferred_element_type=jnp.float32).astype(jnp.bfloat16).reshape(tokens, HK, groups, HD)
        )
        delta = jnp.transpose(jnp.sum(grad_mixed.astype(jnp.float32) * mixed, axis=-1), (1, 2, 0))

        def add_grads(state, block, offset):
            grad_query, grad_keys, grad_values = state
            keys, values_block, key_seg = block
            masked, visible, shaped = key_scores(keys, key_seg, offset)
            rows = keys.shape[0]
            probs = jnp.exp(masked - lse[..., None])
            probs_low = probs.astype(jnp.bfloat16)
            value_heads = values_block.reshape(rows, HK, HD)
            grad_probs = jnp.einsum(
                "qkgd,skd->kgqs", grad_mixed, value_heads, preferred_element_type=jnp.float32
            )
            grad_scores = (probs * (grad_probs - delta[..., None])).astype(jnp.bfloat16)
            grad_query = (
                grad_query
                + jnp.einsum(
                    "kgqs,skd->qkgd", grad_scores, shaped, preferred_element_type=jnp.float32
                )
                * scale
            )
            key_part = (
                jnp.einsum(
                    "kgqs,qkgd->skd", grad_scores, grouped, preferred_element_type=jnp.float32
                )
                * scale
            )
            value_part = jnp.einsum(
                "kgqs,qkgd->skd", probs_low, grad_mixed, preferred_element_type=jnp.float32
            )
            old_keys = lax.dynamic_slice_in_dim(grad_keys, offset, rows, 0)
            grad_keys = lax.dynamic_update_slice_in_dim(
                grad_keys, old_keys + key_part.reshape(rows, HK * HD), offset, 0
            )
            old_values = lax.dynamic_slice_in_dim(grad_values, offset, rows, 0)
            grad_values = lax.dynamic_update_slice_in_dim(
                grad_values, old_values + value_part.reshape(rows, HK * HD), offset, 0
            )
            return (grad_query, grad_keys, grad_values)

        back_state = (
            jnp.zeros((tokens, HK, groups, HD), jnp.float32),
            jnp.zeros((length, HK * HD), jnp.float32),
            jnp.zeros((length, HK * HD), jnp.float32),
        )
        grad_query, grad_keys_all, grad_values_all = fold_with(
            add_grads,
            back_state,
            (
                lax.all_gather(keys_flat, "ctx", axis=0, tiled=True),
                lax.all_gather(values, "ctx", axis=0, tiled=True),
                lax.all_gather(query_seg, "ctx", axis=0, tiled=True),
            ),
        )
        grad_keys_own, grad_values_own = (
            lax.psum_scatter(
                grad_keys_all.astype(jnp.bfloat16), "ctx", scatter_dimension=0, tiled=True
            ).astype(jnp.float32),
            lax.psum_scatter(
                grad_values_all.astype(jnp.bfloat16), "ctx", scatter_dimension=0, tiled=True
            ).astype(jnp.float32),
        )
        turned_query = rotate_back(grad_query.reshape(tokens, HQ, HD), cosine, sine)
        grad_query_gain = grad_query_gain + jnp.sum(turned_query * query_norm, axis=(0, 1))
        grad_query_low = (
            norm_back(query_heads, turned_query * gain_query.astype(jnp.float32))
            .reshape(tokens, HQ * HD)
            .astype(jnp.bfloat16)
        )
        turned_key = rotate_back(grad_keys_own.reshape(tokens, HK, HD), cosine, sine)
        grad_key_gain = grad_key_gain + jnp.sum(turned_key * key_norm, axis=(0, 1))
        grad_key_low = (
            norm_back(key_heads, turned_key * gain_key.astype(jnp.float32))
            .reshape(tokens, HK * HD)
            .astype(jnp.bfloat16)
        )
        grad_value_low = grad_values_own.astype(jnp.bfloat16)
        grad_scaled_in = (
            contract_last(grad_query_low, whole_query)
            + contract_last(grad_key_low, whole_key)
            + contract_last(grad_value_low, whole_value)
        )
        grad_attention_gain = grad_attention_gain + jnp.sum(grad_scaled_in * normed, axis=0)
        input_grads.append(
            grad_residual + norm_back(hidden, grad_scaled_in * gain_in.astype(jnp.float32))
        )
        stored.append(
            (
                scaled_in,
                grad_query_low,
                grad_key_low,
                grad_value_low,
                ff_in,
                grad_gate,
                grad_up,
                grad_proj,
                mixed_low,
                grad_out,
                hidden_low,
            )
        )
    columns = [jnp.concatenate([entry[index] for entry in stored], axis=0) for index in range(11)]
    (
        all_in,
        all_query,
        all_key,
        all_value,
        all_feed,
        all_gate,
        all_up,
        all_proj,
        all_mixed,
        all_out,
        all_hidden,
    ) = columns
    rows = query_weight.shape[0]
    head_rows = query_gain.shape[0]
    count = lax.axis_size(("dp", "ctx")) * rows
    row_ids = jnp.arange(count, dtype=jnp.int32)
    local = row_ids % rows
    place = jnp.clip(row_ids // rows * head_rows + local, 0, HD - 1)
    owned = local < head_rows
    gains = jnp.stack(
        [
            grad_attention_gain,
            grad_feed_gain,
            jnp.where(owned, jnp.take(grad_query_gain, place), 0.0),
            jnp.where(owned, jnp.take(grad_key_gain, place), 0.0),
        ],
        axis=1,
    )
    summed = lax.psum_scatter(
        jnp.concatenate(
            [
                contract_first(all_in, all_query).astype(BF),
                contract_first(all_in, all_key).astype(BF),
                contract_first(all_in, all_value).astype(BF),
                contract_first(all_feed, all_gate).astype(BF),
                contract_first(all_feed, all_up).astype(BF),
                contract_first(all_proj, all_mixed).astype(BF),
                contract_first(all_out, all_hidden).astype(BF),
                gains.astype(BF),
                jnp.zeros((count, 124), BF),
            ],
            axis=1,
        ),
        ("dp", "ctx"),
        scatter_dimension=0,
        tiled=True,
    ).astype(F32)
    widths = [HQ * HD, HK * HD, HK * HD, FF, FF, HQ * HD, FF, 128]
    pieces = []
    edge = 0
    for width in widths:
        pieces.append(summed[:, edge : edge + width])
        edge = edge + width
    gain_block = pieces[7]
    block_out = jnp.stack(outputs)[:, None]
    input_grad = jnp.stack(input_grads)[:, None]
    return (
        block_out,
        input_grad,
        gain_block[:, 0],
        gain_block[:head_rows, 2],
        gain_block[:head_rows, 3],
        pieces[0],
        pieces[1],
        pieces[2],
        pieces[5].T,
        gain_block[:, 1],
        pieces[3],
        pieces[4],
        pieces[6].T,
    )


def solution(mesh):
    shape = dict(mesh.shape)
    chips_hold_sequences = shape["dp"] == 4 and shape["ctx"] == 8

    def step(*arrays):
        if chips_hold_sequences and arrays[0].shape[2] == 64:
            return fused(*arrays)
        return general(*arrays)

    return jax.shard_map(
        step,
        mesh=mesh,
        in_specs=(
            P(None, "dp", "ctx", None),
            P(None, "dp", "ctx"),
            P(("dp", "ctx")),
            P(("dp", "ctx")),
            P(("dp", "ctx")),
            P(("dp", "ctx"), None),
            P(("dp", "ctx"), None),
            P(("dp", "ctx"), None),
            P(None, ("dp", "ctx")),
            P(("dp", "ctx")),
            P(("dp", "ctx"), None),
            P(("dp", "ctx"), None),
            P(None, ("dp", "ctx")),
            P(None, "dp", "ctx", None),
        ),
        out_specs=(
            P(None, "dp", "ctx", None),
            P(None, "dp", "ctx", None),
            P(("dp", "ctx")),
            P(("dp", "ctx")),
            P(("dp", "ctx")),
            P(("dp", "ctx"), None),
            P(("dp", "ctx"), None),
            P(("dp", "ctx"), None),
            P(None, ("dp", "ctx")),
            P(("dp", "ctx")),
            P(("dp", "ctx"), None),
            P(("dp", "ctx"), None),
            P(None, ("dp", "ctx")),
        ),
        check_vma=False,
    )
```

```python
import functools
import types

import jax
import jax.numpy as jnp
from jax import lax
from jax.experimental import pallas as pl
from jax.experimental.pallas import tpu as pltpu
from jax.sharding import PartitionSpec as P

D = 1024
HQ = 16
HK = 8
HD = 128
FF = 3072
MB = 4

NORM_EPS = 1e-06
ROPE_BASE = 1000000.0
MASKED = -1e30
SCALE = HD ** (-0.5)
BF = jnp.bfloat16
F32 = jnp.float32
MESH = pl.DeviceIdType.MESH


def normalize(value):
    return value * lax.rsqrt(jnp.mean(value * value, axis=-1, keepdims=True) + NORM_EPS)


def norm_back(value, grad):
    scale = lax.rsqrt(jnp.mean(value * value, axis=-1, keepdims=True) + NORM_EPS)
    return scale * grad - value * (scale * scale * scale) * jnp.mean(
        grad * value, axis=-1, keepdims=True
    )


def rope_angles(first, count):
    positions = (first + jnp.arange(count, dtype=jnp.int32)).astype(F32)
    frequency = ROPE_BASE ** (-(jnp.arange(HD // 2, dtype=F32) * 2.0) / HD)
    return positions[:, None] * frequency[None, :]


WIDTHS = dict(
    e=128,
    k=HK * HD // 2,
    v=HK * HD // 2,
    q=HQ * HD // 2,
    o=HQ * HD // 2,
    g=FF // 4,
    u=FF // 4,
    d=FF // 4,
)
ORDER = tuple(WIDTHS)
FEED = ("g", "u", "d")
GATHER_Y = dict(e=0, k=0, v=0, q=0, o=0)
SUM_Y = dict(e=128, k=256, v=256, q=512, o=512)
HALF_HQ, HALF_HK = HQ // 2, HK // 2


def split_columns(name, by):
    return by[name], WIDTHS[name] - by[name]


def dot(left, right):
    return jnp.dot(left, right, preferred_element_type=F32)


def dot_nt(left, right):
    return lax.dot_general(left, right, (((1,), (1,)), ((), ())), preferred_element_type=F32)


def dot_tn(left, right):
    return lax.dot_general(left, right, (((0,), (0,)), ((), ())), preferred_element_type=F32)


class Semaphores:
    def __init__(self):
        self.count = 0

    def take(self, number=1):
        first = self.count
        self.count += number
        return first


def layer_kernel(names, tokens, *refs):
    at = types.SimpleNamespace(**dict(zip(names, refs)))
    sends, recvs = at.sends, at.recvs
    places = Semaphores()
    dp, ctx = lax.axis_index("dp"), lax.axis_index("ctx")
    x, c = lax.div(dp, 2), lax.rem(dp, 2)
    z, y = lax.div(ctx, 2), lax.rem(ctx, 2)
    ox, oc, oy = 1 - x, 1 - c, 1 - y
    sibling = (2 * x + oc, ctx)
    x_next = (2 * ox + c, ctx)
    x_cross = (2 * ox + oc, ctx)
    y_next = (dp, 2 * z + oy)
    length = 8 * tokens
    own_rows = 4 * tokens
    half = length // 2

    def z_at(step):
        return lax.rem(z + step, 4)

    def z_device(step):
        return (dp, 2 * z_at(step) + y)

    def remote(src, dst, place, device, recv_place=None):
        return pltpu.make_async_remote_copy(
            src_ref=src,
            dst_ref=dst,
            send_sem=sends.at[place],
            recv_sem=recvs.at[place if recv_place is None else recv_place],
            device_id=device,
            device_id_type=MESH,
        )

    def arrived(region, place, device):
        remote(region, region, place, device).wait_recv()

    barrier = pltpu.get_barrier_semaphore()
    me = c * 8 + ctx
    for other in range(1, 16):
        there = lax.rem(me + other, 16)
        pl.semaphore_signal(
            barrier, inc=1, device_id=(2 * x + lax.div(there, 8), lax.rem(there, 8)), device_id_type=MESH
        )
    pl.semaphore_signal(barrier, inc=1, device_id=x_next, device_id_type=MESH)
    pl.semaphore_signal(barrier, inc=1, device_id=x_cross, device_id_type=MESH)
    pl.semaphore_wait(barrier, 17)

    weight = {n: getattr(at, "w_" + n) for n in ORDER}
    shard = {n: getattr(at, "in_" + n) for n in ORDER}
    s0 = {n: places.take(3) for n in ORDER}
    lc = {n: places.take() for n in ORDER}
    sz = {n: places.take(9) for n in ORDER}
    s2 = {n: places.take(2) for n in ORDER}
    s3 = {n: places.take(2) for n in ORDER}
    gather_sends = {n: [] for n in ORDER}

    def part(name, xx, cc):
        if name == "e":
            return shard[name]
        width = WIDTHS[name]
        which = 2 * xx + cc if name in FEED else cc
        return shard[name].at[:, pl.ds(pl.multiple_of(which * width, width), width)]

    def local(name):
        return pltpu.make_async_copy(part(name, x, c), weight[name].at[x, c, z, y], recvs.at[lc[name]])

    def begin(name, copy):
        copy.start()
        gather_sends[name].append(copy)

    def gather_core(name):
        here = weight[name].at[x, c, z, y]
        begin(name, remote(part(name, x, oc), here, s0[name], sibling))
        if name in FEED:
            begin(name, remote(part(name, ox, c), here, s0[name] + 1, x_next))
            begin(name, remote(part(name, ox, oc), here, s0[name] + 2, x_cross))
        local(name).start()

    def gather_z(name):
        w = weight[name]
        here = w.at[x, c, z, y]
        for step in (1, 2, 3):
            begin(name, remote(part(name, x, c), here, sz[name] + step - 1, z_device(step)))
        block = w.at[x, oc, z, y]
        arrived(block, s0[name], sibling)
        for step in (1, 2, 3):
            begin(name, remote(block, block, sz[name] + 2 + step, z_device(step)))
        if name in FEED:
            arrived(w.at[ox, c, z, y], s0[name] + 1, x_next)
            arrived(w.at[ox, oc, z, y], s0[name] + 2, x_cross)
            block = w.at[ox, :, z, y]
            for step in (1, 2, 3):
                begin(name, remote(block, block, sz[name] + 5 + step, z_device(step)))

    def gather_two(name):
        w = weight[name]
        local(name).wait()
        for step in (1, 2, 3):
            source = lax.rem(z + 4 - step, 4)
            device = (dp, 2 * source + y)
            arrived(w.at[x, c, source, y], sz[name] + step - 1, device)
            arrived(w.at[x, oc, source, y], sz[name] + 2 + step, device)
            if name in FEED:
                arrived(w.at[ox, :, source, y], sz[name] + 5 + step, device)
        if name in FEED:
            block = w.at[:, :, :, y]
            begin(name, remote(block, block, s2[name], y_next))
            return
        first, second = split_columns(name, GATHER_Y)
        if first:
            one = w.at[x, :, :, y, :, pl.ds(0, first)]
            begin(name, remote(one, one, s2[name], x_next))
        if second:
            two = w.at[x, :, :, y, :, pl.ds(first, second)]
            begin(name, remote(two, two, s2[name] + 1, y_next))

    def gather_three(name):
        w = weight[name]
        first, second = split_columns(name, GATHER_Y)
        if first:
            arrived(w.at[ox, :, :, y, :, pl.ds(0, first)], s2[name], x_next)
            one = w.at[:, :, :, y, :, pl.ds(0, first)]
            begin(name, remote(one, one, s3[name], y_next))
        if second:
            arrived(w.at[x, :, :, oy, :, pl.ds(first, second)], s2[name] + 1, y_next)
            two = w.at[x, :, :, :, :, pl.ds(first, second)]
            begin(name, remote(two, two, s3[name] + 1, x_next))

    def gather_done(name):
        w = weight[name]
        if name in FEED:
            arrived(w.at[:, :, :, oy], s2[name], y_next)
            return
        first, second = split_columns(name, GATHER_Y)
        if first:
            arrived(w.at[:, :, :, oy, :, pl.ds(0, first)], s3[name], y_next)
        if second:
            arrived(w.at[ox, :, :, :, :, pl.ds(first, second)], s3[name] + 1, x_next)

    def gather_sent(name):
        for copy in gather_sends[name]:
            copy.wait_send()

    slot = 2 * lax.rem(z, 2) + y
    target_core = lax.div(z, 2)

    class Reshard:
        def __init__(self, source, landing):
            self.source, self.landing = source, landing
            self.place, self.recv, self.own = places.take(4), places.take(4), places.take()

        def device(self, m):
            return (2 * x + target_core, 2 * m + c)

        def keeps(self, m):
            return (target_core == c) & (z == m) & (y == c)

        def copy(self, m):
            return remote(
                self.source.at[m], self.landing(target_core, slot), self.place + m, self.device(m), self.recv + slot
            )

        def keep(self, m):
            return pltpu.make_async_copy(
                self.source.at[m], self.landing(target_core, slot), recvs.at[self.own]
            )

        def start(self):
            for m in range(MB):
                pl.when(jnp.logical_not(self.keeps(m)))(lambda m=m: self.copy(m).start())
                pl.when(self.keeps(m))(lambda m=m: self.keep(m).start())

        def wait(self):
            for j in range(4):
                mine = (y == c) & (4 * c + j == ctx)
                region = self.landing(c, j)
                device = (2 * x + y, 4 * c + j)
                pl.when(jnp.logical_not(mine))(
                    lambda j=j, region=region, device=device: arrived(region, self.recv + j, device)
                )
                pl.when(mine)(
                    lambda region=region: pltpu.make_async_copy(
                        region, region, recvs.at[self.own]
                    ).wait()
                )

        def sent(self):
            for m in range(MB):
                pl.when(jnp.logical_not(self.keeps(m)))(lambda m=m: self.copy(m).wait_send())

    class Return:
        def __init__(self, source, landing):
            self.source, self.landing = source, landing
            self.place, self.recv, self.own = places.take(4), places.take(4), places.take()

        def keeps(self, j):
            return (y == c) & (4 * c + j == ctx)

        def copy(self, j):
            return remote(
                self.source.at[j], self.landing.at[z], self.place + j, (2 * x + y, 4 * c + j), self.recv + z
            )

        def keep(self, j):
            return pltpu.make_async_copy(
                self.source.at[j], self.landing.at[z], recvs.at[self.own]
            )

        def start(self, j):
            pl.when(jnp.logical_not(self.keeps(j)))(lambda: self.copy(j).start())
            pl.when(self.keeps(j))(lambda: self.keep(j).start())

        def finish(self):
            for j in range(4):
                pl.when(jnp.logical_not(self.keeps(j)))(lambda j=j: self.copy(j).wait_send())
                pl.when(self.keeps(j))(lambda j=j: self.keep(j).wait())
            for m in range(MB):
                mine = (target_core == c) & (z == m) & (y == c)
                device = (2 * x + target_core, 2 * m + c)
                pl.when(jnp.logical_not(mine))(
                    lambda m=m, device=device: arrived(self.landing.at[m], self.recv + m, device)
                )

    hidden_own, cot_all, seg_all = at.hidden_own, at.cot_all, at.seg_all
    hidden_move = Reshard(at.hidden_in, lambda core, j: hidden_own.at[j])
    cot_move = Reshard(at.cotangent, lambda core, j: cot_all.at[4 * (2 * x + core) + j])
    out_move = Return(at.out_own, at.block_out)
    grad_move = Return(at.grad_own, at.input_grad)
    seg_place, seg_recv, seg_own = places.take(8), places.take(8), places.take()

    def seg_cases():
        for m in range(MB):
            for core in range(2):
                keeps = (core == c) & (z == m) & (y == c)
                yield m, core, keeps

    def seg_copy(m, core):
        return remote(
            at.segments.at[m], seg_all.at[ctx], seg_place + 2 * m + core, (2 * x + core, 2 * m + c), seg_recv + ctx
        )

    def seg_start():
        for m, core, keeps in seg_cases():
            pl.when(jnp.logical_not(keeps))(lambda m=m, core=core: seg_copy(m, core).start())
            pl.when(keeps)(
                lambda m=m: pltpu.make_async_copy(
                    at.segments.at[m], seg_all.at[ctx], recvs.at[seg_own]
                ).start()
            )

    def seg_wait():
        for m, core, keeps in seg_cases():
            pl.when(jnp.logical_not(keeps))(lambda m=m, core=core: seg_copy(m, core).wait_send())
        for j in range(8):
            mine = (y == c) & (ctx == j)
            pl.when(jnp.logical_not(mine))(
                lambda j=j: arrived(seg_all.at[j], seg_recv + j, (2 * x + y, j))
            )
            pl.when(mine)(
                lambda j=j: pltpu.make_async_copy(
                    seg_all.at[j], seg_all.at[j], recvs.at[seg_own]
                ).wait()
            )

    class Swap:
        def __init__(self, source, there, here):
            self.place = places.take()
            self.out = remote(source, there, self.place, sibling)
            self.here = here

        def start(self):
            self.out.start()

        def wait(self):
            self.out.wait_send()
            arrived(self.here, self.place, sibling)

    def swap_rows(ref):
        mine, theirs = ref.at[pl.ds(own_at, own_rows)], ref.at[pl.ds(other_at, own_rows)]
        return Swap(mine, mine, theirs)

    own_at = pl.multiple_of(c * own_rows, own_rows)
    other_at = pl.multiple_of(oc * own_rows, own_rows)

    class Spread:
        def __init__(self, block):
            self.block = block
            self.place = places.take(3)

        def start(self):
            own = self.block(x, c)
            self.near = remote(own, own, self.place, sibling)
            self.across = remote(own, own, self.place + 1, x_next)
            self.near.start()
            self.across.start()

        def near_wait(self):
            arrived(self.block(x, oc), self.place, sibling)

        def pass_on(self):
            arrived(self.block(ox, c), self.place + 1, x_next)
            block = self.block(ox, c)
            self.far = remote(block, block, self.place + 2, sibling)
            self.far.start()

        def far_wait(self):
            arrived(self.block(ox, oc), self.place + 2, sibling)

        def sent(self):
            for copy in (self.near, self.across, self.far):
                copy.wait_send()

    r1 = {n: places.take(2) for n in ORDER}
    r2 = {n: places.take(2) for n in ORDER}
    r3 = {n: places.take(3) for n in ORDER}
    r4 = {n: places.take(3) for n in ORDER}
    sum_sends = []
    grads = dict(weight, d=at.grad_d)

    def send(copy):
        copy.start()
        sum_sends.append(copy)

    def sum_z(name):
        w = grads[name]
        for step in (1, 2, 3):
            there = z_at(step)
            block = w.at[:, :, there, y] if name in FEED else w.at[x, :, there, y]
            send(remote(block, getattr(at, "r3_" + name).at[step - 1], r3[name] + step - 1, z_device(step)))

    def sum_one(name):
        w = grads[name]
        if name in FEED:
            send(remote(w.at[:, :, :, oy], getattr(at, "r1a_" + name), r1[name], y_next))
            return
        first, second = split_columns(name, SUM_Y)
        send(remote(w.at[:, :, :, oy, :, pl.ds(0, first)], getattr(at, "r1a_" + name), r1[name], y_next))
        if second:
            send(remote(w.at[ox, :, :, :, :, pl.ds(first, second)], getattr(at, "r1b_" + name), r1[name] + 1, x_next))

    def sum_two(name):
        w = grads[name]
        arrived(getattr(at, "r1a_" + name), r1[name], y_next)
        first, second = (WIDTHS[name], 0) if name in FEED else split_columns(name, SUM_Y)

        @pl.loop(0, 16)
        def _(i):
            xx, cc, zz = lax.div(i, 8), lax.rem(lax.div(i, 4), 2), lax.rem(i, 4)
            w[xx, cc, zz, y, :, pl.ds(0, first)] += getattr(at, "r1a_" + name)[xx, cc, zz]

        if name in FEED:
            sum_z(name)
            return
        send(remote(w.at[ox, :, :, y, :, pl.ds(0, first)], getattr(at, "r2a_" + name), r2[name], x_next))
        if second:
            arrived(getattr(at, "r1b_" + name), r1[name] + 1, x_next)

            @pl.loop(0, 16)
            def _(i):
                cc, zz, yy = lax.div(i, 8), lax.rem(lax.div(i, 2), 4), lax.rem(i, 2)
                w[x, cc, zz, yy, :, pl.ds(first, second)] += getattr(at, "r1b_" + name)[cc, zz, yy]

            send(remote(w.at[x, :, :, oy, :, pl.ds(first, second)], getattr(at, "r2b_" + name), r2[name] + 1, y_next))

    def sum_three(name):
        w = grads[name]
        first, second = split_columns(name, SUM_Y)
        arrived(getattr(at, "r2a_" + name), r2[name], x_next)
        if second:
            arrived(getattr(at, "r2b_" + name), r2[name] + 1, y_next)

        @pl.loop(0, 8)
        def _(i):
            cc, zz = lax.div(i, 4), lax.rem(i, 4)
            w[x, cc, zz, y, :, pl.ds(0, first)] += getattr(at, "r2a_" + name)[cc, zz]
            if second:
                w[x, cc, zz, y, :, pl.ds(first, second)] += getattr(at, "r2b_" + name)[cc, zz]

        sum_z(name)

    def sum_four(name):
        w, landed = grads[name], getattr(at, "r3_" + name)
        for step in (1, 2, 3):
            arrived(landed.at[step - 1], r3[name] + step - 1, (dp, 2 * lax.rem(z + 4 - step, 4) + y))

        def total(*place):
            mine = w[(*place, z, y)] if name in FEED else w[(x, *place, z, y)]
            value = mine.astype(F32)
            for step in range(3):
                value = value + landed[(step, *place)].astype(F32)
            return value

        width = WIDTHS[name]
        staged, result = getattr(at, "r4_" + name), getattr(at, "out_" + name)
        if name in FEED:
            columns = pl.ds(pl.multiple_of(dp * width, width), width)
            for i, (xx, cc, device) in enumerate(((ox, oc, x_cross), (ox, c, x_next), (x, oc, sibling))):
                staged[i] = total(xx, cc)
                send(remote(staged.at[i], result.at[:, columns], r4[name] + i, device))
            result[:, columns] = total(x, c)
            return
        staged[...] = total(oc)
        if name == "e":
            send(remote(staged, at.r5_e, r4[name], sibling))
            result[...] = total(c)
        else:
            columns = pl.ds(pl.multiple_of(c * width, width), width)
            send(remote(staged, result.at[:, columns], r4[name], sibling))
            result[:, columns] = total(c)

    def sum_done(name):
        width = WIDTHS[name]
        if name == "e":
            arrived(at.r5_e, r4[name], sibling)
            at.out_e[...] = at.out_e[...] + at.r5_e[...]
        elif name in FEED:
            for i, (xx, cc, device) in enumerate(((ox, oc, x_cross), (ox, c, x_next), (x, oc, sibling))):
                columns = pl.ds(pl.multiple_of((2 * xx + cc) * width, width), width)
                arrived(getattr(at, "out_" + name).at[:, columns], r4[name] + i, device)
        else:
            columns = pl.ds(pl.multiple_of(oc * width, width), width)
            arrived(getattr(at, "out_" + name).at[:, columns], r4[name], sibling)

    gains, head_gains = at.gains, at.head_gains
    scaled, ff_in, grad_proj = at.scaled, at.ff_in, at.grad_proj
    residual, grad_residual = at.residual, at.grad_residual
    acc_own = at.acc_own
    scaled_swap, proj_swap = swap_rows(scaled), swap_rows(grad_proj)
    ff_spread = Spread(lambda xx, cc: ff_in.at[2 * xx + cc])
    cot_spread = Spread(lambda xx, cc: cot_all.at[pl.ds(4 * (2 * xx + cc), 4)])
    partials = [Swap(at.partial_out.at[i], at.partial_in.at[i], at.partial_in.at[i]) for i in range(2)]
    feed_near = [
        [Swap(at.near_out.at[i, k], at.near_in.at[i, k], at.near_in.at[i, k]) for k in range(2)] for i in range(2)
    ]
    feed_cross = []
    for i in range(2):
        place = places.take()
        feed_cross.append((remote(at.cross_out.at[i], at.cross_in.at[i], place, x_next), place))

    def selector():
        row = lax.broadcasted_iota(jnp.int32, (D, HD), 0)
        column = lax.broadcasted_iota(jnp.int32, (D, HD), 1)
        local_row = row & 31
        hit = ((row >> 5) * 4 + local_row == column) & (local_row < 4)
        return jnp.where(hit, 1.0, 0.0).astype(BF)

    def prepare_gains():
        columns = weight["e"][...].reshape(D, 128).astype(F32)
        for i in range(8):
            gains[:, i * 128 : (i + 1) * 128] = columns[i * 128 : (i + 1) * 128].T[:8]
        head_gains[...] = dot(gains[...].astype(BF), selector())

    def prepare_mask():
        rows = [seg_all[2 * j, 0:1] + seg_all[2 * j + 1, 0:1] for j in range(4)]
        for i in range(4):
            query = jnp.broadcast_to(rows[i], (128, 128)).T
            for j in range(4):
                place = slice(i * 128, (i + 1) * 128), slice(j * 128, (j + 1) * 128)
                if j > i:
                    at.bias[place] = jnp.full((128, 128), MASKED, F32)
                    continue
                seen = query == jnp.broadcast_to(rows[j], (128, 128))
                if i == j:
                    seen = seen & (
                        lax.broadcasted_iota(jnp.int32, (128, 128), 1)
                        <= lax.broadcasted_iota(jnp.int32, (128, 128), 0)
                    )
                at.bias[place] = jnp.where(seen, 0.0, MASKED)

    def own_block(j):
        return pl.ds(pl.multiple_of(c * own_rows + j * tokens, tokens), tokens)

    def here_block(j):
        return pl.ds(pl.multiple_of(j * tokens, tokens), tokens)

    def scale_input():
        @pl.loop(0, 4)
        def _(j):
            value = normalize(hidden_own[j].astype(F32)) * gains[0:1]
            scaled[own_block(j)] = value.astype(BF)

    def columns_of(name, t, size=256):
        return weight[name][:, :, :, :, :, pl.ds(pl.multiple_of(t * size, size), size)].reshape(D, size)

    def rows_of(name, t):
        return weight[name][lax.div(t, 2), lax.rem(t, 2)].reshape(D // 4, WIDTHS[name])

    cosine, sine = at.cosine, at.sine

    def turn(value):
        return value * cosine[...] + pltpu.roll(value, HD // 2, 1) * sine[...]

    def project_heads(name, gain, kept, turned):
        @pl.loop(0, WIDTHS[name] // 256)
        def _(t):
            both = dot(scaled[...], columns_of(name, t))
            for i in range(2):
                value = both[:, i * HD : (i + 1) * HD]
                kept[2 * t + i] = value
                turned[2 * t + i] = turn(normalize(value) * gain).astype(BF)

    def project_values():
        @pl.loop(0, WIDTHS["v"] // 256)
        def _(t):
            both = dot(scaled[...], columns_of("v", t))
            for i in range(2):
                at.values[2 * t + i] = both[:, i * HD : (i + 1) * HD].astype(BF)

    def probabilities(head, pair, block):
        rows = slice(block * half, (block + 1) * half)
        seen = slice(0, (block + 1) * half)
        scores = dot_nt(at.queries[head, rows], at.keys[pair, seen]) * SCALE + at.bias[rows, seen]
        terms = jnp.exp(scores - jnp.max(scores, axis=-1, keepdims=True))
        return terms * (1.0 / jnp.sum(terms, axis=-1, keepdims=True))

    def attend(first, last):
        @pl.loop(first, last)
        def _(head):
            pair = lax.div(head, 2)
            for block in range(2):
                seen = slice(0, (block + 1) * half)
                low = probabilities(head, pair, block).astype(BF)
                at.mixed[
                    block * half : (block + 1) * half, pl.ds(pl.multiple_of(head * HD, HD), HD)
                ] = dot(low, at.values[pair, seen]).astype(BF)

    def column_quarters(body):
        @pl.loop(0, 4)
        def _(t):
            body(t, pl.ds(pl.multiple_of(t * (D // 4), D // 4), D // 4))

    def partial_product(index, terms):
        def rows_times(first, t):
            return sum(dot_nt(left(pl.ds(first, own_rows)), rows_of(name, t)) for left, name in terms)

        def theirs(t, columns):
            at.partial_out[index, :, columns] = rows_times(other_at, t).astype(BF)

        def mine(t, columns):
            acc_own[:, columns] = rows_times(own_at, t)

        column_quarters(theirs)
        partials[index].start()
        column_quarters(mine)

    def own_sum(index, j):
        return acc_own[here_block(j)] + at.partial_in[index, here_block(j)].astype(F32)

    def feed_product(index, terms):
        def rows_times(xx, cc, t):
            first = pl.multiple_of((2 * xx + cc) * own_rows, own_rows)
            return sum(dot_nt(left[pl.ds(first, own_rows)], rows_of(name, t)) for left, name in terms)

        def give(k, xx):
            def body(t, columns):
                at.near_out[index, k, :, columns] = rows_times(xx, oc, t).astype(BF)

            column_quarters(body)
            feed_near[index][k].start()

        def keep(xx):
            def body(t, columns):
                acc_own[:, columns] = rows_times(xx, c, t)

            column_quarters(body)

        give(0, ox)
        keep(ox)
        feed_near[index][0].wait()
        near = at.near_in

        @pl.loop(0, 4)
        def _(j):
            rows = here_block(j)
            at.cross_out[index, rows] = (acc_own[rows] + near[index, 0, rows].astype(F32)).astype(BF)

        feed_cross[index][0].start()
        give(1, x)
        keep(x)

    def feed_wait(index):
        feed_near[index][1].wait()
        copy, place = feed_cross[index]
        copy.wait_send()
        arrived(at.cross_in.at[index], place, x_next)

    def feed_sum(index, j):
        rows = here_block(j)
        return acc_own[rows] + at.near_in[index, 1, rows].astype(F32) + at.cross_in[index, rows].astype(F32)

    def add_residual():
        @pl.loop(0, 4)
        def _(j):
            value = hidden_own[j].astype(F32) + own_sum(0, j)
            residual[here_block(j)] = value
            ff_in[2 * x + c, here_block(j)] = (normalize(value) * gains[1:2]).astype(BF)

    gate_part, up_part, hidden_low = at.gate_part, at.up_part, at.hidden_low

    def chip_rows(xx):
        return pl.ds(pl.multiple_of(xx * length, length), length)

    def feed_forward(xx):
        rows = chip_rows(xx)

        @pl.loop(0, WIDTHS["g"] // 256)
        def _(t):
            columns = pl.ds(pl.multiple_of(t * 256, 256), 256)
            left = ff_in[pl.ds(2 * xx, 2)].reshape(length, D)
            gate = dot(left, columns_of("g", t))
            up = dot(left, columns_of("u", t))
            sigmoid = 1.0 / (1.0 + jnp.exp(-gate))
            swish = gate * sigmoid
            hidden_low[rows, columns] = (swish * up).astype(BF)
            up_part[rows, columns] = swish.astype(BF)
            gate_part[rows, columns] = (up * sigmoid * (1.0 + gate * (1.0 - sigmoid))).astype(BF)

    def write_out():
        @pl.loop(0, 4)
        def _(j):
            at.out_own[j] = (residual[here_block(j)] + feed_sum(0, j)).astype(BF)

        for j in range(4):
            out_move.start(j)

    def grad_hidden():
        @pl.loop(0, 2 * (WIDTHS["d"] // 256))
        def _(i):
            xx, t = lax.div(i, 3), lax.rem(i, 3)
            rows, columns = chip_rows(xx), pl.ds(pl.multiple_of(t * 256, 256), 256)
            grad = dot(cot_all[pl.ds(8 * xx, 8)].reshape(length, D), columns_of("d", t))
            gate_part[rows, columns] = (grad * gate_part[rows, columns].astype(F32)).astype(BF)
            up_part[rows, columns] = (grad * up_part[rows, columns].astype(F32)).astype(BF)

    turned_rows = at.turned_rows

    def transpose_rows(load, count):
        @pl.loop(0, D // 128)
        def _(t):
            place = pl.ds(pl.multiple_of(t * 128, 128), 128)
            turned_rows[place, :count] = load(place).reshape(count, 128).T

    def weight_grad(name, right, count):
        if name != "d":
            gather_sent(name)

        @pl.loop(0, WIDTHS[name] // 256)
        def _(t):
            columns = pl.ds(pl.multiple_of(t * 256, 256), 256)
            grad = dot(turned_rows[:, :count], right(columns))
            grads[name][:, :, :, :, :, columns] = grad.astype(BF).reshape(2, 2, 4, 2, 32, 256)

    grad_gains = at.grad_gains

    def back_residual():
        grad_gains[...] = jnp.zeros_like(grad_gains)

        @pl.loop(0, 4)
        def _(j):
            value = residual[here_block(j)]
            grad = feed_sum(1, j)
            scale = lax.rsqrt(jnp.mean(value * value, axis=-1, keepdims=True) + NORM_EPS)
            grad_gains[1:2] += jnp.sum(grad * (value * scale), axis=0, keepdims=True)
            total = cot_all[4 * (2 * x + c) + j].astype(F32) + norm_back(value, grad * gains[1:2])
            grad_residual[here_block(j)] = total
            grad_proj[own_block(j)] = total.astype(BF)

    grad_mixed, grad_heads = ff_in, cot_all

    def back_mixed():
        @pl.loop(0, WIDTHS["o"] // 256)
        def _(t):
            columns = pl.ds(pl.multiple_of(t * 256, 256), 256)
            grad = dot(grad_proj[...], columns_of("o", t)).astype(BF)
            grad_mixed[:2, :, columns] = grad.reshape(2, half, 256)

    def put_heads(first, columns, value):
        grad_heads[first : first + 8, :, columns] = value.astype(BF).reshape(8, tokens, HD)

    def head_columns(first, columns):
        return grad_heads[first : first + 8, :, columns].reshape(length, columns.size)

    def head_rows(first, rows, start, width):
        block = first + lax.div(rows.start, tokens)
        return grad_heads[pl.ds(block, 4), :, start : start + width].reshape(own_rows, width)

    grad_head_gains = at.grad_head_gains

    def turn_back(value):
        return value * cosine[...] - pltpu.roll(value, HD // 2, 1) * sine[...]

    def back_head(value, grad, row, first, columns):
        scale = lax.rsqrt(jnp.mean(value * value, axis=-1, keepdims=True) + NORM_EPS)
        turned = turn_back(grad)
        grad_head_gains[row : row + 1] += jnp.sum(turned * (value * scale), axis=0, keepdims=True)
        put_heads(first, columns, norm_back(value, turned * head_gains[row : row + 1]))

    grad_key, grad_value, grad_query = at.grad_key, at.grad_value, at.grad_query

    def back_attend(first, last):
        if first == 0:
            grad_head_gains[...] = jnp.zeros_like(grad_head_gains)

        @pl.loop(first, last)
        def _(pair):
            for i in range(2):
                head = 2 * pair + i
                lanes = pl.ds(pl.multiple_of(head * HD, HD), HD)
                for block in (1, 0):
                    rows = slice(block * half, (block + 1) * half)
                    seen = slice(0, (block + 1) * half)
                    probs = probabilities(head, pair, block)
                    grad_out = grad_mixed[block, :, lanes]
                    grad_probs = dot_nt(grad_out, at.values[pair, seen])
                    delta = jnp.sum(probs * grad_probs, axis=-1, keepdims=True)
                    grad_scores = (probs * (grad_probs - delta)).astype(BF)
                    grad_query[rows] = dot(grad_scores, at.keys[pair, seen]) * SCALE
                    key_part = dot_tn(grad_scores, at.queries[head, rows]) * SCALE
                    value_part = dot_tn(probs.astype(BF), grad_out)
                    if i == 0 and block == 1:
                        grad_key[...] = key_part
                        grad_value[...] = value_part
                    else:
                        grad_key[seen] += key_part
                        grad_value[seen] += value_part
                back_head(at.query_acc[head], grad_query[...], 2, 0, lanes)
            lanes = pl.ds(pl.multiple_of(pair * HD, HD), HD)
            back_head(at.key_acc[pair], grad_key[...], 3, 8, lanes)
            put_heads(8, pl.ds(pl.multiple_of(WIDTHS["k"] + pair * HD, HD), HD), grad_value[...])

    def back_input():
        @pl.loop(0, 4)
        def _(j):
            value = hidden_own[j].astype(F32)
            grad = own_sum(1, j)
            scale = lax.rsqrt(jnp.mean(value * value, axis=-1, keepdims=True) + NORM_EPS)
            grad_gains[0:1] += jnp.sum(grad * (value * scale), axis=0, keepdims=True)
            at.grad_own[j] = (
                grad_residual[here_block(j)] + norm_back(value, grad * gains[0:1])
            ).astype(BF)

        for j in range(4):
            grad_move.start(j)

    def gain_grads():
        gather_sent("e")
        grad_gains[...] += dot_nt(grad_head_gains[...].astype(BF), selector())
        for i in range(8):
            block = jnp.concatenate(
                [grad_gains[:, i * 128 : (i + 1) * 128], jnp.zeros((120, 128), F32)], axis=0
            ).T
            weight["e"][i // 4, (i // 2) % 2, 2 * (i % 2) : 2 * (i % 2) + 2] = block.astype(BF).reshape(2, 2, 32, 128)

    for name in ("e", "k", "v", "q", "o"):
        gather_core(name)
    gather_z("e")
    gather_z("k")
    seg_start()
    hidden_move.start()
    gather_two("e")
    gather_z("v")
    gather_two("k")
    gather_z("q")
    gather_three("e")
    gather_two("v")
    gather_three("k")
    gather_z("o")
    gather_done("e")
    prepare_gains()
    seg_wait()
    prepare_mask()
    hidden_move.wait()
    scale_input()
    scaled_swap.start()
    gather_two("q")
    for name in FEED:
        gather_core(name)
    gather_z("g")
    gather_three("v")
    gather_done("k")
    scaled_swap.wait()
    project_heads("k", head_gains[3:4], at.key_acc, at.keys)
    gather_two("o")
    gather_three("q")
    cot_move.start()
    gather_done("v")
    project_values()
    gather_two("g")
    gather_z("u")
    gather_three("o")
    gather_done("q")
    project_heads("q", head_gains[2:3], at.query_acc, at.queries)
    cot_move.wait()
    cot_spread.start()
    attend(0, 4)
    gather_two("u")
    gather_z("d")
    cot_spread.pass_on()
    attend(4, 8)
    gather_done("o")
    partial_product(0, [(lambda rows: at.mixed[rows], "o")])
    partials[0].wait()
    add_residual()
    ff_spread.start()
    gather_two("d")
    cot_spread.near_wait()
    cot_spread.far_wait()
    transpose_rows(lambda columns: cot_all[:, :, columns], 2 * length)
    gather_done("g")
    gather_done("u")
    ff_spread.near_wait()
    feed_forward(x)
    ff_spread.pass_on()
    ff_spread.far_wait()
    feed_forward(ox)

    weight_grad("d", lambda columns: hidden_low[:, columns], 2 * length)
    sum_one("d")
    gather_done("d")
    grad_hidden()
    feed_product(1, [(gate_part, "g"), (up_part, "u")])
    transpose_rows(lambda columns: ff_in[:, :, columns], 2 * length)
    weight_grad("g", lambda columns: gate_part[:, columns], 2 * length)
    sum_one("g")
    weight_grad("u", lambda columns: up_part[:, columns], 2 * length)
    sum_one("u")
    feed_wait(1)
    back_residual()
    proj_swap.start()
    ff_spread.sent()
    cot_spread.sent()
    sum_two("d")
    proj_swap.wait()
    back_mixed()
    transpose_rows(lambda columns: grad_proj[:, columns], length)
    weight_grad("o", lambda columns: at.mixed[:, columns], length)
    sum_one("o")
    back_attend(0, 2)
    sum_two("g")
    back_attend(2, 4)
    sum_two("u")
    sum_four("d")
    partial_product(
        1,
        [
            (lambda rows: head_rows(0, rows, 0, WIDTHS["q"]), "q"),
            (lambda rows: head_rows(8, rows, 0, WIDTHS["k"]), "k"),
            (lambda rows: head_rows(8, rows, WIDTHS["k"], WIDTHS["v"]), "v"),
        ],
    )
    transpose_rows(lambda columns: scaled[:, columns], length)
    weight_grad("q", lambda columns: head_columns(0, columns), length)
    sum_one("q")
    weight_grad("k", lambda columns: head_columns(8, columns), length)
    sum_one("k")
    weight_grad("v", lambda columns: head_columns(8, pl.ds(columns.start + WIDTHS["k"], 256)), length)
    sum_one("v")
    sum_two("o")
    partials[1].wait()
    back_input()
    gain_grads()
    sum_one("e")
    sum_four("g")
    feed_product(0, [(hidden_low, "d")])
    feed_wait(0)
    write_out()
    sum_three("o")
    sum_two("q")
    sum_four("u")
    sum_three("q")
    sum_two("k")
    sum_four("o")
    sum_three("k")
    sum_two("v")
    sum_two("e")
    sum_three("v")
    sum_three("e")
    for name in ("q", "k", "v", "e"):
        sum_four(name)
    for name in ("d", "g", "u", "o", "q", "k", "v", "e"):
        sum_done(name)
    for copy in sum_sends:
        copy.wait_send()
    gather_sent("d")
    hidden_move.sent()
    cot_move.sent()
    out_move.finish()
    grad_move.finish()
    assert places.count <= SEMAPHORES, places.count


SEMAPHORES = 320


def fused(
    hidden_in,
    segments,
    attention_gain,
    query_gain,
    key_gain,
    query_weight,
    key_weight,
    value_weight,
    out_weight,
    feedforward_gain,
    gate_weight,
    up_weight,
    down_weight,
    cotangent,
):
    tokens = hidden_in.shape[2]
    length = 8 * tokens
    rows = query_weight.shape[0]
    odd = lax.rem(lax.axis_index("ctx"), 2)
    numbers = segments[:, 0].astype(F32)
    blank = jnp.zeros_like(numbers)
    numbers = jnp.where(
        odd == 0, jnp.concatenate([numbers, blank], axis=1), jnp.concatenate([blank, numbers], axis=1)
    )
    numbers = jnp.broadcast_to(numbers[:, None], (MB, 8, 2 * tokens))

    def column(gain):
        return jnp.pad(gain, (0, rows - gain.shape[0]))

    extra = jnp.stack(
        [attention_gain, feedforward_gain, column(query_gain), column(key_gain)], axis=1
    )
    extra = jnp.pad(extra, ((0, 0), (0, 124)))
    angles = rope_angles(0, length)
    cosine = jnp.concatenate([jnp.cos(angles), jnp.cos(angles)], axis=-1)
    sine = jnp.concatenate([-jnp.sin(angles), jnp.sin(angles)], axis=-1)

    vmem, anywhere = pl.BlockSpec(memory_space=pltpu.VMEM), pl.BlockSpec(memory_space=pl.ANY)
    inputs = dict(
        hidden_in=(hidden_in[:, 0], anywhere),
        cotangent=(cotangent[:, 0], anywhere),
        segments=(numbers, vmem),
        cosine=(cosine, vmem),
        sine=(sine, vmem),
        in_e=(extra, anywhere),
        in_k=(key_weight, anywhere),
        in_v=(value_weight, anywhere),
        in_q=(query_weight, anywhere),
        in_o=(out_weight.T, anywhere),
        in_g=(gate_weight, anywhere),
        in_u=(up_weight, anywhere),
        in_d=(down_weight.T, anywhere),
    )
    block = (MB, tokens, D)
    outputs = dict(block_out=(block, BF, anywhere), input_grad=(block, BF, anywhere))
    for name, width in WIDTHS.items():
        outputs["out_" + name] = ((rows, width * (4 if name in FEED else 1 if name == "e" else 2)), F32, vmem)
    own = 4 * tokens
    scratch = dict(
        hidden_own=((4, tokens, D), BF),
        cot_all=((16, tokens, D), BF),
        seg_all=((8, 8, 2 * tokens), F32),
        gains=((8, D), F32),
        head_gains=((8, HD), F32),
        grad_gains=((8, D), F32),
        grad_head_gains=((8, HD), F32),
        bias=((length, length), F32),
        scaled=((length, D), BF),
        query_acc=((HALF_HQ, length, HD), F32),
        key_acc=((HALF_HK, length, HD), F32),
        queries=((HALF_HQ, length, HD), BF),
        keys=((HALF_HK, length, HD), BF),
        values=((HALF_HK, length, HD), BF),
        mixed=((length, HALF_HQ * HD), BF),
        acc_own=((own, D), F32),
        partial_out=((2, own, D), BF),
        partial_in=((2, own, D), BF),
        near_out=((2, 2, own, D), BF),
        near_in=((2, 2, own, D), BF),
        cross_out=((2, own, D), BF),
        cross_in=((2, own, D), BF),
        residual=((own, D), F32),
        grad_residual=((own, D), F32),
        ff_in=((4, own, D), BF),
        gate_part=((2 * length, FF // 4), BF),
        up_part=((2 * length, FF // 4), BF),
        hidden_low=((2 * length, FF // 4), BF),
        grad_d=((2, 2, 4, 2, rows, FF // 4), BF),
        grad_proj=((length, D), BF),
        grad_key=((length, HD), F32),
        grad_value=((length, HD), F32),
        grad_query=((length, HD), F32),
        turned_rows=((D, 2 * length), BF),
        out_own=((4, tokens, D), BF),
        grad_own=((4, tokens, D), BF),
        r5_e=((rows, 128), F32),
    )
    for name, width in WIDTHS.items():
        scratch["w_" + name] = ((2, 2, 4, 2, rows, width), BF)
        if name in FEED:
            scratch["r1a_" + name] = ((2, 2, 4, rows, width), BF)
            scratch["r3_" + name] = ((3, 2, 2, rows, width), BF)
            scratch["r4_" + name] = ((3, rows, width), F32)
            continue
        first, second = split_columns(name, SUM_Y)
        scratch["r1a_" + name] = ((2, 2, 4, rows, first), BF)
        scratch["r2a_" + name] = ((2, 4, rows, first), BF)
        if second:
            scratch["r1b_" + name] = ((2, 4, 2, rows, second), BF)
            scratch["r2b_" + name] = ((2, 4, rows, second), BF)
        scratch["r3_" + name] = ((3, 2, rows, width), BF)
        scratch["r4_" + name] = ((rows, width), F32)
    names = (*inputs, *outputs, *scratch, "sends", "recvs")
    results = pl.pallas_call(
        functools.partial(layer_kernel, names, tokens),
        out_shape=[jax.ShapeDtypeStruct(shape, dtype) for shape, dtype, _ in outputs.values()],
        in_specs=[spec for _, spec in inputs.values()],
        out_specs=[spec for _, _, spec in outputs.values()],
        scratch_shapes=[pltpu.VMEM(shape, dtype) for shape, dtype in scratch.values()]
        + [pltpu.SemaphoreType.DMA((SEMAPHORES,))] * 2,
        compiler_params=pltpu.CompilerParams(
            collective_id=0, has_side_effects=True, vmem_limit_bytes=64 * 2**20 - 2**16
        ),
        name="layer",
    )(*(value for value, _ in inputs.values()))
    got = types.SimpleNamespace(**dict(zip(outputs, results)))
    gain_grads = got.out_e
    heads = query_gain.shape[0]
    return (
        got.block_out[:, None],
        got.input_grad.astype(F32)[:, None],
        gain_grads[:, 0],
        gain_grads[:heads, 2],
        gain_grads[:heads, 3],
        got.out_q,
        got.out_k,
        got.out_v,
        got.out_o.T,
        gain_grads[:, 1],
        got.out_g,
        got.out_u,
        got.out_d.T,
    )


def rope_tables(first, count):
    angles = rope_angles(first, count)
    cosine = jnp.concatenate([jnp.cos(angles), jnp.cos(angles)], axis=-1)
    sine = jnp.concatenate([jnp.sin(angles), jnp.sin(angles)], axis=-1)
    return (cosine[:, None, :], sine[:, None, :])


def rotate(value, cosine, sine):
    half = value.shape[-1] // 2
    turned = jnp.concatenate([-value[..., half:], value[..., :half]], axis=-1)
    return value * cosine + turned * sine


def rotate_back(grad, cosine, sine):
    half = grad.shape[-1] // 2
    scaled = grad * sine
    return grad * cosine + jnp.concatenate([scaled[..., half:], -scaled[..., :half]], axis=-1)


def contract_last(left, right):
    return lax.dot_general(
        left, right, (((1,), (1,)), ((), ())), preferred_element_type=jnp.float32
    )


def contract_first(left, right):
    return lax.dot_general(
        left, right, (((0,), (0,)), ((), ())), preferred_element_type=jnp.float32
    )


def block_rows(rows):
    size = min(rows, 512)
    while rows % size:
        size -= 1
    return size


def over_blocks(state, pieces, update):
    rows = pieces[0].shape[0]
    size = block_rows(rows)
    count = rows // size
    stacked = tuple((piece.reshape((count, size) + piece.shape[1:]) for piece in pieces))
    offsets = size * jnp.arange(count, dtype=jnp.int32)

    def step(current, item):
        block = item[:-1]
        offset = item[-1]
        current = update(current, block, offset)
        return (current, None)

    final, unused = lax.scan(step, state, stacked + (offsets,))
    return final


def general(
    hidden_in,
    segments,
    attention_gain,
    query_gain,
    key_gain,
    query_weight,
    key_weight,
    value_weight,
    out_weight,
    feedforward_gain,
    gate_weight,
    up_weight,
    down_weight,
    cotangent,
):
    tokens = hidden_in.shape[2]
    groups = HQ // HK
    scale = HD ** (-0.5)
    first = lax.axis_index("ctx") * tokens
    length = lax.axis_size("ctx") * tokens
    query_pos = first + jnp.arange(tokens, dtype=jnp.int32)
    cosine, sine = rope_tables(first, tokens)
    sources = (
        query_weight,
        key_weight,
        value_weight,
        gate_weight,
        up_weight,
        out_weight.T,
        down_weight.T,
    )
    whole = lax.all_gather(jnp.concatenate(sources, axis=1), ("dp", "ctx"), axis=0, tiled=True)
    parts = []
    edge = 0
    for source in sources:
        parts.append(whole[:, edge : edge + source.shape[1]])
        edge = edge + source.shape[1]
    whole_query, whole_key, whole_value, whole_gate, whole_up, whole_out, whole_down = parts
    gain_in, gain_query, gain_key, gain_feed = (
        lax.all_gather(gain, ("dp", "ctx"), axis=0, tiled=True)
        for gain in (attention_gain, query_gain, key_gain, feedforward_gain)
    )
    grad_attention_gain = jnp.zeros((D,), jnp.float32)
    grad_feed_gain = jnp.zeros((D,), jnp.float32)
    grad_query_gain = jnp.zeros((HD,), jnp.float32)
    grad_key_gain = jnp.zeros((HD,), jnp.float32)
    outputs = []
    input_grads = []
    stored = []
    for batch in range(MB):
        hidden = hidden_in[batch, 0].astype(jnp.float32)
        query_seg = segments[batch, 0]
        grad_out = cotangent[batch, 0]
        normed = normalize(hidden)
        scaled_in = (normed * gain_in.astype(jnp.float32)).astype(jnp.bfloat16)
        query_heads = jnp.dot(scaled_in, whole_query, preferred_element_type=jnp.float32).reshape(
            tokens, HQ, HD
        )
        key_heads = jnp.dot(scaled_in, whole_key, preferred_element_type=jnp.float32).reshape(
            tokens, HK, HD
        )
        values = jnp.dot(scaled_in, whole_value, preferred_element_type=jnp.float32).astype(
            jnp.bfloat16
        )
        query_norm = normalize(query_heads)
        key_norm = normalize(key_heads)
        query_scale = gain_query.astype(jnp.float32)
        key_scale = gain_key.astype(jnp.float32)
        queries = rotate(query_norm * query_scale, cosine, sine).astype(jnp.bfloat16)
        keys_low = rotate(key_norm * key_scale, cosine, sine).astype(jnp.bfloat16)
        grouped = queries.reshape(tokens, HK, groups, HD)
        keys_flat = keys_low.reshape(tokens, HK * HD)

        def key_scores(keys, key_seg, offset):
            rows = keys.shape[0]
            shaped = keys.reshape(rows, HK, HD)
            raw = (
                jnp.einsum("qkgd,skd->kgqs", grouped, shaped, preferred_element_type=jnp.float32)
                * scale
            )
            key_pos = offset + jnp.arange(rows, dtype=jnp.int32)
            visible = (key_pos[None, :] <= query_pos[:, None]) & (
                key_seg[None, :] == query_seg[:, None]
            )
            return (jnp.where(visible, raw, MASKED), visible, shaped)

        def fold_with(update, state, pieces):
            return over_blocks(state, pieces, update)

        def add_lse(state, block, offset):
            keys, key_seg = block
            masked, visible, shaped = key_scores(keys, key_seg, offset)
            top, total = state
            new_top = jnp.maximum(top, jnp.max(masked, axis=-1))
            terms = jnp.where(visible, jnp.exp(masked - new_top[..., None]), 0.0)
            return (new_top, total * jnp.exp(top - new_top) + jnp.sum(terms, axis=-1))

        start_state = (
            jnp.full((HK, groups, tokens), MASKED, jnp.float32),
            jnp.zeros((HK, groups, tokens), jnp.float32),
        )
        top, total = fold_with(
            add_lse,
            start_state,
            (
                lax.all_gather(keys_flat, "ctx", axis=0, tiled=True),
                lax.all_gather(query_seg, "ctx", axis=0, tiled=True),
            ),
        )
        lse = top + jnp.log(total)

        def add_mixed(state, block, offset):
            keys, values_block, key_seg = block
            masked, visible, shaped = key_scores(keys, key_seg, offset)
            probs = jnp.exp(masked - lse[..., None]).astype(jnp.bfloat16)
            value_heads = values_block.reshape(values_block.shape[0], HK, HD)
            return state + jnp.einsum(
                "kgqs,skd->qkgd", probs, value_heads, preferred_element_type=jnp.float32
            )

        mixed = fold_with(
            add_mixed,
            jnp.zeros((tokens, HK, groups, HD), jnp.float32),
            (
                lax.all_gather(keys_flat, "ctx", axis=0, tiled=True),
                lax.all_gather(values, "ctx", axis=0, tiled=True),
                lax.all_gather(query_seg, "ctx", axis=0, tiled=True),
            ),
        )
        mixed_low = mixed.reshape(tokens, HQ * HD).astype(jnp.bfloat16)
        residual = hidden + contract_last(mixed_low, whole_out)
        feed_normed = normalize(residual)
        feed_scale = gain_feed.astype(jnp.float32)
        ff_in = (feed_normed * feed_scale).astype(jnp.bfloat16)
        gate = jnp.dot(ff_in, whole_gate, preferred_element_type=jnp.float32)
        up_part = jnp.dot(ff_in, whole_up, preferred_element_type=jnp.float32)
        sigmoid = jax.nn.sigmoid(gate)
        swish = gate * sigmoid
        hidden_low = (swish * up_part).astype(jnp.bfloat16)
        block_out = residual + contract_last(hidden_low, whole_down)
        outputs.append(block_out.astype(jnp.bfloat16))
        grad_hidden = jnp.dot(grad_out, whole_down, preferred_element_type=jnp.float32)
        grad_gate = (grad_hidden * up_part * (sigmoid * (1.0 + gate * (1.0 - sigmoid)))).astype(
            jnp.bfloat16
        )
        grad_up = (grad_hidden * swish).astype(jnp.bfloat16)
        grad_feed_in = contract_last(grad_gate, whole_gate) + contract_last(grad_up, whole_up)
        grad_feed_gain = grad_feed_gain + jnp.sum(grad_feed_in * feed_normed, axis=0)
        grad_residual = grad_out.astype(jnp.float32) + norm_back(
            residual, grad_feed_in * gain_feed.astype(jnp.float32)
        )
        grad_proj = grad_residual.astype(jnp.bfloat16)
        grad_mixed = (
            jnp.dot(grad_proj, whole_out, preferred_element_type=jnp.float32).astype(jnp.bfloat16).reshape(tokens, HK, groups, HD)
        )
        delta = jnp.transpose(jnp.sum(grad_mixed.astype(jnp.float32) * mixed, axis=-1), (1, 2, 0))

        def add_grads(state, block, offset):
            grad_query, grad_keys, grad_values = state
            keys, values_block, key_seg = block
            masked, visible, shaped = key_scores(keys, key_seg, offset)
            rows = keys.shape[0]
            probs = jnp.exp(masked - lse[..., None])
            probs_low = probs.astype(jnp.bfloat16)
            value_heads = values_block.reshape(rows, HK, HD)
            grad_probs = jnp.einsum(
                "qkgd,skd->kgqs", grad_mixed, value_heads, preferred_element_type=jnp.float32
            )
            grad_scores = (probs * (grad_probs - delta[..., None])).astype(jnp.bfloat16)
            grad_query = (
                grad_query
                + jnp.einsum(
                    "kgqs,skd->qkgd", grad_scores, shaped, preferred_element_type=jnp.float32
                )
                * scale
            )
            key_part = (
                jnp.einsum(
                    "kgqs,qkgd->skd", grad_scores, grouped, preferred_element_type=jnp.float32
                )
                * scale
            )
            value_part = jnp.einsum(
                "kgqs,qkgd->skd", probs_low, grad_mixed, preferred_element_type=jnp.float32
            )
            old_keys = lax.dynamic_slice_in_dim(grad_keys, offset, rows, 0)
            grad_keys = lax.dynamic_update_slice_in_dim(
                grad_keys, old_keys + key_part.reshape(rows, HK * HD), offset, 0
            )
            old_values = lax.dynamic_slice_in_dim(grad_values, offset, rows, 0)
            grad_values = lax.dynamic_update_slice_in_dim(
                grad_values, old_values + value_part.reshape(rows, HK * HD), offset, 0
            )
            return (grad_query, grad_keys, grad_values)

        back_state = (
            jnp.zeros((tokens, HK, groups, HD), jnp.float32),
            jnp.zeros((length, HK * HD), jnp.float32),
            jnp.zeros((length, HK * HD), jnp.float32),
        )
        grad_query, grad_keys_all, grad_values_all = fold_with(
            add_grads,
            back_state,
            (
                lax.all_gather(keys_flat, "ctx", axis=0, tiled=True),
                lax.all_gather(values, "ctx", axis=0, tiled=True),
                lax.all_gather(query_seg, "ctx", axis=0, tiled=True),
            ),
        )
        grad_keys_own, grad_values_own = (
            lax.psum_scatter(
                grad_keys_all.astype(jnp.bfloat16), "ctx", scatter_dimension=0, tiled=True
            ).astype(jnp.float32),
            lax.psum_scatter(
                grad_values_all.astype(jnp.bfloat16), "ctx", scatter_dimension=0, tiled=True
            ).astype(jnp.float32),
        )
        turned_query = rotate_back(grad_query.reshape(tokens, HQ, HD), cosine, sine)
        grad_query_gain = grad_query_gain + jnp.sum(turned_query * query_norm, axis=(0, 1))
        grad_query_low = (
            norm_back(query_heads, turned_query * gain_query.astype(jnp.float32))
            .reshape(tokens, HQ * HD)
            .astype(jnp.bfloat16)
        )
        turned_key = rotate_back(grad_keys_own.reshape(tokens, HK, HD), cosine, sine)
        grad_key_gain = grad_key_gain + jnp.sum(turned_key * key_norm, axis=(0, 1))
        grad_key_low = (
            norm_back(key_heads, turned_key * gain_key.astype(jnp.float32))
            .reshape(tokens, HK * HD)
            .astype(jnp.bfloat16)
        )
        grad_value_low = grad_values_own.astype(jnp.bfloat16)
        grad_scaled_in = (
            contract_last(grad_query_low, whole_query)
            + contract_last(grad_key_low, whole_key)
            + contract_last(grad_value_low, whole_value)
        )
        grad_attention_gain = grad_attention_gain + jnp.sum(grad_scaled_in * normed, axis=0)
        input_grads.append(
            grad_residual + norm_back(hidden, grad_scaled_in * gain_in.astype(jnp.float32))
        )
        stored.append(
            (
                scaled_in,
                grad_query_low,
                grad_key_low,
                grad_value_low,
                ff_in,
                grad_gate,
                grad_up,
                grad_proj,
                mixed_low,
                grad_out,
                hidden_low,
            )
        )
    columns = [jnp.concatenate([entry[index] for entry in stored], axis=0) for index in range(11)]
    (
        all_in,
        all_query,
        all_key,
        all_value,
        all_feed,
        all_gate,
        all_up,
        all_proj,
        all_mixed,
        all_out,
        all_hidden,
    ) = columns
    rows = query_weight.shape[0]
    head_rows = query_gain.shape[0]
    count = lax.axis_size(("dp", "ctx")) * rows
    row_ids = jnp.arange(count, dtype=jnp.int32)
    local = row_ids % rows
    place = jnp.clip(row_ids // rows * head_rows + local, 0, HD - 1)
    owned = local < head_rows
    gains = jnp.stack(
        [
            grad_attention_gain,
            grad_feed_gain,
            jnp.where(owned, jnp.take(grad_query_gain, place), 0.0),
            jnp.where(owned, jnp.take(grad_key_gain, place), 0.0),
        ],
        axis=1,
    )
    summed = lax.psum_scatter(
        jnp.concatenate(
            [
                contract_first(all_in, all_query).astype(BF),
                contract_first(all_in, all_key).astype(BF),
                contract_first(all_in, all_value).astype(BF),
                contract_first(all_feed, all_gate).astype(BF),
                contract_first(all_feed, all_up).astype(BF),
                contract_first(all_proj, all_mixed).astype(BF),
                contract_first(all_out, all_hidden).astype(BF),
                gains.astype(BF),
                jnp.zeros((count, 124), BF),
            ],
            axis=1,
        ),
        ("dp", "ctx"),
        scatter_dimension=0,
        tiled=True,
    ).astype(F32)
    widths = [HQ * HD, HK * HD, HK * HD, FF, FF, HQ * HD, FF, 128]
    pieces = []
    edge = 0
    for width in widths:
        pieces.append(summed[:, edge : edge + width])
        edge = edge + width
    gain_block = pieces[7]
    block_out = jnp.stack(outputs)[:, None]
    input_grad = jnp.stack(input_grads)[:, None]
    return (
        block_out,
        input_grad,
        gain_block[:, 0],
        gain_block[:head_rows, 2],
        gain_block[:head_rows, 3],
        pieces[0],
        pieces[1],
        pieces[2],
        pieces[5].T,
        gain_block[:, 1],
        pieces[3],
        pieces[4],
        pieces[6].T,
    )


def solution(mesh):
    shape = dict(mesh.shape)
    chips_hold_sequences = shape["dp"] == 4 and shape["ctx"] == 8

    def step(*arrays):
        if chips_hold_sequences and arrays[0].shape[2] == 64:
            return fused(*arrays)
        return general(*arrays)

    return jax.shard_map(
        step,
        mesh=mesh,
        in_specs=(
            P(None, "dp", "ctx", None),
            P(None, "dp", "ctx"),
            P(("dp", "ctx")),
            P(("dp", "ctx")),
            P(("dp", "ctx")),
            P(("dp", "ctx"), None),
            P(("dp", "ctx"), None),
            P(("dp", "ctx"), None),
            P(None, ("dp", "ctx")),
            P(("dp", "ctx")),
            P(("dp", "ctx"), None),
            P(("dp", "ctx"), None),
            P(None, ("dp", "ctx")),
            P(None, "dp", "ctx", None),
        ),
        out_specs=(
            P(None, "dp", "ctx", None),
            P(None, "dp", "ctx", None),
            P(("dp", "ctx")),
            P(("dp", "ctx")),
            P(("dp", "ctx")),
            P(("dp", "ctx"), None),
            P(("dp", "ctx"), None),
            P(("dp", "ctx"), None),
            P(None, ("dp", "ctx")),
            P(("dp", "ctx")),
            P(("dp", "ctx"), None),
            P(("dp", "ctx"), None),
            P(None, ("dp", "ctx")),
        ),
        check_vma=False,
    )
```

```python
import functools
import types

import jax
import jax.numpy as jnp
import numpy as np
from jax import lax
from jax.experimental import pallas as pl
from jax.experimental.pallas import tpu as pltpu
from jax.sharding import PartitionSpec as P

D = 1024
HQ = 16
HK = 8
HD = 128
FF = 3072
MB = 4

NORM_EPS = 1e-06
ROPE_BASE = 1000000.0
MASKED = -1e30
SCALE = HD ** (-0.5)
BF = jnp.bfloat16
F32 = jnp.float32
MESH = pl.DeviceIdType.MESH


def normalize(value):
    return value * lax.rsqrt(jnp.mean(value * value, axis=-1, keepdims=True) + NORM_EPS)


def norm_back(value, grad):
    scale = lax.rsqrt(jnp.mean(value * value, axis=-1, keepdims=True) + NORM_EPS)
    return scale * grad - value * (scale * scale * scale) * jnp.mean(
        grad * value, axis=-1, keepdims=True
    )


def rope_angles(first, count):
    positions = (first + jnp.arange(count, dtype=jnp.int32)).astype(F32)
    frequency = ROPE_BASE ** (-(jnp.arange(HD // 2, dtype=F32) * 2.0) / HD)
    return positions[:, None] * frequency[None, :]


KEYS = HK * HD // 2
WIDTHS = dict(
    k=KEYS + 128,
    v=KEYS,
    q=HQ * HD // 2,
    o=HQ * HD // 2,
    g=FF // 4,
    u=FF // 4,
    d=FF // 4,
)
ORDER = tuple(WIDTHS)
FEED = ("g", "u", "d")
PIECES = dict(k=(256, 384), v=(512,), q=(512, 512), o=(512, 512), g=(768,), u=(768,), d=(384, 384))
SUM_Y = dict(k=256, v=256, q=512, o=256)
HALF_HQ, HALF_HK = HQ // 2, HK // 2


def split_columns(name):
    return SUM_Y[name], WIDTHS[name] - SUM_Y[name]


def dot(left, right):
    return jnp.dot(left, right, preferred_element_type=F32)


def dot_nt(left, right):
    return lax.dot_general(left, right, (((1,), (1,)), ((), ())), preferred_element_type=F32)


def dot_tn(left, right):
    return lax.dot_general(left, right, (((0,), (0,)), ((), ())), preferred_element_type=F32)


class Semaphores:
    def __init__(self):
        self.count = 0

    def take(self, number=1):
        first = self.count
        self.count += number
        return first


def layer_kernel(names, tokens, *refs):
    at = types.SimpleNamespace(**dict(zip(names, refs)))
    sends, recvs = at.sends, at.recvs
    places = Semaphores()
    dp, ctx = lax.axis_index("dp"), lax.axis_index("ctx")
    x, c = lax.div(dp, 2), lax.rem(dp, 2)
    z, y = lax.div(ctx, 2), lax.rem(ctx, 2)
    ox, oc, oy = 1 - x, 1 - c, 1 - y
    sibling = (2 * x + oc, ctx)
    x_next = (2 * ox + c, ctx)
    x_cross = (2 * ox + oc, ctx)
    y_next = (dp, 2 * z + oy)
    length = 8 * tokens
    own_rows = 4 * tokens
    half = length // 2

    def z_at(step):
        return lax.rem(z + step, 4)

    def z_device(step):
        return (dp, 2 * z_at(step) + y)

    def remote(src, dst, place, device, recv_place=None):
        return pltpu.make_async_remote_copy(
            src_ref=src,
            dst_ref=dst,
            send_sem=sends.at[place],
            recv_sem=recvs.at[place if recv_place is None else recv_place],
            device_id=device,
            device_id_type=MESH,
        )

    def arrived(region, place, device):
        remote(region, region, place, device).wait_recv()

    barrier = pltpu.get_barrier_semaphore()
    me = c * 8 + ctx
    for other in range(1, 16):
        there = lax.rem(me + other, 16)
        pl.semaphore_signal(
            barrier, inc=1, device_id=(2 * x + lax.div(there, 8), lax.rem(there, 8)), device_id_type=MESH
        )
    pl.semaphore_signal(barrier, inc=1, device_id=x_next, device_id_type=MESH)
    pl.semaphore_signal(barrier, inc=1, device_id=x_cross, device_id_type=MESH)
    pl.semaphore_wait(barrier, 17)

    weight = {n: getattr(at, "w_" + n) for n in ORDER}
    shard = {n: getattr(at, "in_" + n) for n in ORDER}
    s0 = {n: places.take(3 if n in FEED else 1) for n in ORDER}
    lc = {n: places.take() for n in ORDER}
    pieces = []
    for n in ORDER:
        start = 0
        for size in PIECES[n]:
            pieces.append((n, pl.ds(start, size), places.take(4), places.take(), None if n in FEED else places.take()))
            start += size
    gather_sends = {n: [] for n in ORDER}

    def part(name, xx, cc):
        width = KEYS if name == "k" else WIDTHS[name]
        which = 2 * xx + cc if name in FEED else cc
        return shard[name].at[:, pl.ds(pl.multiple_of(which * width, width), width)]

    def keys_at(ref):
        return ref.at[:, pl.ds(0, KEYS)]

    def local(name):
        if name == "k":
            return pltpu.make_async_copy(part(name, x, c), keys_at(weight[name].at[x, c, z, y]), recvs.at[lc[name]])
        return pltpu.make_async_copy(part(name, x, c), weight[name].at[x, c, z, y], recvs.at[lc[name]])

    def begin(name, copy):
        copy.start()
        gather_sends[name].append(copy)

    extra_place = places.take()

    def gather_extra():
        rows = at.share_rows
        rows[...] = jnp.zeros_like(rows)
        for i, gain in enumerate((at.attention_gain, at.feedforward_gain, at.query_gain, at.key_gain)):
            rows[i : i + 1, : gain.shape[1]] = gain[...].astype(F32)
        columns = rows[...].T[: at.extra.shape[0]].astype(BF)
        at.extra[...] = columns
        weight["k"][x, c, z, y, :, KEYS:] = columns
        here = weight["k"].at[x, c, z, y, :, pl.ds(KEYS, 128)]
        begin("k", remote(at.extra, here, extra_place, sibling))

    def gather_core(name):
        here = weight[name].at[x, c, z, y]
        begin(name, remote(part(name, x, oc), keys_at(here) if name == "k" else here, s0[name], sibling))
        if name in FEED:
            begin(name, remote(part(name, ox, c), here, s0[name] + 1, x_next))
            begin(name, remote(part(name, ox, oc), here, s0[name] + 2, x_cross))
        local(name).start()

    def gather_core_done(name):
        w = weight[name]
        local(name).wait()
        if name == "k":
            arrived(keys_at(w.at[x, oc, z, y]), s0[name], sibling)
        else:
            arrived(w.at[x, oc, z, y], s0[name], sibling)
        if name in FEED:
            arrived(w.at[ox, c, z, y], s0[name] + 1, x_next)
            arrived(w.at[ox, oc, z, y], s0[name] + 2, x_cross)

    middle = (z == 1) | (z == 2)
    far = jnp.where(z == 1, 3, 0)

    def z_block(piece, zz):
        name, columns = piece[:2]
        w = weight[name]
        return w.at[:, :, zz, y, :, columns] if name in FEED else w.at[x, :, zz, y, :, columns]

    def z_copies(piece):
        block = z_block(piece, z)
        for there in range(4):
            distance = jnp.abs(there - z)
            sending = (distance == 1) | (distance == 2)
            yield sending, lambda there=there: remote(
                block, block, piece[2] + there, (dp, 2 * there + y), piece[2] + z
            )

    def z_forward(piece):
        block = z_block(piece, far)
        return remote(block, block, piece[2] + z, (dp, 2 * (3 - far) + y), piece[2] + far)

    def gather_z(number):
        piece = pieces[number]
        if piece[1].start == 0:
            gather_core_done(piece[0])
        if number == 1:
            arrived(weight["k"].at[x, oc, z, y, :, pl.ds(KEYS, 128)], extra_place, sibling)
        for sending, copy in z_copies(piece):
            pl.when(sending)(lambda copy=copy: copy().start())

    def gather_two(number):
        piece = pieces[number]
        name, columns, sem, y_sem, _ = piece
        w = weight[name]

        @pl.when(middle)
        def _():
            arrived(z_block(piece, far), sem + far, (dp, 2 * far + y))
            z_forward(piece).start()

        for source in range(4):
            waiting = (z != source) & jnp.logical_not(middle & (far == source))
            pl.when(waiting)(
                lambda source=source: arrived(z_block(piece, source), sem + source, (dp, 2 * source + y))
            )
        block = w.at[:, :, :, y, :, columns] if name in FEED else w.at[x, :, :, y, :, columns]
        begin(name, remote(block, block, y_sem, y_next))

    def gather_three(number):
        name, columns, _, y_sem, x_sem = pieces[number]
        w = weight[name]
        arrived(w.at[x, :, :, oy, :, columns], y_sem, y_next)
        block = w.at[x, :, :, :, :, columns]
        begin(name, remote(block, block, x_sem, x_next))

    def gather_done(name):
        w = weight[name]
        for piece in pieces:
            if piece[0] == name and name in FEED:
                arrived(w.at[:, :, :, oy, :, piece[1]], piece[3], y_next)
            elif piece[0] == name:
                arrived(w.at[ox, :, :, :, :, piece[1]], piece[4], x_next)

    def gather_sent(name):
        for copy in gather_sends[name]:
            copy.wait_send()
        for piece in pieces:
            if piece[0] == name:
                for sending, copy in z_copies(piece):
                    pl.when(sending)(lambda copy=copy: copy().wait_send())
                pl.when(middle)(lambda piece=piece: z_forward(piece).wait_send())

    slot = 2 * lax.rem(z, 2) + y
    target_core = lax.div(z, 2)

    class Reshard:
        def __init__(self, source, landing):
            self.source, self.landing = source, landing
            self.place, self.recv, self.own = places.take(4), places.take(4), places.take()

        def device(self, m):
            return (2 * x + target_core, 2 * m + c)

        def keeps(self, m):
            return (target_core == c) & (z == m) & (y == c)

        def copy(self, m):
            return remote(
                self.source.at[m], self.landing(target_core, slot), self.place + m, self.device(m), self.recv + slot
            )

        def keep(self, m):
            return pltpu.make_async_copy(
                self.source.at[m], self.landing(target_core, slot), recvs.at[self.own]
            )

        def start(self):
            for m in range(MB):
                pl.when(jnp.logical_not(self.keeps(m)))(lambda m=m: self.copy(m).start())
                pl.when(self.keeps(m))(lambda m=m: self.keep(m).start())

        def wait(self):
            for j in range(4):
                mine = (y == c) & (4 * c + j == ctx)
                region = self.landing(c, j)
                device = (2 * x + y, 4 * c + j)
                pl.when(jnp.logical_not(mine))(
                    lambda j=j, region=region, device=device: arrived(region, self.recv + j, device)
                )
                pl.when(mine)(
                    lambda region=region: pltpu.make_async_copy(
                        region, region, recvs.at[self.own]
                    ).wait()
                )

        def sent(self):
            for m in range(MB):
                pl.when(jnp.logical_not(self.keeps(m)))(lambda m=m: self.copy(m).wait_send())

    class Return:
        def __init__(self, source, landing):
            self.source, self.landing = source, landing
            self.place, self.recv, self.own = places.take(4), places.take(4), places.take()

        def keeps(self, j):
            return (y == c) & (4 * c + j == ctx)

        def copy(self, j):
            return remote(
                self.source.at[j], self.landing.at[z], self.place + j, (2 * x + y, 4 * c + j), self.recv + z
            )

        def keep(self, j):
            return pltpu.make_async_copy(
                self.source.at[j], self.landing.at[z], recvs.at[self.own]
            )

        def start(self, j):
            pl.when(jnp.logical_not(self.keeps(j)))(lambda: self.copy(j).start())
            pl.when(self.keeps(j))(lambda: self.keep(j).start())

        def finish(self):
            for j in range(4):
                pl.when(jnp.logical_not(self.keeps(j)))(lambda j=j: self.copy(j).wait_send())
                pl.when(self.keeps(j))(lambda j=j: self.keep(j).wait())
            for m in range(MB):
                mine = (target_core == c) & (z == m) & (y == c)
                device = (2 * x + target_core, 2 * m + c)
                pl.when(jnp.logical_not(mine))(
                    lambda m=m, device=device: arrived(self.landing.at[m], self.recv + m, device)
                )

    hidden_own, cot_all = at.hidden_own, at.cot_all
    hidden_move = Reshard(at.hidden_in, lambda core, j: hidden_own.at[j])
    number_move = Reshard(at.number_out, lambda core, j: at.number_own.at[j])
    cot_move = Reshard(at.cotangent, lambda core, j: cot_all.at[4 * (2 * x + core) + j])
    out_move = Return(at.out_own, at.block_out)
    grad_move = Return(at.grad_own, at.input_grad)
    class Swap:
        def __init__(self, source, there, here):
            self.place = places.take()
            self.out = remote(source, there, self.place, sibling)
            self.here = here

        def start(self):
            self.out.start()

        def wait(self):
            self.out.wait_send()
            arrived(self.here, self.place, sibling)

    def swap_rows(ref):
        mine, theirs = ref.at[pl.ds(own_at, own_rows)], ref.at[pl.ds(other_at, own_rows)]
        return Swap(mine, mine, theirs)

    own_at = pl.multiple_of(c * own_rows, own_rows)
    other_at = pl.multiple_of(oc * own_rows, own_rows)

    class Spread:
        def __init__(self, block):
            self.block = block
            self.place = places.take(3)

        def start(self):
            own = self.block(x, c)
            self.near = remote(own, own, self.place, sibling)
            self.across = remote(own, own, self.place + 1, x_next)
            self.near.start()
            self.across.start()

        def near_wait(self):
            arrived(self.block(x, oc), self.place, sibling)

        def pass_on(self):
            arrived(self.block(ox, c), self.place + 1, x_next)
            block = self.block(ox, c)
            self.far = remote(block, block, self.place + 2, sibling)
            self.far.start()

        def far_wait(self):
            arrived(self.block(ox, oc), self.place + 2, sibling)

        def sent(self):
            for copy in (self.near, self.across, self.far):
                copy.wait_send()

    r1 = {n: places.take(1 if n in FEED else 2) for n in ORDER}
    r2 = {n: places.take(0 if n in FEED else 2) for n in ORDER}
    r3 = {n: places.take(4) for n in ORDER}
    r4 = {n: places.take(3 if n in FEED else 1) for n in ORDER}
    sum_sends = []
    grads = dict(weight, d=at.grad_d)

    def send(copy):
        copy.start()
        sum_sends.append(copy)

    def sum_block(name, zz):
        w = grads[name]
        return w.at[:, :, zz, y] if name in FEED else w.at[x, :, zz, y]

    end = jnp.logical_not(middle)
    neighbour = jnp.where(z == 0, 1, 2)

    def sum_z_copies(name):
        landing = getattr(at, "r3_" + name)
        for there in range(4):
            distance = jnp.abs(there - z)
            sending = (distance == 1) | ((distance == 2) & end)
            yield sending, lambda there=there: remote(
                sum_block(name, there), landing.at[z], r3[name] + there, (dp, 2 * there + y), r3[name] + z
            )

        yield end, lambda: remote(
            sum_block(name, 3 - z), landing.at[neighbour], r3[name] + z, (dp, 2 * neighbour + y), r3[name] + neighbour
        )

    def sum_z_late(name):
        landing = getattr(at, "r3_" + name)
        return remote(sum_block(name, far), landing.at[z], r3[name] + far, (dp, 2 * far + y), r3[name] + z)

    def sum_z(name):
        for sending, copy in sum_z_copies(name):
            pl.when(sending)(lambda copy=copy: copy().start())

    def sum_z_pass(name):
        landing, w = getattr(at, "r3_" + name), grads[name]

        @pl.when(middle)
        def _():
            arrived(landing.at[z], r3[name] + z, (dp, 2 * (3 - far) + y))
            if name in FEED:
                for xx in range(2):
                    for cc in range(2):
                        w[xx, cc, far, y] += landing[z, xx, cc]
            else:
                for cc in range(2):
                    w[x, cc, far, y] += landing[z, cc]
            sum_z_late(name).start()

    def sum_one(name):
        w = grads[name]
        if name in FEED:
            send(remote(w.at[:, :, :, oy], getattr(at, "r1a_" + name), r1[name], y_next))
            return
        first, second = split_columns(name)
        send(remote(w.at[:, :, :, oy, :, pl.ds(0, first)], getattr(at, "r1a_" + name), r1[name], y_next))
        if second:
            send(remote(w.at[ox, :, :, :, :, pl.ds(first, second)], getattr(at, "r1b_" + name), r1[name] + 1, x_next))

    def sum_two(name):
        w = grads[name]
        arrived(getattr(at, "r1a_" + name), r1[name], y_next)
        first, second = (WIDTHS[name], 0) if name in FEED else split_columns(name)

        @pl.loop(0, 16)
        def _(i):
            xx, cc, zz = lax.div(i, 8), lax.rem(lax.div(i, 4), 2), lax.rem(i, 4)
            w[xx, cc, zz, y, :, pl.ds(0, first)] += getattr(at, "r1a_" + name)[xx, cc, zz]

        if name in FEED:
            sum_z(name)
            return
        send(remote(w.at[ox, :, :, y, :, pl.ds(0, first)], getattr(at, "r2a_" + name), r2[name], x_next))
        if second:
            arrived(getattr(at, "r1b_" + name), r1[name] + 1, x_next)

            @pl.loop(0, 16)
            def _(i):
                cc, zz, yy = lax.div(i, 8), lax.rem(lax.div(i, 2), 4), lax.rem(i, 2)
                w[x, cc, zz, yy, :, pl.ds(first, second)] += getattr(at, "r1b_" + name)[cc, zz, yy]

            send(remote(w.at[x, :, :, oy, :, pl.ds(first, second)], getattr(at, "r2b_" + name), r2[name] + 1, y_next))

    def sum_three(name):
        w = grads[name]
        first, second = split_columns(name)
        arrived(getattr(at, "r2a_" + name), r2[name], x_next)
        if second:
            arrived(getattr(at, "r2b_" + name), r2[name] + 1, y_next)

        @pl.loop(0, 8)
        def _(i):
            cc, zz = lax.div(i, 4), lax.rem(i, 4)
            w[x, cc, zz, y, :, pl.ds(0, first)] += getattr(at, "r2a_" + name)[cc, zz]
            if second:
                w[x, cc, zz, y, :, pl.ds(first, second)] += getattr(at, "r2b_" + name)[cc, zz]

        sum_z(name)

    def sum_four(name):
        w, landed = grads[name], getattr(at, "r3_" + name)
        for source in range(4):
            coming = (z != source) & (jnp.abs(source - z) != 3)
            pl.when(coming)(
                lambda source=source: arrived(landed.at[source], r3[name] + source, (dp, 2 * source + y))
            )

        def total(*place):
            mine = w[(*place, z, y)] if name in FEED else w[(x, *place, z, y)]
            value = mine.astype(F32)
            value = value + landed[(jnp.where(z == 0, 1, z - 1), *place)].astype(F32)
            value = value + landed[(jnp.where(z == 0, 2, jnp.where(z == 3, 1, z + 1)), *place)].astype(F32)
            third = landed[(far, *place)].astype(F32)
            return jnp.where(middle, value + third, value)

        width = WIDTHS[name]
        staged, result = getattr(at, "r4_" + name), getattr(at, "out_" + name)
        if name in FEED:
            columns = pl.ds(pl.multiple_of(dp * width, width), width)
            for i, (xx, cc, device) in enumerate(((ox, oc, x_cross), (ox, c, x_next), (x, oc, sibling))):
                staged[i] = total(xx, cc)
                send(remote(staged.at[i], result.at[:, columns], r4[name] + i, device))
            result[:, columns] = total(x, c)
            return
        staged[...] = total(oc)
        columns = pl.ds(pl.multiple_of(c * width, width), width)
        send(remote(staged, result.at[:, columns], r4[name], sibling))
        result[:, columns] = total(c)

    def sum_done(name):
        width = WIDTHS[name]
        if name in FEED:
            for i, (xx, cc, device) in enumerate(((ox, oc, x_cross), (ox, c, x_next), (x, oc, sibling))):
                columns = pl.ds(pl.multiple_of((2 * xx + cc) * width, width), width)
                arrived(getattr(at, "out_" + name).at[:, columns], r4[name] + i, device)
        else:
            columns = pl.ds(pl.multiple_of(oc * width, width), width)
            arrived(getattr(at, "out_" + name).at[:, columns], r4[name], sibling)

    gains, head_gains = at.gains, at.head_gains
    scaled, ff_in, grad_proj = at.scaled, at.ff_in, at.grad_proj
    residual, grad_residual = at.residual, at.grad_residual
    acc_own = at.acc_own
    scaled_swap, proj_swap = swap_rows(scaled), swap_rows(grad_proj)
    ff_spread = Spread(lambda xx, cc: ff_in.at[2 * xx + cc])
    cot_spread = Spread(lambda xx, cc: cot_all.at[pl.ds(4 * (2 * xx + cc), 4)])
    partials = [Swap(at.partial_out.at[i], at.partial_in.at[i], at.partial_in.at[i]) for i in range(2)]
    feed_near = [
        [Swap(at.near_out.at[i, k], at.near_in.at[i, k], at.near_in.at[i, k]) for k in range(2)] for i in range(2)
    ]
    feed_cross = []
    for i in range(2):
        place = places.take()
        feed_cross.append((remote(at.cross_out.at[i], at.cross_in.at[i], place, x_next), place))

    def selector():
        row = lax.broadcasted_iota(jnp.int32, (D, HD), 0)
        column = lax.broadcasted_iota(jnp.int32, (D, HD), 1)
        local_row = row & 31
        hit = ((row >> 5) * 4 + local_row == column) & (local_row < 4)
        return jnp.where(hit, 1.0, 0.0).astype(BF)

    def prepare_gains():
        columns = weight["k"][:, :, :, :, :, KEYS:].reshape(D, 128).astype(F32)
        for i in range(8):
            gains[:, i * 128 : (i + 1) * 128] = columns[i * 128 : (i + 1) * 128].T[:8]
        head_gains[...] = dot(gains[...].astype(BF), selector())

    def prepare_numbers():
        for m in range(MB):
            at.share_rows[:1, :tokens] = at.segments[m].astype(F32)
            at.number_out[m] = jnp.broadcast_to(at.share_rows[:1], (128, 128)).T[:tokens].astype(BF)

    def prepare_mask():
        def number(i):
            return scaled[i * 128 : (i + 1) * 128, D:].astype(F32)

        for j in range(4):
            key = number(j).T
            for i in range(4):
                place = slice(i * 128, (i + 1) * 128), slice(j * 128, (j + 1) * 128)
                if j > i:
                    at.bias[place] = jnp.full((128, 128), MASKED, F32)
                    continue
                seen = number(i) == key
                if i == j:
                    seen = seen & (
                        lax.broadcasted_iota(jnp.int32, (128, 128), 1)
                        <= lax.broadcasted_iota(jnp.int32, (128, 128), 0)
                    )
                at.bias[place] = jnp.where(seen, 0.0, MASKED)

    def own_block(j):
        return pl.ds(pl.multiple_of(c * own_rows + j * tokens, tokens), tokens)

    def here_block(j):
        return pl.ds(pl.multiple_of(j * tokens, tokens), tokens)

    def scale_input():
        @pl.loop(0, 4)
        def _(j):
            value = normalize(hidden_own[j].astype(F32)) * gains[0:1]
            scaled[own_block(j), :D] = value.astype(BF)
            scaled[own_block(j), D:] = at.number_own[j]

    def columns_of(name, t, size=256):
        return weight[name][:, :, :, :, :, pl.ds(pl.multiple_of(t * size, size), size)].reshape(D, size)

    def rows_of(name, t):
        if name == "k":
            return weight[name][lax.div(t, 2), lax.rem(t, 2), :, :, :, :KEYS].reshape(D // 4, KEYS)
        return weight[name][lax.div(t, 2), lax.rem(t, 2)].reshape(D // 4, WIDTHS[name])

    cosine, sine = at.cosine, at.sine

    def turn(value):
        return value * cosine[...] + pltpu.roll(value, HD // 2, 1) * sine[...]

    def project_heads(name, count, gain, kept, turned):
        @pl.loop(0, count // 2)
        def _(t):
            both = dot(scaled[:, :D], columns_of(name, t))
            for i in range(2):
                value = both[:, i * HD : (i + 1) * HD]
                kept[2 * t + i] = value
                turned[2 * t + i] = turn(normalize(value) * gain).astype(BF)

    def project_values():
        @pl.loop(0, WIDTHS["v"] // 256)
        def _(t):
            both = dot(scaled[:, :D], columns_of("v", t))
            for i in range(2):
                at.values[2 * t + i] = both[:, i * HD : (i + 1) * HD].astype(BF)

    def probabilities(head, pair, block):
        rows = slice(block * half, (block + 1) * half)
        seen = slice(0, (block + 1) * half)
        scores = dot_nt(at.queries[head, rows], at.keys[pair, seen]) * SCALE + at.bias[rows, seen]
        terms = jnp.exp(scores - jnp.max(scores, axis=-1, keepdims=True))
        return terms * (1.0 / jnp.sum(terms, axis=-1, keepdims=True))

    def attend(first, last):
        @pl.loop(first, last)
        def _(head):
            pair = lax.div(head, 2)
            for block in range(2):
                seen = slice(0, (block + 1) * half)
                low = probabilities(head, pair, block).astype(BF)
                at.mixed[
                    block * half : (block + 1) * half, pl.ds(pl.multiple_of(head * HD, HD), HD)
                ] = dot(low, at.values[pair, seen]).astype(BF)

    def column_quarters(body):
        @pl.loop(0, 4)
        def _(t):
            body(t, pl.ds(pl.multiple_of(t * (D // 4), D // 4), D // 4))

    def partial_product(index, terms):
        def rows_times(first, t):
            return sum(dot_nt(left(pl.ds(first, own_rows)), rows_of(name, t)) for left, name in terms)

        def theirs(t, columns):
            at.partial_out[index, :, columns] = rows_times(other_at, t).astype(BF)

        def mine(t, columns):
            acc_own[:, columns] = rows_times(own_at, t)

        column_quarters(theirs)
        partials[index].start()
        column_quarters(mine)

    def own_sum(index, j):
        return acc_own[here_block(j)] + at.partial_in[index, here_block(j)].astype(F32)

    def feed_product(index, terms):
        def rows_times(xx, cc, t):
            first = pl.multiple_of((2 * xx + cc) * own_rows, own_rows)
            return sum(dot_nt(left[pl.ds(first, own_rows)], rows_of(name, t)) for left, name in terms)

        def give(k, xx):
            def body(t, columns):
                at.near_out[index, k, :, columns] = rows_times(xx, oc, t).astype(BF)

            column_quarters(body)
            feed_near[index][k].start()

        def keep(xx):
            def body(t, columns):
                acc_own[:, columns] = rows_times(xx, c, t)

            column_quarters(body)

        give(0, ox)
        keep(ox)
        feed_near[index][0].wait()
        near = at.near_in

        @pl.loop(0, 4)
        def _(j):
            rows = here_block(j)
            at.cross_out[index, rows] = (acc_own[rows] + near[index, 0, rows].astype(F32)).astype(BF)

        feed_cross[index][0].start()
        give(1, x)
        keep(x)

    def feed_wait(index):
        feed_near[index][1].wait()
        copy, place = feed_cross[index]
        copy.wait_send()
        arrived(at.cross_in.at[index], place, x_next)

    def feed_sum(index, j):
        rows = here_block(j)
        return acc_own[rows] + at.near_in[index, 1, rows].astype(F32) + at.cross_in[index, rows].astype(F32)

    def add_residual():
        @pl.loop(0, 4)
        def _(j):
            value = hidden_own[j].astype(F32) + own_sum(0, j)
            residual[here_block(j)] = value
            ff_in[2 * x + c, here_block(j)] = (normalize(value) * gains[1:2]).astype(BF)

    gate_part, up_part, hidden_low = at.gate_part, at.up_part, at.hidden_low

    def chip_rows(xx):
        return pl.ds(pl.multiple_of(xx * length, length), length)

    def feed_forward(xx):
        rows = chip_rows(xx)

        @pl.loop(0, WIDTHS["g"] // 256)
        def _(t):
            columns = pl.ds(pl.multiple_of(t * 256, 256), 256)
            left = ff_in[pl.ds(2 * xx, 2)].reshape(length, D)
            gate = dot(left, columns_of("g", t))
            up = dot(left, columns_of("u", t))
            sigmoid = 1.0 / (1.0 + jnp.exp(-gate))
            swish = gate * sigmoid
            hidden_low[rows, columns] = (swish * up).astype(BF)
            up_part[rows, columns] = swish.astype(BF)
            gate_part[rows, columns] = (up * sigmoid * (1.0 + gate * (1.0 - sigmoid))).astype(BF)

    def write_out():
        @pl.loop(0, 4)
        def _(j):
            at.out_own[j] = (residual[here_block(j)] + feed_sum(0, j)).astype(BF)

        for j in range(4):
            out_move.start(j)

    def grad_hidden():
        @pl.loop(0, 2 * (WIDTHS["d"] // 256))
        def _(i):
            xx, t = lax.div(i, 3), lax.rem(i, 3)
            rows, columns = chip_rows(xx), pl.ds(pl.multiple_of(t * 256, 256), 256)
            grad = dot(cot_all[pl.ds(8 * xx, 8)].reshape(length, D), columns_of("d", t))
            gate_part[rows, columns] = (grad * gate_part[rows, columns].astype(F32)).astype(BF)
            up_part[rows, columns] = (grad * up_part[rows, columns].astype(F32)).astype(BF)

    turned_rows = at.turned_rows

    def transpose_rows(load, count):
        @pl.loop(0, D // 128)
        def _(t):
            place = pl.ds(pl.multiple_of(t * 128, 128), 128)
            turned_rows[place, :count] = load(place).reshape(count, 128).T

    def weight_grad(name, right, count):
        if name != "d":
            gather_sent(name)

        @pl.loop(0, (KEYS if name == "k" else WIDTHS[name]) // 256)
        def _(t):
            columns = pl.ds(pl.multiple_of(t * 256, 256), 256)
            grad = dot(turned_rows[:, :count], right(columns))
            grads[name][:, :, :, :, :, columns] = grad.astype(BF).reshape(2, 2, 4, 2, 32, 256)

    grad_gains = at.grad_gains

    def back_residual():
        grad_gains[...] = jnp.zeros_like(grad_gains)

        @pl.loop(0, 4)
        def _(j):
            value = residual[here_block(j)]
            grad = feed_sum(1, j)
            scale = lax.rsqrt(jnp.mean(value * value, axis=-1, keepdims=True) + NORM_EPS)
            grad_gains[1:2] += jnp.sum(grad * (value * scale), axis=0, keepdims=True)
            total = cot_all[4 * (2 * x + c) + j].astype(F32) + norm_back(value, grad * gains[1:2])
            grad_residual[here_block(j)] = total
            grad_proj[own_block(j)] = total.astype(BF)

    grad_mixed, grad_heads = ff_in, cot_all

    def back_mixed():
        @pl.loop(0, WIDTHS["o"] // 256)
        def _(t):
            columns = pl.ds(pl.multiple_of(t * 256, 256), 256)
            grad = dot(grad_proj[...], columns_of("o", t)).astype(BF)
            grad_mixed[:2, :, columns] = grad.reshape(2, half, 256)

    def put_heads(first, columns, value):
        grad_heads[first : first + 8, :, columns] = value.astype(BF).reshape(8, tokens, HD)

    def head_columns(first, columns):
        return grad_heads[first : first + 8, :, columns].reshape(length, columns.size)

    def head_rows(first, rows, start, width):
        block = first + lax.div(rows.start, tokens)
        return grad_heads[pl.ds(block, 4), :, start : start + width].reshape(own_rows, width)

    grad_head_gains = at.grad_head_gains

    def turn_back(value):
        return value * cosine[...] - pltpu.roll(value, HD // 2, 1) * sine[...]

    def back_head(value, grad, row, first, columns):
        scale = lax.rsqrt(jnp.mean(value * value, axis=-1, keepdims=True) + NORM_EPS)
        turned = turn_back(grad)
        grad_head_gains[row : row + 1] += jnp.sum(turned * (value * scale), axis=0, keepdims=True)
        put_heads(first, columns, norm_back(value, turned * head_gains[row : row + 1]))

    grad_key, grad_value, grad_query = at.grad_key, at.grad_value, at.grad_query

    def back_attend(first, last):
        if first == 0:
            grad_head_gains[...] = jnp.zeros_like(grad_head_gains)

        @pl.loop(first, last)
        def _(pair):
            for i in range(2):
                head = 2 * pair + i
                lanes = pl.ds(pl.multiple_of(head * HD, HD), HD)
                for block in (1, 0):
                    rows = slice(block * half, (block + 1) * half)
                    seen = slice(0, (block + 1) * half)
                    probs = probabilities(head, pair, block)
                    grad_out = grad_mixed[block, :, lanes]
                    grad_probs = dot_nt(grad_out, at.values[pair, seen])
                    delta = jnp.sum(probs * grad_probs, axis=-1, keepdims=True)
                    grad_scores = (probs * (grad_probs - delta)).astype(BF)
                    grad_query[rows] = dot(grad_scores, at.keys[pair, seen]) * SCALE
                    key_part = dot_tn(grad_scores, at.queries[head, rows]) * SCALE
                    value_part = dot_tn(probs.astype(BF), grad_out)
                    if i == 0 and block == 1:
                        grad_key[...] = key_part
                        grad_value[...] = value_part
                    else:
                        grad_key[seen] += key_part
                        grad_value[seen] += value_part
                back_head(at.query_acc[head], grad_query[...], 2, 0, lanes)
            lanes = pl.ds(pl.multiple_of(pair * HD, HD), HD)
            back_head(at.key_acc[pair], grad_key[...], 3, 8, lanes)
            put_heads(8, pl.ds(pl.multiple_of(KEYS + pair * HD, HD), HD), grad_value[...])

    def back_input():
        @pl.loop(0, 4)
        def _(j):
            value = hidden_own[j].astype(F32)
            grad = own_sum(1, j)
            scale = lax.rsqrt(jnp.mean(value * value, axis=-1, keepdims=True) + NORM_EPS)
            grad_gains[0:1] += jnp.sum(grad * (value * scale), axis=0, keepdims=True)
            at.grad_own[j] = (
                grad_residual[here_block(j)] + norm_back(value, grad * gains[0:1])
            ).astype(BF)

        for j in range(4):
            grad_move.start(j)

    def gain_grads():
        grad_gains[...] += dot_nt(grad_head_gains[...].astype(BF), selector())
        for i in range(8):
            block = jnp.concatenate(
                [grad_gains[:, i * 128 : (i + 1) * 128], jnp.zeros((120, 128), F32)], axis=0
            ).T
            weight["k"][i // 4, (i // 2) % 2, 2 * (i % 2) : 2 * (i % 2) + 2, :, :, KEYS:] = block.astype(BF).reshape(
                2, 2, 32, 128
            )

    gather_core("k")
    gather_extra()
    gather_z(0)
    gather_core("v")
    gather_z(1)
    for name in ("q", "o", *FEED):
        gather_core(name)
    prepare_numbers()
    gather_two(0)
    gather_z(2)
    gather_two(1)
    gather_three(0)
    gather_z(3)
    gather_two(2)
    gather_three(1)
    gather_z(4)
    hidden_move.start()
    number_move.start()
    gather_two(3)
    gather_three(2)
    gather_z(5)
    gather_two(4)
    gather_three(3)
    gather_z(6)
    gather_two(5)
    gather_three(4)
    gather_z(7)
    gather_done("k")
    prepare_gains()
    hidden_move.wait()
    number_move.wait()
    scale_input()
    scaled_swap.start()
    gather_two(6)
    gather_three(5)
    gather_z(8)
    scaled_swap.wait()
    prepare_mask()
    project_heads("k", HALF_HK, head_gains[3:4], at.key_acc, at.keys)
    gather_done("v")
    project_values()
    gather_three(6)
    gather_two(7)
    gather_z(9)
    gather_done("q")
    project_heads("q", HALF_HQ, head_gains[2:3], at.query_acc, at.queries)
    gather_two(8)
    gather_z(10)
    cot_move.start()
    attend(0, 4)
    gather_two(9)
    attend(4, 8)
    gather_done("o")
    partial_product(0, [(lambda rows: at.mixed[rows], "o")])
    gather_two(10)
    partials[0].wait()
    add_residual()
    ff_spread.start()
    cot_move.wait()
    cot_spread.start()
    gather_done("g")
    gather_done("u")
    ff_spread.near_wait()
    feed_forward(x)
    ff_spread.pass_on()
    cot_spread.pass_on()
    cot_spread.near_wait()
    cot_spread.far_wait()
    transpose_rows(lambda columns: cot_all[:, :, columns], 2 * length)
    ff_spread.far_wait()
    feed_forward(ox)

    weight_grad("d", lambda columns: hidden_low[:, columns], 2 * length)
    sum_one("d")
    gather_done("d")
    grad_hidden()
    feed_product(1, [(gate_part, "g"), (up_part, "u")])
    transpose_rows(lambda columns: ff_in[:, :, columns], 2 * length)
    weight_grad("g", lambda columns: gate_part[:, columns], 2 * length)
    sum_one("g")
    weight_grad("u", lambda columns: up_part[:, columns], 2 * length)
    sum_one("u")
    feed_wait(1)
    back_residual()
    proj_swap.start()
    ff_spread.sent()
    cot_spread.sent()
    sum_two("d")
    proj_swap.wait()
    back_mixed()
    transpose_rows(lambda columns: grad_proj[:, columns], length)
    weight_grad("o", lambda columns: at.mixed[:, columns], length)
    sum_one("o")
    back_attend(0, 2)
    sum_two("g")
    sum_z_pass("d")
    back_attend(2, 4)
    sum_two("u")
    sum_z_pass("g")
    partial_product(
        1,
        [
            (lambda rows: head_rows(0, rows, 0, WIDTHS["q"]), "q"),
            (lambda rows: head_rows(8, rows, 0, KEYS), "k"),
            (lambda rows: head_rows(8, rows, KEYS, KEYS), "v"),
        ],
    )
    transpose_rows(lambda columns: scaled[:, columns], length)
    weight_grad("q", lambda columns: head_columns(0, columns), length)
    sum_one("q")
    weight_grad("v", lambda columns: head_columns(8, pl.ds(columns.start + KEYS, 256)), length)
    sum_one("v")
    weight_grad("k", lambda columns: head_columns(8, columns), length)
    partials[1].wait()
    back_input()
    gain_grads()
    sum_one("k")
    sum_two("o")
    sum_z_pass("u")
    sum_four("d")
    feed_product(0, [(hidden_low, "d")])
    feed_wait(0)
    write_out()
    sum_three("o")
    sum_four("g")
    sum_two("q")
    sum_z_pass("o")
    sum_four("u")
    sum_three("q")
    sum_two("v")
    sum_z_pass("q")
    sum_four("o")
    sum_three("v")
    sum_two("k")
    sum_z_pass("v")
    sum_four("q")
    sum_three("k")
    sum_z_pass("k")
    sum_four("v")
    sum_four("k")
    for name in ("d", "g", "u", "o", "q", "v", "k"):
        sum_done(name)
    for copy in sum_sends:
        copy.wait_send()
    for name in ORDER:
        for sending, copy in sum_z_copies(name):
            pl.when(sending)(lambda copy=copy: copy().wait_send())
        pl.when(middle)(lambda name=name: sum_z_late(name).wait_send())
    gather_sent("d")
    hidden_move.sent()
    number_move.sent()
    cot_move.sent()
    out_move.finish()
    grad_move.finish()
    assert places.count == SEMAPHORES, places.count


SEMAPHORES = 204


def fused(
    hidden_in,
    segments,
    attention_gain,
    query_gain,
    key_gain,
    query_weight,
    key_weight,
    value_weight,
    out_weight,
    feedforward_gain,
    gate_weight,
    up_weight,
    down_weight,
    cotangent,
):
    tokens = hidden_in.shape[2]
    length = 8 * tokens
    rows = query_weight.shape[0]
    heads = query_gain.shape[0]
    positions = np.arange(length, dtype=np.float32)
    frequency = (ROPE_BASE ** (-(np.arange(HD // 2, dtype=np.float32) * 2.0) / HD)).astype(np.float32)
    angles = (positions[:, None] * frequency[None, :]).astype(np.float64)
    cosine = np.concatenate([np.cos(angles), np.cos(angles)], axis=-1).astype(np.float32)
    sine = np.concatenate([-np.sin(angles), np.sin(angles)], axis=-1).astype(np.float32)

    vmem, anywhere = pl.BlockSpec(memory_space=pltpu.VMEM), pl.BlockSpec(memory_space=pl.ANY)
    inputs = dict(
        hidden_in=(hidden_in[:, 0], anywhere),
        cotangent=(cotangent[:, 0], anywhere),
        segments=(segments, vmem),
        cosine=(jnp.asarray(cosine), vmem),
        sine=(jnp.asarray(sine), vmem),
        attention_gain=(attention_gain[None], vmem),
        feedforward_gain=(feedforward_gain[None], vmem),
        query_gain=(query_gain[None], vmem),
        key_gain=(key_gain[None], vmem),
        in_k=(key_weight, anywhere),
        in_v=(value_weight, anywhere),
        in_q=(query_weight, anywhere),
        in_o=(out_weight.T, anywhere),
        in_g=(gate_weight, anywhere),
        in_u=(up_weight, anywhere),
        in_d=(down_weight.T, anywhere),
    )
    block = (MB, tokens, D)
    outputs = dict(block_out=(block, BF, anywhere), input_grad=(block, BF, anywhere))
    for name, width in WIDTHS.items():
        outputs["out_" + name] = ((rows, width * (4 if name in FEED else 2)), F32, vmem)
    own = 4 * tokens
    scratch = dict(
        share_rows=((128, 128), F32),
        extra=((rows, 128), BF),
        number_out=((MB, tokens, 128), BF),
        number_own=((4, tokens, 128), BF),
        hidden_own=((4, tokens, D), BF),
        cot_all=((16, tokens, D), BF),
        gains=((8, D), F32),
        head_gains=((8, HD), F32),
        grad_gains=((8, D), F32),
        grad_head_gains=((8, HD), F32),
        bias=((length, length), F32),
        scaled=((length, D + 128), BF),
        query_acc=((HALF_HQ, length, HD), F32),
        key_acc=((HALF_HK, length, HD), F32),
        queries=((HALF_HQ, length, HD), BF),
        keys=((HALF_HK, length, HD), BF),
        values=((HALF_HK, length, HD), BF),
        mixed=((length, HALF_HQ * HD), BF),
        acc_own=((own, D), F32),
        partial_out=((2, own, D), BF),
        partial_in=((2, own, D), BF),
        near_out=((2, 2, own, D), BF),
        near_in=((2, 2, own, D), BF),
        cross_out=((2, own, D), BF),
        cross_in=((2, own, D), BF),
        residual=((own, D), F32),
        grad_residual=((own, D), F32),
        ff_in=((4, own, D), BF),
        gate_part=((2 * length, FF // 4), BF),
        up_part=((2 * length, FF // 4), BF),
        hidden_low=((2 * length, FF // 4), BF),
        grad_d=((2, 2, 4, 2, rows, FF // 4), BF),
        grad_proj=((length, D), BF),
        grad_key=((length, HD), F32),
        grad_value=((length, HD), F32),
        grad_query=((length, HD), F32),
        turned_rows=((D, 2 * length), BF),
        out_own=((4, tokens, D), BF),
        grad_own=((4, tokens, D), BF),
    )
    for name, width in WIDTHS.items():
        scratch["w_" + name] = ((2, 2, 4, 2, rows, width), BF)
        if name in FEED:
            scratch["r1a_" + name] = ((2, 2, 4, rows, width), BF)
            scratch["r3_" + name] = ((4, 2, 2, rows, width), BF)
            scratch["r4_" + name] = ((3, rows, width), F32)
            continue
        first, second = split_columns(name)
        scratch["r1a_" + name] = ((2, 2, 4, rows, first), BF)
        scratch["r2a_" + name] = ((2, 4, rows, first), BF)
        if second:
            scratch["r1b_" + name] = ((2, 4, 2, rows, second), BF)
            scratch["r2b_" + name] = ((2, 4, rows, second), BF)
        scratch["r3_" + name] = ((4, 2, rows, width), BF)
        scratch["r4_" + name] = ((rows, width), F32)
    names = (*inputs, *outputs, *scratch, "sends", "recvs")
    results = pl.pallas_call(
        functools.partial(layer_kernel, names, tokens),
        out_shape=[jax.ShapeDtypeStruct(shape, dtype) for shape, dtype, _ in outputs.values()],
        in_specs=[spec for _, spec in inputs.values()],
        out_specs=[spec for _, _, spec in outputs.values()],
        scratch_shapes=[pltpu.VMEM(shape, dtype) for shape, dtype in scratch.values()]
        + [pltpu.SemaphoreType.DMA((SEMAPHORES,))] * 2,
        compiler_params=pltpu.CompilerParams(
            collective_id=0, has_side_effects=True, vmem_limit_bytes=64 * 2**20 - 2**16
        ),
        name="layer",
    )(*(value for value, _ in inputs.values()))
    got = finish(types.SimpleNamespace(**dict(zip(outputs, results))), rows, heads)
    return (
        got.block_out[:, None],
        got.input_grad[:, None],
        got.attention_gain[0],
        got.query_gain[0],
        got.key_gain[0],
        got.out_q,
        got.out_k,
        got.out_v,
        got.out_o.T,
        got.feedforward_gain[0],
        got.out_g,
        got.out_u,
        got.out_d.T,
    )


def finish_kernel(names, heads, *refs):
    at = types.SimpleNamespace(**dict(zip(names, refs)))
    moved = [n[4:] for n in names if n.startswith("got_")]
    brought = [
        pltpu.make_async_copy(getattr(at, "got_" + n), getattr(at, "here_" + n), at.brought.at[i])
        for i, n in enumerate(moved)
    ]
    for copy in brought:
        copy.start()
    taken = []

    def take(name, source):
        copy = pltpu.make_async_copy(source, getattr(at, name), at.taken.at[len(taken)])
        copy.start()
        taken.append(copy)

    def ready(name):
        brought[moved.index(name)].wait()
        return getattr(at, "here_" + name)

    value = ready("input_grad")
    for m in range(MB):
        at.wide_grad[m] = value[m].astype(F32)
    take("input_grad", at.wide_grad)
    for name in moved:
        if name not in ("input_grad", "out_k"):
            take(name, ready(name))
    value = ready("out_k")
    at.keys[:, :KEYS] = value[:, :KEYS]
    at.keys[:, KEYS:] = value[:, KEYS + 128 : 2 * KEYS + 128]
    take("out_k", at.keys)
    gains = value[:, KEYS : KEYS + 128] + value[:, 2 * KEYS + 128 :]
    blank = jnp.zeros((128 - gains.shape[0], 128), F32)
    turned = jnp.concatenate([gains, blank], axis=0).T
    at.attention_gain[...] = turned[0:1, : gains.shape[0]]
    at.feedforward_gain[...] = turned[1:2, : gains.shape[0]]
    at.query_gain[...] = turned[2:3, :heads]
    at.key_gain[...] = turned[3:4, :heads]
    for copy in taken:
        copy.wait()


def finish(got, rows, heads):
    vmem, anywhere = pl.BlockSpec(memory_space=pltpu.VMEM), pl.BlockSpec(memory_space=pl.ANY)
    inputs = vars(got)
    outputs = {n: (v.shape, v.dtype, anywhere) for n, v in inputs.items()}
    outputs.update(
        input_grad=(got.input_grad.shape, F32, anywhere),
        out_k=((rows, 2 * KEYS), F32, anywhere),
        attention_gain=((1, rows), F32, vmem),
        feedforward_gain=((1, rows), F32, vmem),
        query_gain=((1, heads), F32, vmem),
        key_gain=((1, heads), F32, vmem),
    )
    scratch = {"here_" + n: (v.shape, v.dtype) for n, v in inputs.items()}
    scratch.update(wide_grad=(got.input_grad.shape, F32), keys=((rows, 2 * KEYS), F32))
    names = (*("got_" + n for n in inputs), *outputs, *scratch, "brought", "taken")
    results = pl.pallas_call(
        functools.partial(finish_kernel, names, heads),
        out_shape=[jax.ShapeDtypeStruct(shape, dtype) for shape, dtype, _ in outputs.values()],
        in_specs=[anywhere] * len(inputs),
        out_specs=[spec for _, _, spec in outputs.values()],
        scratch_shapes=[pltpu.VMEM(shape, dtype) for shape, dtype in scratch.values()]
        + [pltpu.SemaphoreType.DMA((len(inputs),))] * 2,
        compiler_params=pltpu.CompilerParams(vmem_limit_bytes=64 * 2**20 - 2**16),
        name="results",
    )(*inputs.values())
    return types.SimpleNamespace(**dict(zip(outputs, results)))


def rope_tables(first, count):
    angles = rope_angles(first, count)
    cosine = jnp.concatenate([jnp.cos(angles), jnp.cos(angles)], axis=-1)
    sine = jnp.concatenate([jnp.sin(angles), jnp.sin(angles)], axis=-1)
    return (cosine[:, None, :], sine[:, None, :])


def rotate(value, cosine, sine):
    half = value.shape[-1] // 2
    turned = jnp.concatenate([-value[..., half:], value[..., :half]], axis=-1)
    return value * cosine + turned * sine


def rotate_back(grad, cosine, sine):
    half = grad.shape[-1] // 2
    scaled = grad * sine
    return grad * cosine + jnp.concatenate([scaled[..., half:], -scaled[..., :half]], axis=-1)


def contract_last(left, right):
    return lax.dot_general(
        left, right, (((1,), (1,)), ((), ())), preferred_element_type=jnp.float32
    )


def contract_first(left, right):
    return lax.dot_general(
        left, right, (((0,), (0,)), ((), ())), preferred_element_type=jnp.float32
    )


def block_rows(rows):
    size = min(rows, 512)
    while rows % size:
        size -= 1
    return size


def over_blocks(state, pieces, update):
    rows = pieces[0].shape[0]
    size = block_rows(rows)
    count = rows // size
    stacked = tuple((piece.reshape((count, size) + piece.shape[1:]) for piece in pieces))
    offsets = size * jnp.arange(count, dtype=jnp.int32)

    def step(current, item):
        block = item[:-1]
        offset = item[-1]
        current = update(current, block, offset)
        return (current, None)

    final, unused = lax.scan(step, state, stacked + (offsets,))
    return final


def general(
    hidden_in,
    segments,
    attention_gain,
    query_gain,
    key_gain,
    query_weight,
    key_weight,
    value_weight,
    out_weight,
    feedforward_gain,
    gate_weight,
    up_weight,
    down_weight,
    cotangent,
):
    tokens = hidden_in.shape[2]
    groups = HQ // HK
    scale = HD ** (-0.5)
    first = lax.axis_index("ctx") * tokens
    length = lax.axis_size("ctx") * tokens
    query_pos = first + jnp.arange(tokens, dtype=jnp.int32)
    cosine, sine = rope_tables(first, tokens)
    sources = (
        query_weight,
        key_weight,
        value_weight,
        gate_weight,
        up_weight,
        out_weight.T,
        down_weight.T,
    )
    whole = lax.all_gather(jnp.concatenate(sources, axis=1), ("dp", "ctx"), axis=0, tiled=True)
    parts = []
    edge = 0
    for source in sources:
        parts.append(whole[:, edge : edge + source.shape[1]])
        edge = edge + source.shape[1]
    whole_query, whole_key, whole_value, whole_gate, whole_up, whole_out, whole_down = parts
    gain_in, gain_query, gain_key, gain_feed = (
        lax.all_gather(gain, ("dp", "ctx"), axis=0, tiled=True)
        for gain in (attention_gain, query_gain, key_gain, feedforward_gain)
    )
    grad_attention_gain = jnp.zeros((D,), jnp.float32)
    grad_feed_gain = jnp.zeros((D,), jnp.float32)
    grad_query_gain = jnp.zeros((HD,), jnp.float32)
    grad_key_gain = jnp.zeros((HD,), jnp.float32)
    outputs = []
    input_grads = []
    stored = []
    for batch in range(MB):
        hidden = hidden_in[batch, 0].astype(jnp.float32)
        query_seg = segments[batch, 0]
        grad_out = cotangent[batch, 0]
        normed = normalize(hidden)
        scaled_in = (normed * gain_in.astype(jnp.float32)).astype(jnp.bfloat16)
        query_heads = jnp.dot(scaled_in, whole_query, preferred_element_type=jnp.float32).reshape(
            tokens, HQ, HD
        )
        key_heads = jnp.dot(scaled_in, whole_key, preferred_element_type=jnp.float32).reshape(
            tokens, HK, HD
        )
        values = jnp.dot(scaled_in, whole_value, preferred_element_type=jnp.float32).astype(
            jnp.bfloat16
        )
        query_norm = normalize(query_heads)
        key_norm = normalize(key_heads)
        query_scale = gain_query.astype(jnp.float32)
        key_scale = gain_key.astype(jnp.float32)
        queries = rotate(query_norm * query_scale, cosine, sine).astype(jnp.bfloat16)
        keys_low = rotate(key_norm * key_scale, cosine, sine).astype(jnp.bfloat16)
        grouped = queries.reshape(tokens, HK, groups, HD)
        keys_flat = keys_low.reshape(tokens, HK * HD)

        def key_scores(keys, key_seg, offset):
            rows = keys.shape[0]
            shaped = keys.reshape(rows, HK, HD)
            raw = (
                jnp.einsum("qkgd,skd->kgqs", grouped, shaped, preferred_element_type=jnp.float32)
                * scale
            )
            key_pos = offset + jnp.arange(rows, dtype=jnp.int32)
            visible = (key_pos[None, :] <= query_pos[:, None]) & (
                key_seg[None, :] == query_seg[:, None]
            )
            return (jnp.where(visible, raw, MASKED), visible, shaped)

        def fold_with(update, state, pieces):
            return over_blocks(state, pieces, update)

        def add_lse(state, block, offset):
            keys, key_seg = block
            masked, visible, shaped = key_scores(keys, key_seg, offset)
            top, total = state
            new_top = jnp.maximum(top, jnp.max(masked, axis=-1))
            terms = jnp.where(visible, jnp.exp(masked - new_top[..., None]), 0.0)
            return (new_top, total * jnp.exp(top - new_top) + jnp.sum(terms, axis=-1))

        start_state = (
            jnp.full((HK, groups, tokens), MASKED, jnp.float32),
            jnp.zeros((HK, groups, tokens), jnp.float32),
        )
        top, total = fold_with(
            add_lse,
            start_state,
            (
                lax.all_gather(keys_flat, "ctx", axis=0, tiled=True),
                lax.all_gather(query_seg, "ctx", axis=0, tiled=True),
            ),
        )
        lse = top + jnp.log(total)

        def add_mixed(state, block, offset):
            keys, values_block, key_seg = block
            masked, visible, shaped = key_scores(keys, key_seg, offset)
            probs = jnp.exp(masked - lse[..., None]).astype(jnp.bfloat16)
            value_heads = values_block.reshape(values_block.shape[0], HK, HD)
            return state + jnp.einsum(
                "kgqs,skd->qkgd", probs, value_heads, preferred_element_type=jnp.float32
            )

        mixed = fold_with(
            add_mixed,
            jnp.zeros((tokens, HK, groups, HD), jnp.float32),
            (
                lax.all_gather(keys_flat, "ctx", axis=0, tiled=True),
                lax.all_gather(values, "ctx", axis=0, tiled=True),
                lax.all_gather(query_seg, "ctx", axis=0, tiled=True),
            ),
        )
        mixed_low = mixed.reshape(tokens, HQ * HD).astype(jnp.bfloat16)
        residual = hidden + contract_last(mixed_low, whole_out)
        feed_normed = normalize(residual)
        feed_scale = gain_feed.astype(jnp.float32)
        ff_in = (feed_normed * feed_scale).astype(jnp.bfloat16)
        gate = jnp.dot(ff_in, whole_gate, preferred_element_type=jnp.float32)
        up_part = jnp.dot(ff_in, whole_up, preferred_element_type=jnp.float32)
        sigmoid = jax.nn.sigmoid(gate)
        swish = gate * sigmoid
        hidden_low = (swish * up_part).astype(jnp.bfloat16)
        block_out = residual + contract_last(hidden_low, whole_down)
        outputs.append(block_out.astype(jnp.bfloat16))
        grad_hidden = jnp.dot(grad_out, whole_down, preferred_element_type=jnp.float32)
        grad_gate = (grad_hidden * up_part * (sigmoid * (1.0 + gate * (1.0 - sigmoid)))).astype(
            jnp.bfloat16
        )
        grad_up = (grad_hidden * swish).astype(jnp.bfloat16)
        grad_feed_in = contract_last(grad_gate, whole_gate) + contract_last(grad_up, whole_up)
        grad_feed_gain = grad_feed_gain + jnp.sum(grad_feed_in * feed_normed, axis=0)
        grad_residual = grad_out.astype(jnp.float32) + norm_back(
            residual, grad_feed_in * gain_feed.astype(jnp.float32)
        )
        grad_proj = grad_residual.astype(jnp.bfloat16)
        grad_mixed = (
            jnp.dot(grad_proj, whole_out, preferred_element_type=jnp.float32).astype(jnp.bfloat16).reshape(tokens, HK, groups, HD)
        )
        delta = jnp.transpose(jnp.sum(grad_mixed.astype(jnp.float32) * mixed, axis=-1), (1, 2, 0))

        def add_grads(state, block, offset):
            grad_query, grad_keys, grad_values = state
            keys, values_block, key_seg = block
            masked, visible, shaped = key_scores(keys, key_seg, offset)
            rows = keys.shape[0]
            probs = jnp.exp(masked - lse[..., None])
            probs_low = probs.astype(jnp.bfloat16)
            value_heads = values_block.reshape(rows, HK, HD)
            grad_probs = jnp.einsum(
                "qkgd,skd->kgqs", grad_mixed, value_heads, preferred_element_type=jnp.float32
            )
            grad_scores = (probs * (grad_probs - delta[..., None])).astype(jnp.bfloat16)
            grad_query = (
                grad_query
                + jnp.einsum(
                    "kgqs,skd->qkgd", grad_scores, shaped, preferred_element_type=jnp.float32
                )
                * scale
            )
            key_part = (
                jnp.einsum(
                    "kgqs,qkgd->skd", grad_scores, grouped, preferred_element_type=jnp.float32
                )
                * scale
            )
            value_part = jnp.einsum(
                "kgqs,qkgd->skd", probs_low, grad_mixed, preferred_element_type=jnp.float32
            )
            old_keys = lax.dynamic_slice_in_dim(grad_keys, offset, rows, 0)
            grad_keys = lax.dynamic_update_slice_in_dim(
                grad_keys, old_keys + key_part.reshape(rows, HK * HD), offset, 0
            )
            old_values = lax.dynamic_slice_in_dim(grad_values, offset, rows, 0)
            grad_values = lax.dynamic_update_slice_in_dim(
                grad_values, old_values + value_part.reshape(rows, HK * HD), offset, 0
            )
            return (grad_query, grad_keys, grad_values)

        back_state = (
            jnp.zeros((tokens, HK, groups, HD), jnp.float32),
            jnp.zeros((length, HK * HD), jnp.float32),
            jnp.zeros((length, HK * HD), jnp.float32),
        )
        grad_query, grad_keys_all, grad_values_all = fold_with(
            add_grads,
            back_state,
            (
                lax.all_gather(keys_flat, "ctx", axis=0, tiled=True),
                lax.all_gather(values, "ctx", axis=0, tiled=True),
                lax.all_gather(query_seg, "ctx", axis=0, tiled=True),
            ),
        )
        grad_keys_own, grad_values_own = (
            lax.psum_scatter(
                grad_keys_all.astype(jnp.bfloat16), "ctx", scatter_dimension=0, tiled=True
            ).astype(jnp.float32),
            lax.psum_scatter(
                grad_values_all.astype(jnp.bfloat16), "ctx", scatter_dimension=0, tiled=True
            ).astype(jnp.float32),
        )
        turned_query = rotate_back(grad_query.reshape(tokens, HQ, HD), cosine, sine)
        grad_query_gain = grad_query_gain + jnp.sum(turned_query * query_norm, axis=(0, 1))
        grad_query_low = (
            norm_back(query_heads, turned_query * gain_query.astype(jnp.float32))
            .reshape(tokens, HQ * HD)
            .astype(jnp.bfloat16)
        )
        turned_key = rotate_back(grad_keys_own.reshape(tokens, HK, HD), cosine, sine)
        grad_key_gain = grad_key_gain + jnp.sum(turned_key * key_norm, axis=(0, 1))
        grad_key_low = (
            norm_back(key_heads, turned_key * gain_key.astype(jnp.float32))
            .reshape(tokens, HK * HD)
            .astype(jnp.bfloat16)
        )
        grad_value_low = grad_values_own.astype(jnp.bfloat16)
        grad_scaled_in = (
            contract_last(grad_query_low, whole_query)
            + contract_last(grad_key_low, whole_key)
            + contract_last(grad_value_low, whole_value)
        )
        grad_attention_gain = grad_attention_gain + jnp.sum(grad_scaled_in * normed, axis=0)
        input_grads.append(
            grad_residual + norm_back(hidden, grad_scaled_in * gain_in.astype(jnp.float32))
        )
        stored.append(
            (
                scaled_in,
                grad_query_low,
                grad_key_low,
                grad_value_low,
                ff_in,
                grad_gate,
                grad_up,
                grad_proj,
                mixed_low,
                grad_out,
                hidden_low,
            )
        )
    columns = [jnp.concatenate([entry[index] for entry in stored], axis=0) for index in range(11)]
    (
        all_in,
        all_query,
        all_key,
        all_value,
        all_feed,
        all_gate,
        all_up,
        all_proj,
        all_mixed,
        all_out,
        all_hidden,
    ) = columns
    rows = query_weight.shape[0]
    head_rows = query_gain.shape[0]
    count = lax.axis_size(("dp", "ctx")) * rows
    row_ids = jnp.arange(count, dtype=jnp.int32)
    local = row_ids % rows
    place = jnp.clip(row_ids // rows * head_rows + local, 0, HD - 1)
    owned = local < head_rows
    gains = jnp.stack(
        [
            grad_attention_gain,
            grad_feed_gain,
            jnp.where(owned, jnp.take(grad_query_gain, place), 0.0),
            jnp.where(owned, jnp.take(grad_key_gain, place), 0.0),
        ],
        axis=1,
    )
    summed = lax.psum_scatter(
        jnp.concatenate(
            [
                contract_first(all_in, all_query).astype(BF),
                contract_first(all_in, all_key).astype(BF),
                contract_first(all_in, all_value).astype(BF),
                contract_first(all_feed, all_gate).astype(BF),
                contract_first(all_feed, all_up).astype(BF),
                contract_first(all_proj, all_mixed).astype(BF),
                contract_first(all_out, all_hidden).astype(BF),
                gains.astype(BF),
                jnp.zeros((count, 124), BF),
            ],
            axis=1,
        ),
        ("dp", "ctx"),
        scatter_dimension=0,
        tiled=True,
    ).astype(F32)
    widths = [HQ * HD, HK * HD, HK * HD, FF, FF, HQ * HD, FF, 128]
    pieces = []
    edge = 0
    for width in widths:
        pieces.append(summed[:, edge : edge + width])
        edge = edge + width
    gain_block = pieces[7]
    block_out = jnp.stack(outputs)[:, None]
    input_grad = jnp.stack(input_grads)[:, None]
    return (
        block_out,
        input_grad,
        gain_block[:, 0],
        gain_block[:head_rows, 2],
        gain_block[:head_rows, 3],
        pieces[0],
        pieces[1],
        pieces[2],
        pieces[5].T,
        gain_block[:, 1],
        pieces[3],
        pieces[4],
        pieces[6].T,
    )


def solution(mesh):
    shape = dict(mesh.shape)
    chips_hold_sequences = shape["dp"] == 4 and shape["ctx"] == 8

    def step(*arrays):
        if chips_hold_sequences and arrays[0].shape[2] == 64:
            return fused(*arrays)
        return general(*arrays)

    return jax.shard_map(
        step,
        mesh=mesh,
        in_specs=(
            P(None, "dp", "ctx", None),
            P(None, "dp", "ctx"),
            P(("dp", "ctx")),
            P(("dp", "ctx")),
            P(("dp", "ctx")),
            P(("dp", "ctx"), None),
            P(("dp", "ctx"), None),
            P(("dp", "ctx"), None),
            P(None, ("dp", "ctx")),
            P(("dp", "ctx")),
            P(("dp", "ctx"), None),
            P(("dp", "ctx"), None),
            P(None, ("dp", "ctx")),
            P(None, "dp", "ctx", None),
        ),
        out_specs=(
            P(None, "dp", "ctx", None),
            P(None, "dp", "ctx", None),
            P(("dp", "ctx")),
            P(("dp", "ctx")),
            P(("dp", "ctx")),
            P(("dp", "ctx"), None),
            P(("dp", "ctx"), None),
            P(("dp", "ctx"), None),
            P(None, ("dp", "ctx")),
            P(("dp", "ctx")),
            P(("dp", "ctx"), None),
            P(("dp", "ctx"), None),
            P(None, ("dp", "ctx")),
        ),
        check_vma=False,
    )
```

```python
import functools
import types

import jax
import jax.numpy as jnp
import numpy as np
from jax import lax
from jax.experimental import pallas as pl
from jax.experimental.pallas import tpu as pltpu
from jax.sharding import PartitionSpec as P

D = 1024
HQ = 16
HK = 8
HD = 128
FF = 3072
MB = 4

NORM_EPS = 1e-06
ROPE_BASE = 1000000.0
MASKED = -1e30
SCALE = HD ** (-0.5)
BF = jnp.bfloat16
F32 = jnp.float32
MESH = pl.DeviceIdType.MESH


def normalize(value):
    return value * lax.rsqrt(jnp.mean(value * value, axis=-1, keepdims=True) + NORM_EPS)


def norm_back(value, grad):
    scale = lax.rsqrt(jnp.mean(value * value, axis=-1, keepdims=True) + NORM_EPS)
    return scale * grad - value * (scale * scale * scale) * jnp.mean(
        grad * value, axis=-1, keepdims=True
    )


def rope_angles(first, count):
    positions = (first + jnp.arange(count, dtype=jnp.int32)).astype(F32)
    frequency = ROPE_BASE ** (-(jnp.arange(HD // 2, dtype=F32) * 2.0) / HD)
    return positions[:, None] * frequency[None, :]


KEYS = HK * HD // 2
WIDTHS = dict(
    k=KEYS + 128,
    v=KEYS,
    q=HQ * HD // 2,
    o=HQ * HD // 2,
    g=FF // 4,
    u=FF // 4,
    d=FF // 4,
)
ORDER = tuple(WIDTHS)
FEED = ("g", "u", "d")
PIECES = dict(k=(256, 384), v=(512,), q=(512, 512), o=(512, 512), g=(768,), u=(768,), d=(384, 384))
X_FIRST = (2,)
SUM_Y = dict(k=256, v=256, q=512, o=128)
HALF_HQ, HALF_HK = HQ // 2, HK // 2


def split_columns(name):
    return SUM_Y[name], WIDTHS[name] - SUM_Y[name]


def dot(left, right):
    return jnp.dot(left, right, preferred_element_type=F32)


def dot_nt(left, right):
    return lax.dot_general(left, right, (((1,), (1,)), ((), ())), preferred_element_type=F32)


def dot_tn(left, right):
    return lax.dot_general(left, right, (((0,), (0,)), ((), ())), preferred_element_type=F32)


class Semaphores:
    def __init__(self):
        self.count = 0

    def take(self, number=1):
        first = self.count
        self.count += number
        return first


def layer_kernel(names, tokens, *refs):
    at = types.SimpleNamespace(**dict(zip(names, refs)))
    sends, recvs = at.sends, at.recvs
    places = Semaphores()
    dp, ctx = lax.axis_index("dp"), lax.axis_index("ctx")
    x, c = lax.div(dp, 2), lax.rem(dp, 2)
    z, y = lax.div(ctx, 2), lax.rem(ctx, 2)
    ox, oc, oy = 1 - x, 1 - c, 1 - y
    sibling = (2 * x + oc, ctx)
    x_next = (2 * ox + c, ctx)
    x_cross = (2 * ox + oc, ctx)
    y_next = (dp, 2 * z + oy)
    length = 8 * tokens
    own_rows = 4 * tokens
    half = length // 2

    def z_at(step):
        return lax.rem(z + step, 4)

    def z_device(step):
        return (dp, 2 * z_at(step) + y)

    def remote(src, dst, place, device, recv_place=None):
        return pltpu.make_async_remote_copy(
            src_ref=src,
            dst_ref=dst,
            send_sem=sends.at[place],
            recv_sem=recvs.at[place if recv_place is None else recv_place],
            device_id=device,
            device_id_type=MESH,
        )

    def arrived(region, place, device):
        remote(region, region, place, device).wait_recv()

    barrier = pltpu.get_barrier_semaphore()
    me = c * 8 + ctx
    for other in range(1, 16):
        there = lax.rem(me + other, 16)
        pl.semaphore_signal(
            barrier, inc=1, device_id=(2 * x + lax.div(there, 8), lax.rem(there, 8)), device_id_type=MESH
        )
    pl.semaphore_signal(barrier, inc=1, device_id=x_next, device_id_type=MESH)
    pl.semaphore_signal(barrier, inc=1, device_id=x_cross, device_id_type=MESH)
    pl.semaphore_wait(barrier, 17)

    weight = {n: getattr(at, "w_" + n) for n in ORDER}
    shard = {n: getattr(at, "in_" + n) for n in ORDER}
    s0 = {n: places.take(3 if n in FEED else 1) for n in ORDER}
    lc = {n: places.take() for n in ORDER}
    pieces = []
    for n in ORDER:
        start = 0
        for size in PIECES[n]:
            pieces.append((n, pl.ds(start, size), places.take(4), places.take(), None if n in FEED else places.take()))
            start += size
    gather_sends = {n: [] for n in ORDER}

    def part(name, xx, cc):
        width = KEYS if name == "k" else WIDTHS[name]
        which = 2 * xx + cc if name in FEED else cc
        return shard[name].at[:, pl.ds(pl.multiple_of(which * width, width), width)]

    def keys_at(ref):
        return ref.at[:, pl.ds(0, KEYS)]

    def local(name):
        if name == "k":
            return pltpu.make_async_copy(part(name, x, c), keys_at(weight[name].at[x, c, z, y]), recvs.at[lc[name]])
        return pltpu.make_async_copy(part(name, x, c), weight[name].at[x, c, z, y], recvs.at[lc[name]])

    def begin(name, copy):
        copy.start()
        gather_sends[name].append(copy)

    extra_place = places.take()

    def gather_extra():
        rows = at.share_rows
        rows[...] = jnp.zeros_like(rows)
        for i, gain in enumerate((at.attention_gain, at.feedforward_gain, at.query_gain, at.key_gain)):
            rows[i : i + 1, : gain.shape[1]] = gain[...].astype(F32)
        columns = rows[...].T[: at.extra.shape[0]].astype(BF)
        at.extra[...] = columns
        weight["k"][x, c, z, y, :, KEYS:] = columns
        here = weight["k"].at[x, c, z, y, :, pl.ds(KEYS, 128)]
        begin("k", remote(at.extra, here, extra_place, sibling))

    def gather_core(name):
        here = weight[name].at[x, c, z, y]
        begin(name, remote(part(name, x, oc), keys_at(here) if name == "k" else here, s0[name], sibling))
        if name in FEED:
            begin(name, remote(part(name, ox, c), here, s0[name] + 1, x_next))
            begin(name, remote(part(name, ox, oc), here, s0[name] + 2, x_cross))
        local(name).start()

    def gather_core_done(name):
        w = weight[name]
        local(name).wait()
        if name == "k":
            arrived(keys_at(w.at[x, oc, z, y]), s0[name], sibling)
        else:
            arrived(w.at[x, oc, z, y], s0[name], sibling)
        if name in FEED:
            arrived(w.at[ox, c, z, y], s0[name] + 1, x_next)
            arrived(w.at[ox, oc, z, y], s0[name] + 2, x_cross)

    middle = (z == 1) | (z == 2)
    far = jnp.where(z == 1, 3, 0)

    def z_block(piece, zz):
        name, columns = piece[:2]
        w = weight[name]
        return w.at[:, :, zz, y, :, columns] if name in FEED else w.at[x, :, zz, y, :, columns]

    def z_copies(piece):
        block = z_block(piece, z)
        for there in range(4):
            distance = jnp.abs(there - z)
            sending = (distance == 1) | (distance == 2)
            yield sending, lambda there=there: remote(
                block, block, piece[2] + there, (dp, 2 * there + y), piece[2] + z
            )

    def z_forward(piece):
        block = z_block(piece, far)
        return remote(block, block, piece[2] + z, (dp, 2 * (3 - far) + y), piece[2] + far)

    def gather_z(number):
        piece = pieces[number]
        if piece[1].start == 0:
            gather_core_done(piece[0])
        if number == 1:
            arrived(weight["k"].at[x, oc, z, y, :, pl.ds(KEYS, 128)], extra_place, sibling)
        for sending, copy in z_copies(piece):
            pl.when(sending)(lambda copy=copy: copy().start())

    def gather_two(number):
        piece = pieces[number]
        name, columns, sem, y_sem, _ = piece
        w = weight[name]

        @pl.when(middle)
        def _():
            arrived(z_block(piece, far), sem + far, (dp, 2 * far + y))
            z_forward(piece).start()

        for source in range(4):
            waiting = (z != source) & jnp.logical_not(middle & (far == source))
            pl.when(waiting)(
                lambda source=source: arrived(z_block(piece, source), sem + source, (dp, 2 * source + y))
            )
        block = w.at[:, :, :, y, :, columns] if name in FEED else w.at[x, :, :, y, :, columns]
        begin(name, remote(block, block, y_sem, x_next if number in X_FIRST else y_next))

    def gather_three(number):
        name, columns, _, y_sem, x_sem = pieces[number]
        w = weight[name]
        if number in X_FIRST:
            arrived(w.at[ox, :, :, y, :, columns], y_sem, x_next)
            block = w.at[:, :, :, y, :, columns]
            begin(name, remote(block, block, x_sem, y_next))
            return
        arrived(w.at[x, :, :, oy, :, columns], y_sem, y_next)
        block = w.at[x, :, :, :, :, columns]
        begin(name, remote(block, block, x_sem, x_next))

    def gather_done(number):
        name, columns, _, y_sem, x_sem = pieces[number]
        w = weight[name]
        if name in FEED:
            arrived(w.at[:, :, :, oy, :, columns], y_sem, y_next)
        elif number in X_FIRST:
            arrived(w.at[:, :, :, oy, :, columns], x_sem, y_next)
        else:
            arrived(w.at[ox, :, :, :, :, columns], x_sem, x_next)

    def gather_sent(name):
        for copy in gather_sends[name]:
            copy.wait_send()
        for piece in pieces:
            if piece[0] == name:
                for sending, copy in z_copies(piece):
                    pl.when(sending)(lambda copy=copy: copy().wait_send())
                pl.when(middle)(lambda piece=piece: z_forward(piece).wait_send())

    slot = 2 * lax.rem(z, 2) + y
    target_core = lax.div(z, 2)

    class Reshard:
        def __init__(self, source, landing):
            self.source, self.landing = source, landing
            self.place, self.recv, self.own = places.take(4), places.take(4), places.take()

        def device(self, m):
            return (2 * x + target_core, 2 * m + c)

        def keeps(self, m):
            return (target_core == c) & (z == m) & (y == c)

        def copy(self, m):
            return remote(
                self.source.at[m], self.landing(target_core, slot), self.place + m, self.device(m), self.recv + slot
            )

        def keep(self, m):
            return pltpu.make_async_copy(
                self.source.at[m], self.landing(target_core, slot), recvs.at[self.own]
            )

        def start(self):
            for m in range(MB):
                pl.when(jnp.logical_not(self.keeps(m)))(lambda m=m: self.copy(m).start())
                pl.when(self.keeps(m))(lambda m=m: self.keep(m).start())

        def wait(self):
            for j in range(4):
                mine = (y == c) & (4 * c + j == ctx)
                region = self.landing(c, j)
                device = (2 * x + y, 4 * c + j)
                pl.when(jnp.logical_not(mine))(
                    lambda j=j, region=region, device=device: arrived(region, self.recv + j, device)
                )
                pl.when(mine)(
                    lambda region=region: pltpu.make_async_copy(
                        region, region, recvs.at[self.own]
                    ).wait()
                )

        def sent(self):
            for m in range(MB):
                pl.when(jnp.logical_not(self.keeps(m)))(lambda m=m: self.copy(m).wait_send())

    class Return:
        def __init__(self, source, landing):
            self.source, self.landing = source, landing
            self.place, self.recv, self.own = places.take(4), places.take(4), places.take()

        def keeps(self, j):
            return (y == c) & (4 * c + j == ctx)

        def copy(self, j):
            return remote(
                self.source.at[j], self.landing.at[z], self.place + j, (2 * x + y, 4 * c + j), self.recv + z
            )

        def keep(self, j):
            return pltpu.make_async_copy(
                self.source.at[j], self.landing.at[z], recvs.at[self.own]
            )

        def start(self, j):
            pl.when(jnp.logical_not(self.keeps(j)))(lambda: self.copy(j).start())
            pl.when(self.keeps(j))(lambda: self.keep(j).start())

        def finish(self):
            for j in range(4):
                pl.when(jnp.logical_not(self.keeps(j)))(lambda j=j: self.copy(j).wait_send())
                pl.when(self.keeps(j))(lambda j=j: self.keep(j).wait())
            for m in range(MB):
                mine = (target_core == c) & (z == m) & (y == c)
                device = (2 * x + target_core, 2 * m + c)
                pl.when(jnp.logical_not(mine))(
                    lambda m=m, device=device: arrived(self.landing.at[m], self.recv + m, device)
                )

    hidden_own, cot_all = at.hidden_own, at.cot_all
    hidden_move = Reshard(at.hidden_in, lambda core, j: hidden_own.at[j])
    number_move = Reshard(at.number_out, lambda core, j: at.number_own.at[j])
    cot_move = Reshard(at.cotangent, lambda core, j: cot_all.at[4 * (2 * x + core) + j])
    out_move = Return(at.out_own, at.block_out)
    grad_move = Return(at.grad_own, at.input_grad)
    class Swap:
        def __init__(self, source, there, here):
            self.place = places.take()
            self.out = remote(source, there, self.place, sibling)
            self.here = here

        def start(self):
            self.out.start()

        def wait(self):
            self.out.wait_send()
            arrived(self.here, self.place, sibling)

    def swap_rows(ref):
        mine, theirs = ref.at[pl.ds(own_at, own_rows)], ref.at[pl.ds(other_at, own_rows)]
        return Swap(mine, mine, theirs)

    own_at = pl.multiple_of(c * own_rows, own_rows)
    other_at = pl.multiple_of(oc * own_rows, own_rows)

    class Spread:
        def __init__(self, block):
            self.block = block
            self.place = places.take(3)

        def start(self):
            own = self.block(x, c)
            self.near = remote(own, own, self.place, sibling)
            self.across = remote(own, own, self.place + 1, x_next)
            self.near.start()
            self.across.start()

        def near_wait(self):
            arrived(self.block(x, oc), self.place, sibling)

        def pass_on(self):
            arrived(self.block(ox, c), self.place + 1, x_next)
            block = self.block(ox, c)
            self.far = remote(block, block, self.place + 2, sibling)
            self.far.start()

        def far_wait(self):
            arrived(self.block(ox, oc), self.place + 2, sibling)

        def sent(self):
            for copy in (self.near, self.across, self.far):
                copy.wait_send()

    r1 = {n: places.take(1 if n in FEED else 2) for n in ORDER}
    r2 = {n: places.take(0 if n in FEED else 2) for n in ORDER}
    r3 = {n: places.take(4) for n in ORDER}
    r4 = {n: places.take(3 if n in FEED else 1) for n in ORDER}
    sum_sends = []
    grads = dict(weight, d=at.grad_d)

    def send(copy):
        copy.start()
        sum_sends.append(copy)

    def sum_block(name, zz):
        w = grads[name]
        return w.at[:, :, zz, y] if name in FEED else w.at[x, :, zz, y]

    end = jnp.logical_not(middle)
    neighbour = jnp.where(z == 0, 1, 2)

    def sum_z_copies(name):
        landing = getattr(at, "r3_" + name)
        for there in range(4):
            distance = jnp.abs(there - z)
            sending = (distance == 1) | ((distance == 2) & end)
            yield sending, lambda there=there: remote(
                sum_block(name, there), landing.at[z], r3[name] + there, (dp, 2 * there + y), r3[name] + z
            )

        yield end, lambda: remote(
            sum_block(name, 3 - z), landing.at[neighbour], r3[name] + z, (dp, 2 * neighbour + y), r3[name] + neighbour
        )

    def sum_z_late(name):
        landing = getattr(at, "r3_" + name)
        return remote(sum_block(name, far), landing.at[z], r3[name] + far, (dp, 2 * far + y), r3[name] + z)

    def sum_z(name):
        for sending, copy in sum_z_copies(name):
            pl.when(sending)(lambda copy=copy: copy().start())

    def sum_z_pass(name):
        landing, w = getattr(at, "r3_" + name), grads[name]

        @pl.when(middle)
        def _():
            arrived(landing.at[z], r3[name] + z, (dp, 2 * (3 - far) + y))
            if name in FEED:
                for xx in range(2):
                    for cc in range(2):
                        w[xx, cc, far, y] += landing[z, xx, cc]
            else:
                for cc in range(2):
                    w[x, cc, far, y] += landing[z, cc]
            sum_z_late(name).start()

    def sum_one(name):
        w = grads[name]
        if name in FEED:
            send(remote(w.at[:, :, :, oy], getattr(at, "r1a_" + name), r1[name], y_next))
            return
        first, second = split_columns(name)
        send(remote(w.at[:, :, :, oy, :, pl.ds(0, first)], getattr(at, "r1a_" + name), r1[name], y_next))
        if second:
            send(remote(w.at[ox, :, :, :, :, pl.ds(first, second)], getattr(at, "r1b_" + name), r1[name] + 1, x_next))

    def sum_two(name):
        w = grads[name]
        arrived(getattr(at, "r1a_" + name), r1[name], y_next)
        first, second = (WIDTHS[name], 0) if name in FEED else split_columns(name)

        @pl.loop(0, 16)
        def _(i):
            xx, cc, zz = lax.div(i, 8), lax.rem(lax.div(i, 4), 2), lax.rem(i, 4)
            w[xx, cc, zz, y, :, pl.ds(0, first)] += getattr(at, "r1a_" + name)[xx, cc, zz]

        if name in FEED:
            sum_z(name)
            return
        send(remote(w.at[ox, :, :, y, :, pl.ds(0, first)], getattr(at, "r2a_" + name), r2[name], x_next))
        if second:
            arrived(getattr(at, "r1b_" + name), r1[name] + 1, x_next)

            @pl.loop(0, 16)
            def _(i):
                cc, zz, yy = lax.div(i, 8), lax.rem(lax.div(i, 2), 4), lax.rem(i, 2)
                w[x, cc, zz, yy, :, pl.ds(first, second)] += getattr(at, "r1b_" + name)[cc, zz, yy]

            send(remote(w.at[x, :, :, oy, :, pl.ds(first, second)], getattr(at, "r2b_" + name), r2[name] + 1, y_next))

    def sum_three(name):
        w = grads[name]
        first, second = split_columns(name)
        arrived(getattr(at, "r2a_" + name), r2[name], x_next)
        if second:
            arrived(getattr(at, "r2b_" + name), r2[name] + 1, y_next)

        @pl.loop(0, 8)
        def _(i):
            cc, zz = lax.div(i, 4), lax.rem(i, 4)
            w[x, cc, zz, y, :, pl.ds(0, first)] += getattr(at, "r2a_" + name)[cc, zz]
            if second:
                w[x, cc, zz, y, :, pl.ds(first, second)] += getattr(at, "r2b_" + name)[cc, zz]

        sum_z(name)

    def sum_four(name):
        w, landed = grads[name], getattr(at, "r3_" + name)
        for source in range(4):
            coming = (z != source) & (jnp.abs(source - z) != 3)
            pl.when(coming)(
                lambda source=source: arrived(landed.at[source], r3[name] + source, (dp, 2 * source + y))
            )

        def total(*place):
            mine = w[(*place, z, y)] if name in FEED else w[(x, *place, z, y)]
            value = mine.astype(F32)
            value = value + landed[(jnp.where(z == 0, 1, z - 1), *place)].astype(F32)
            value = value + landed[(jnp.where(z == 0, 2, jnp.where(z == 3, 1, z + 1)), *place)].astype(F32)
            third = landed[(far, *place)].astype(F32)
            return jnp.where(middle, value + third, value)

        width = WIDTHS[name]
        staged, result = getattr(at, "r4_" + name), getattr(at, "out_" + name)
        if name in FEED:
            columns = pl.ds(pl.multiple_of(dp * width, width), width)
            for i, (xx, cc, device) in enumerate(((ox, oc, x_cross), (ox, c, x_next), (x, oc, sibling))):
                staged[i] = total(xx, cc).astype(BF)
                send(remote(staged.at[i], getattr(at, "r5_" + name).at[i], r4[name] + i, device))
            result[:, columns] = total(x, c)
            return
        staged[...] = total(oc)
        columns = pl.ds(pl.multiple_of(c * width, width), width)
        send(remote(staged, result.at[:, columns], r4[name], sibling))
        result[:, columns] = total(c)

    def sum_done(name):
        width = WIDTHS[name]
        if name in FEED:
            for i, (xx, cc, device) in enumerate(((ox, oc, x_cross), (ox, c, x_next), (x, oc, sibling))):
                columns = pl.ds(pl.multiple_of((2 * xx + cc) * width, width), width)
                arrived(getattr(at, "r5_" + name).at[i], r4[name] + i, device)
                getattr(at, "out_" + name)[:, columns] = getattr(at, "r5_" + name)[i].astype(F32)
        else:
            columns = pl.ds(pl.multiple_of(oc * width, width), width)
            arrived(getattr(at, "out_" + name).at[:, columns], r4[name], sibling)

    gains, head_gains = at.gains, at.head_gains
    scaled, ff_in, grad_proj = at.scaled, at.ff_in, at.grad_proj
    residual, grad_residual = at.residual, at.grad_residual
    acc_own = at.acc_own
    scaled_swap, proj_swap = swap_rows(scaled), swap_rows(grad_proj)
    ff_spread = Spread(lambda xx, cc: ff_in.at[2 * xx + cc])
    cot_spread = Spread(lambda xx, cc: cot_all.at[pl.ds(4 * (2 * xx + cc), 4)])
    partials = [Swap(at.partial_out.at[i], at.partial_in.at[i], at.partial_in.at[i]) for i in range(2)]
    feed_near = [
        [Swap(at.near_out.at[i, k], at.near_in.at[i, k], at.near_in.at[i, k]) for k in range(2)] for i in range(2)
    ]
    feed_cross = []
    for i in range(2):
        place = places.take()
        feed_cross.append((remote(at.cross_out.at[i], at.cross_in.at[i], place, x_next), place))

    def selector():
        row = lax.broadcasted_iota(jnp.int32, (D, HD), 0)
        column = lax.broadcasted_iota(jnp.int32, (D, HD), 1)
        local_row = row & 31
        hit = ((row >> 5) * 4 + local_row == column) & (local_row < 4)
        return jnp.where(hit, 1.0, 0.0).astype(BF)

    def prepare_gains():
        columns = weight["k"][:, :, :, :, :, KEYS:].reshape(D, 128).astype(F32)
        for i in range(8):
            gains[:, i * 128 : (i + 1) * 128] = columns[i * 128 : (i + 1) * 128].T[:8]
        head_gains[...] = dot(gains[...].astype(BF), selector())

    def prepare_numbers():
        for m in range(MB):
            at.share_rows[:1, :tokens] = at.segments[m].astype(F32)
            at.number_out[m] = jnp.broadcast_to(at.share_rows[:1], (128, 128)).T[:tokens].astype(BF)

    def prepare_mask():
        def number(i):
            return scaled[i * 128 : (i + 1) * 128, D:].astype(F32)

        for j in range(4):
            key = number(j).T
            for i in range(4):
                place = slice(i * 128, (i + 1) * 128), slice(j * 128, (j + 1) * 128)
                if j > i:
                    at.bias[place] = jnp.full((128, 128), MASKED, F32)
                    continue
                seen = number(i) == key
                if i == j:
                    seen = seen & (
                        lax.broadcasted_iota(jnp.int32, (128, 128), 1)
                        <= lax.broadcasted_iota(jnp.int32, (128, 128), 0)
                    )
                at.bias[place] = jnp.where(seen, 0.0, MASKED)

    def own_block(j):
        return pl.ds(pl.multiple_of(c * own_rows + j * tokens, tokens), tokens)

    def here_block(j):
        return pl.ds(pl.multiple_of(j * tokens, tokens), tokens)

    def scale_input():
        @pl.loop(0, 4)
        def _(j):
            value = normalize(hidden_own[j].astype(F32)) * gains[0:1]
            scaled[own_block(j), :D] = value.astype(BF)
            scaled[own_block(j), D:] = at.number_own[j]

    def columns_of(name, t, size=256):
        return weight[name][:, :, :, :, :, pl.ds(pl.multiple_of(t * size, size), size)].reshape(D, size)

    def rows_of(name, t):
        if name == "k":
            return weight[name][lax.div(t, 2), lax.rem(t, 2), :, :, :, :KEYS].reshape(D // 4, KEYS)
        return weight[name][lax.div(t, 2), lax.rem(t, 2)].reshape(D // 4, WIDTHS[name])

    cosine, sine = at.cosine, at.sine

    def turn(value):
        return value * cosine[...] + pltpu.roll(value, HD // 2, 1) * sine[...]

    def project_heads(name, count, gain, kept, turned):
        @pl.loop(0, count // 2)
        def _(t):
            both = dot(scaled[:, :D], columns_of(name, t))
            for i in range(2):
                value = both[:, i * HD : (i + 1) * HD]
                kept[2 * t + i] = value
                turned[2 * t + i] = turn(normalize(value) * gain).astype(BF)

    def project_values():
        @pl.loop(0, WIDTHS["v"] // 256)
        def _(t):
            both = dot(scaled[:, :D], columns_of("v", t))
            for i in range(2):
                at.values[2 * t + i] = both[:, i * HD : (i + 1) * HD].astype(BF)

    def probabilities(head, pair, block):
        rows = slice(block * half, (block + 1) * half)
        seen = slice(0, (block + 1) * half)
        scores = dot_nt(at.queries[head, rows], at.keys[pair, seen]) * SCALE + at.bias[rows, seen]
        terms = jnp.exp(scores - jnp.max(scores, axis=-1, keepdims=True))
        return terms * (1.0 / jnp.sum(terms, axis=-1, keepdims=True))

    def attend(first, last):
        @pl.loop(first, last)
        def _(head):
            pair = lax.div(head, 2)
            for block in range(2):
                seen = slice(0, (block + 1) * half)
                low = probabilities(head, pair, block).astype(BF)
                at.mixed[
                    block * half : (block + 1) * half, pl.ds(pl.multiple_of(head * HD, HD), HD)
                ] = dot(low, at.values[pair, seen]).astype(BF)

    def column_quarters(body):
        @pl.loop(0, 4)
        def _(t):
            body(t, pl.ds(pl.multiple_of(t * (D // 4), D // 4), D // 4))

    def partial_product(index, terms):
        def rows_times(first, t):
            return sum(dot_nt(left(pl.ds(first, own_rows)), rows_of(name, t)) for left, name in terms)

        def theirs(t, columns):
            at.partial_out[index, :, columns] = rows_times(other_at, t).astype(BF)

        def mine(t, columns):
            acc_own[:, columns] = rows_times(own_at, t)

        column_quarters(theirs)
        partials[index].start()
        column_quarters(mine)

    def own_sum(index, j):
        return acc_own[here_block(j)] + at.partial_in[index, here_block(j)].astype(F32)

    def feed_product(index, terms):
        acc = at.acc_feed if index == 0 else acc_own

        def rows_times(xx, cc, t):
            first = pl.multiple_of((2 * xx + cc) * own_rows, own_rows)
            return sum(dot_nt(left[pl.ds(first, own_rows)], rows_of(name, t)) for left, name in terms)

        def give(k, xx):
            def body(t, columns):
                at.near_out[index, k, :, columns] = rows_times(xx, oc, t).astype(BF)

            column_quarters(body)
            feed_near[index][k].start()

        def keep(xx):
            def body(t, columns):
                acc[:, columns] = rows_times(xx, c, t)

            column_quarters(body)

        give(0, ox)
        keep(ox)
        feed_near[index][0].wait()
        near = at.near_in

        @pl.loop(0, 4)
        def _(j):
            rows = here_block(j)
            at.cross_out[index, rows] = (acc[rows] + near[index, 0, rows].astype(F32)).astype(BF)

        if index == 1:
            feed_cross[index][0].start()
        give(1, x)
        keep(x)

    def feed_wait(index):
        feed_near[index][1].wait()
        copy, place = feed_cross[index]
        copy.wait_send()
        arrived(at.cross_in.at[index], place, x_next)

    def feed_sum(index, j):
        rows = here_block(j)
        acc = at.acc_feed if index == 0 else acc_own
        return acc[rows] + at.near_in[index, 1, rows].astype(F32) + at.cross_in[index, rows].astype(F32)

    def add_residual():
        @pl.loop(0, 4)
        def _(j):
            value = hidden_own[j].astype(F32) + own_sum(0, j)
            residual[here_block(j)] = value
            ff_in[2 * x + c, here_block(j)] = (normalize(value) * gains[1:2]).astype(BF)

    gate_part, up_part, hidden_low = at.gate_part, at.up_part, at.hidden_low

    def chip_rows(xx):
        return pl.ds(pl.multiple_of(xx * length, length), length)

    def feed_forward(xx):
        rows = chip_rows(xx)

        @pl.loop(0, WIDTHS["g"] // 256)
        def _(t):
            columns = pl.ds(pl.multiple_of(t * 256, 256), 256)
            left = ff_in[pl.ds(2 * xx, 2)].reshape(length, D)
            gate = dot(left, columns_of("g", t))
            up = dot(left, columns_of("u", t))
            sigmoid = 1.0 / (1.0 + jnp.exp(-gate))
            swish = gate * sigmoid
            hidden_low[rows, columns] = (swish * up).astype(BF)
            up_part[rows, columns] = swish.astype(BF)
            gate_part[rows, columns] = (up * sigmoid * (1.0 + gate * (1.0 - sigmoid))).astype(BF)

    def write_out():
        @pl.loop(0, 4)
        def _(j):
            at.out_own[j] = (residual[here_block(j)] + feed_sum(0, j)).astype(BF)

        for j in range(4):
            out_move.start(j)

    def grad_hidden():
        @pl.loop(0, 2 * (WIDTHS["d"] // 256))
        def _(i):
            xx, t = lax.div(i, 3), lax.rem(i, 3)
            rows, columns = chip_rows(xx), pl.ds(pl.multiple_of(t * 256, 256), 256)
            grad = dot(cot_all[pl.ds(8 * xx, 8)].reshape(length, D), columns_of("d", t))
            gate_part[rows, columns] = (grad * gate_part[rows, columns].astype(F32)).astype(BF)
            up_part[rows, columns] = (grad * up_part[rows, columns].astype(F32)).astype(BF)

    turned_rows = at.turned_rows

    def transpose_rows(load, count):
        @pl.loop(0, D // 128)
        def _(t):
            place = pl.ds(pl.multiple_of(t * 128, 128), 128)
            turned_rows[place, :count] = load(place).reshape(count, 128).T

    def weight_grad(name, right, count):
        if name != "d":
            gather_sent(name)

        @pl.loop(0, (KEYS if name == "k" else WIDTHS[name]) // 256)
        def _(t):
            columns = pl.ds(pl.multiple_of(t * 256, 256), 256)
            grad = dot(turned_rows[:, :count], right(columns))
            grads[name][:, :, :, :, :, columns] = grad.astype(BF).reshape(2, 2, 4, 2, 32, 256)

    grad_gains = at.grad_gains

    def back_residual():
        grad_gains[...] = jnp.zeros_like(grad_gains)

        @pl.loop(0, 4)
        def _(j):
            value = residual[here_block(j)]
            grad = feed_sum(1, j)
            scale = lax.rsqrt(jnp.mean(value * value, axis=-1, keepdims=True) + NORM_EPS)
            grad_gains[1:2] += jnp.sum(grad * (value * scale), axis=0, keepdims=True)
            total = cot_all[4 * (2 * x + c) + j].astype(F32) + norm_back(value, grad * gains[1:2])
            grad_residual[here_block(j)] = total
            grad_proj[own_block(j)] = total.astype(BF)

    grad_mixed, grad_heads = ff_in, cot_all

    def back_mixed():
        @pl.loop(0, WIDTHS["o"] // 256)
        def _(t):
            columns = pl.ds(pl.multiple_of(t * 256, 256), 256)
            grad = dot(grad_proj[...], columns_of("o", t)).astype(BF)
            grad_mixed[:2, :, columns] = grad.reshape(2, half, 256)

    def put_heads(first, columns, value):
        grad_heads[first : first + 8, :, columns] = value.astype(BF).reshape(8, tokens, HD)

    def head_columns(first, columns):
        return grad_heads[first : first + 8, :, columns].reshape(length, columns.size)

    def head_rows(first, rows, start, width):
        block = first + lax.div(rows.start, tokens)
        return grad_heads[pl.ds(block, 4), :, start : start + width].reshape(own_rows, width)

    grad_head_gains = at.grad_head_gains

    def turn_back(value):
        return value * cosine[...] - pltpu.roll(value, HD // 2, 1) * sine[...]

    def back_head(value, grad, row, first, columns):
        scale = lax.rsqrt(jnp.mean(value * value, axis=-1, keepdims=True) + NORM_EPS)
        turned = turn_back(grad)
        grad_head_gains[row : row + 1] += jnp.sum(turned * (value * scale), axis=0, keepdims=True)
        put_heads(first, columns, norm_back(value, turned * head_gains[row : row + 1]))

    grad_key, grad_value, grad_query = at.grad_key, at.grad_value, at.grad_query

    def back_attend(first, last):
        if first == 0:
            grad_head_gains[...] = jnp.zeros_like(grad_head_gains)

        @pl.loop(first, last)
        def _(pair):
            for i in range(2):
                head = 2 * pair + i
                lanes = pl.ds(pl.multiple_of(head * HD, HD), HD)
                for block in (1, 0):
                    rows = slice(block * half, (block + 1) * half)
                    seen = slice(0, (block + 1) * half)
                    probs = probabilities(head, pair, block)
                    grad_out = grad_mixed[block, :, lanes]
                    grad_probs = dot_nt(grad_out, at.values[pair, seen])
                    delta = jnp.sum(probs * grad_probs, axis=-1, keepdims=True)
                    grad_scores = (probs * (grad_probs - delta)).astype(BF)
                    grad_query[rows] = dot(grad_scores, at.keys[pair, seen]) * SCALE
                    key_part = dot_tn(grad_scores, at.queries[head, rows]) * SCALE
                    value_part = dot_tn(probs.astype(BF), grad_out)
                    if i == 0 and block == 1:
                        grad_key[...] = key_part
                        grad_value[...] = value_part
                    else:
                        grad_key[seen] += key_part
                        grad_value[seen] += value_part
                back_head(at.query_acc[head], grad_query[...], 2, 0, lanes)
            lanes = pl.ds(pl.multiple_of(pair * HD, HD), HD)
            back_head(at.key_acc[pair], grad_key[...], 3, 8, lanes)
            put_heads(8, pl.ds(pl.multiple_of(KEYS + pair * HD, HD), HD), grad_value[...])

    def back_input():
        @pl.loop(0, 4)
        def _(j):
            value = hidden_own[j].astype(F32)
            grad = own_sum(1, j)
            scale = lax.rsqrt(jnp.mean(value * value, axis=-1, keepdims=True) + NORM_EPS)
            grad_gains[0:1] += jnp.sum(grad * (value * scale), axis=0, keepdims=True)
            at.grad_own[j] = (
                grad_residual[here_block(j)] + norm_back(value, grad * gains[0:1])
            ).astype(BF)

        for j in range(4):
            grad_move.start(j)

    def gain_grads():
        grad_gains[...] += dot_nt(grad_head_gains[...].astype(BF), selector())
        for i in range(8):
            block = jnp.concatenate(
                [grad_gains[:, i * 128 : (i + 1) * 128], jnp.zeros((120, 128), F32)], axis=0
            ).T
            weight["k"][i // 4, (i // 2) % 2, 2 * (i % 2) : 2 * (i % 2) + 2, :, :, KEYS:] = block.astype(BF).reshape(
                2, 2, 32, 128
            )

    gather_core("k")
    gather_extra()
    gather_z(0)
    gather_core("v")
    gather_z(1)
    for name in ("q", "o", *FEED):
        gather_core(name)
    prepare_numbers()
    gather_two(0)
    gather_z(2)
    gather_two(1)
    gather_three(0)
    gather_z(3)
    gather_two(2)
    gather_three(1)
    gather_z(4)
    hidden_move.start()
    number_move.start()
    gather_two(3)
    gather_three(2)
    gather_z(5)
    gather_two(4)
    gather_z(6)
    gather_done(0)
    gather_done(1)
    gather_three(3)
    prepare_gains()
    gather_two(5)
    gather_z(7)
    hidden_move.wait()
    number_move.wait()
    scale_input()
    scaled_swap.start()
    gather_two(6)
    gather_z(8)
    scaled_swap.wait()
    prepare_mask()
    project_heads("k", HALF_HK, head_gains[3:4], at.key_acc, at.keys)
    gather_done(2)
    gather_three(4)
    project_values()
    gather_two(7)
    gather_z(9)
    gather_done(3)
    gather_three(5)
    gather_done(4)
    gather_three(6)
    project_heads("q", HALF_HQ, head_gains[2:3], at.query_acc, at.queries)
    gather_two(8)
    gather_z(10)
    cot_move.start()
    attend(0, 4)
    gather_two(9)
    attend(4, 8)
    gather_done(5)
    gather_done(6)
    partial_product(0, [(lambda rows: at.mixed[rows], "o")])
    partials[0].wait()
    add_residual()
    ff_spread.start()
    gather_two(10)
    cot_move.wait()
    cot_spread.start()
    gather_done(7)
    gather_done(8)
    ff_spread.near_wait()
    feed_forward(x)
    ff_spread.pass_on()
    ff_spread.far_wait()
    feed_forward(ox)
    cot_spread.pass_on()
    cot_spread.near_wait()
    cot_spread.far_wait()
    transpose_rows(lambda columns: cot_all[:, :, columns], 2 * length)

    weight_grad("d", lambda columns: hidden_low[:, columns], 2 * length)
    sum_one("d")
    gather_done(9)
    gather_done(10)
    grad_hidden()
    feed_product(1, [(gate_part, "g"), (up_part, "u")])
    transpose_rows(lambda columns: ff_in[:, :, columns], 2 * length)
    weight_grad("g", lambda columns: gate_part[:, columns], 2 * length)
    sum_one("g")
    weight_grad("u", lambda columns: up_part[:, columns], 2 * length)
    feed_wait(1)
    back_residual()
    proj_swap.start()
    ff_spread.sent()
    cot_spread.sent()
    sum_two("d")
    proj_swap.wait()
    back_mixed()
    transpose_rows(lambda columns: grad_proj[:, columns], length)
    weight_grad("o", lambda columns: at.mixed[:, columns], length)
    sum_one("o")
    sum_one("u")
    back_attend(0, 2)
    sum_two("g")
    sum_z_pass("d")
    back_attend(2, 4)
    partial_product(
        1,
        [
            (lambda rows: head_rows(0, rows, 0, WIDTHS["q"]), "q"),
            (lambda rows: head_rows(8, rows, 0, KEYS), "k"),
            (lambda rows: head_rows(8, rows, KEYS, KEYS), "v"),
        ],
    )
    transpose_rows(lambda columns: scaled[:, columns], length)
    weight_grad("q", lambda columns: head_columns(0, columns), length)
    sum_one("q")
    sum_two("o")
    weight_grad("v", lambda columns: head_columns(8, pl.ds(columns.start + KEYS, 256)), length)
    weight_grad("k", lambda columns: head_columns(8, columns), length)
    sum_two("u")
    sum_one("v")
    feed_product(0, [(hidden_low, "d")])
    feed_cross[0][0].start()
    partials[1].wait()
    back_input()
    gain_grads()
    sum_z_pass("g")
    sum_four("d")
    sum_three("o")
    sum_z_pass("u")
    sum_four("g")
    sum_two("q")
    sum_one("k")
    sum_z_pass("o")
    sum_four("u")
    feed_wait(0)
    write_out()
    sum_three("q")
    sum_two("v")
    sum_z_pass("q")
    sum_four("o")
    sum_three("v")
    sum_two("k")
    sum_z_pass("v")
    sum_four("q")
    sum_three("k")
    sum_four("v")
    sum_z_pass("k")
    sum_four("k")
    for name in ("d", "g", "u", "o", "q", "v", "k"):
        sum_done(name)
    for copy in sum_sends:
        copy.wait_send()
    for name in ORDER:
        for sending, copy in sum_z_copies(name):
            pl.when(sending)(lambda copy=copy: copy().wait_send())
        pl.when(middle)(lambda name=name: sum_z_late(name).wait_send())
    gather_sent("d")
    hidden_move.sent()
    number_move.sent()
    cot_move.sent()
    out_move.finish()
    grad_move.finish()
    assert places.count == SEMAPHORES, places.count


SEMAPHORES = 204


def fused(
    hidden_in,
    segments,
    attention_gain,
    query_gain,
    key_gain,
    query_weight,
    key_weight,
    value_weight,
    out_weight,
    feedforward_gain,
    gate_weight,
    up_weight,
    down_weight,
    cotangent,
):
    tokens = hidden_in.shape[2]
    length = 8 * tokens
    rows = query_weight.shape[0]
    heads = query_gain.shape[0]
    positions = np.arange(length, dtype=np.float32)
    frequency = (ROPE_BASE ** (-(np.arange(HD // 2, dtype=np.float32) * 2.0) / HD)).astype(np.float32)
    angles = (positions[:, None] * frequency[None, :]).astype(np.float64)
    cosine = np.concatenate([np.cos(angles), np.cos(angles)], axis=-1).astype(np.float32)
    sine = np.concatenate([-np.sin(angles), np.sin(angles)], axis=-1).astype(np.float32)

    vmem, anywhere = pl.BlockSpec(memory_space=pltpu.VMEM), pl.BlockSpec(memory_space=pl.ANY)
    inputs = dict(
        hidden_in=(hidden_in[:, 0], anywhere),
        cotangent=(cotangent[:, 0], anywhere),
        segments=(segments, vmem),
        cosine=(jnp.asarray(cosine), vmem),
        sine=(jnp.asarray(sine), vmem),
        attention_gain=(attention_gain[None], vmem),
        feedforward_gain=(feedforward_gain[None], vmem),
        query_gain=(query_gain[None], vmem),
        key_gain=(key_gain[None], vmem),
        in_k=(key_weight, anywhere),
        in_v=(value_weight, anywhere),
        in_q=(query_weight, anywhere),
        in_o=(out_weight.T, anywhere),
        in_g=(gate_weight, anywhere),
        in_u=(up_weight, anywhere),
        in_d=(down_weight.T, anywhere),
    )
    block = (MB, tokens, D)
    outputs = dict(block_out=(block, BF, anywhere), input_grad=(block, BF, anywhere))
    for name, width in WIDTHS.items():
        outputs["out_" + name] = ((rows, width * (4 if name in FEED else 2)), F32, vmem)
    own = 4 * tokens
    scratch = dict(
        share_rows=((128, 128), F32),
        extra=((rows, 128), BF),
        number_out=((MB, tokens, 128), BF),
        number_own=((4, tokens, 128), BF),
        hidden_own=((4, tokens, D), BF),
        cot_all=((16, tokens, D), BF),
        gains=((8, D), F32),
        head_gains=((8, HD), F32),
        grad_gains=((8, D), F32),
        grad_head_gains=((8, HD), F32),
        bias=((length, length), F32),
        scaled=((length, D + 128), BF),
        query_acc=((HALF_HQ, length, HD), F32),
        key_acc=((HALF_HK, length, HD), F32),
        queries=((HALF_HQ, length, HD), BF),
        keys=((HALF_HK, length, HD), BF),
        values=((HALF_HK, length, HD), BF),
        mixed=((length, HALF_HQ * HD), BF),
        acc_own=((own, D), F32),
        acc_feed=((own, D), F32),
        partial_out=((2, own, D), BF),
        partial_in=((2, own, D), BF),
        near_out=((2, 2, own, D), BF),
        near_in=((2, 2, own, D), BF),
        cross_out=((2, own, D), BF),
        cross_in=((2, own, D), BF),
        residual=((own, D), F32),
        grad_residual=((own, D), F32),
        ff_in=((4, own, D), BF),
        gate_part=((2 * length, FF // 4), BF),
        up_part=((2 * length, FF // 4), BF),
        hidden_low=((2 * length, FF // 4), BF),
        grad_d=((2, 2, 4, 2, rows, FF // 4), BF),
        grad_proj=((length, D), BF),
        grad_key=((length, HD), F32),
        grad_value=((length, HD), F32),
        grad_query=((length, HD), F32),
        turned_rows=((D, 2 * length), BF),
        out_own=((4, tokens, D), BF),
        grad_own=((4, tokens, D), BF),
    )
    for name, width in WIDTHS.items():
        scratch["w_" + name] = ((2, 2, 4, 2, rows, width), BF)
        if name in FEED:
            scratch["r1a_" + name] = ((2, 2, 4, rows, width), BF)
            scratch["r3_" + name] = ((4, 2, 2, rows, width), BF)
            scratch["r4_" + name] = ((3, rows, width), BF)
            scratch["r5_" + name] = ((3, rows, width), BF)
            continue
        first, second = split_columns(name)
        scratch["r1a_" + name] = ((2, 2, 4, rows, first), BF)
        scratch["r2a_" + name] = ((2, 4, rows, first), BF)
        if second:
            scratch["r1b_" + name] = ((2, 4, 2, rows, second), BF)
            scratch["r2b_" + name] = ((2, 4, rows, second), BF)
        scratch["r3_" + name] = ((4, 2, rows, width), BF)
        scratch["r4_" + name] = ((rows, width), F32)
    names = (*inputs, *outputs, *scratch, "sends", "recvs")
    results = pl.pallas_call(
        functools.partial(layer_kernel, names, tokens),
        out_shape=[jax.ShapeDtypeStruct(shape, dtype) for shape, dtype, _ in outputs.values()],
        in_specs=[spec for _, spec in inputs.values()],
        out_specs=[spec for _, _, spec in outputs.values()],
        scratch_shapes=[pltpu.VMEM(shape, dtype) for shape, dtype in scratch.values()]
        + [pltpu.SemaphoreType.DMA((SEMAPHORES,))] * 2,
        compiler_params=pltpu.CompilerParams(
            collective_id=0, has_side_effects=True, vmem_limit_bytes=64 * 2**20 - 2**16
        ),
        name="layer",
    )(*(value for value, _ in inputs.values()))
    got = finish(types.SimpleNamespace(**dict(zip(outputs, results))), rows, heads)
    return (
        got.block_out[:, None],
        got.input_grad[:, None],
        got.attention_gain[0],
        got.query_gain[0],
        got.key_gain[0],
        got.out_q,
        got.out_k,
        got.out_v,
        got.out_o.T,
        got.feedforward_gain[0],
        got.out_g,
        got.out_u,
        got.out_d.T,
    )


def finish_kernel(names, heads, *refs):
    at = types.SimpleNamespace(**dict(zip(names, refs)))
    moved = [n[4:] for n in names if n.startswith("got_")]
    brought = [
        pltpu.make_async_copy(getattr(at, "got_" + n), getattr(at, "here_" + n), at.brought.at[i])
        for i, n in enumerate(moved)
    ]
    for copy in brought:
        copy.start()
    taken = []

    def take(name, source):
        copy = pltpu.make_async_copy(source, getattr(at, name), at.taken.at[len(taken)])
        copy.start()
        taken.append(copy)

    def ready(name):
        brought[moved.index(name)].wait()
        return getattr(at, "here_" + name)

    value = ready("input_grad")
    for m in range(MB):
        at.wide_grad[m] = value[m].astype(F32)
    take("input_grad", at.wide_grad)
    for name in moved:
        if name not in ("input_grad", "out_k"):
            take(name, ready(name))
    value = ready("out_k")
    at.keys[:, :KEYS] = value[:, :KEYS]
    at.keys[:, KEYS:] = value[:, KEYS + 128 : 2 * KEYS + 128]
    take("out_k", at.keys)
    gains = value[:, KEYS : KEYS + 128] + value[:, 2 * KEYS + 128 :]
    blank = jnp.zeros((128 - gains.shape[0], 128), F32)
    turned = jnp.concatenate([gains, blank], axis=0).T
    at.attention_gain[...] = turned[0:1, : gains.shape[0]]
    at.feedforward_gain[...] = turned[1:2, : gains.shape[0]]
    at.query_gain[...] = turned[2:3, :heads]
    at.key_gain[...] = turned[3:4, :heads]
    for copy in taken:
        copy.wait()


def finish(got, rows, heads):
    vmem, anywhere = pl.BlockSpec(memory_space=pltpu.VMEM), pl.BlockSpec(memory_space=pl.ANY)
    inputs = vars(got)
    outputs = {n: (v.shape, v.dtype, anywhere) for n, v in inputs.items()}
    outputs.update(
        input_grad=(got.input_grad.shape, F32, anywhere),
        out_k=((rows, 2 * KEYS), F32, anywhere),
        attention_gain=((1, rows), F32, vmem),
        feedforward_gain=((1, rows), F32, vmem),
        query_gain=((1, heads), F32, vmem),
        key_gain=((1, heads), F32, vmem),
    )
    scratch = {"here_" + n: (v.shape, v.dtype) for n, v in inputs.items()}
    scratch.update(wide_grad=(got.input_grad.shape, F32), keys=((rows, 2 * KEYS), F32))
    names = (*("got_" + n for n in inputs), *outputs, *scratch, "brought", "taken")
    results = pl.pallas_call(
        functools.partial(finish_kernel, names, heads),
        out_shape=[jax.ShapeDtypeStruct(shape, dtype) for shape, dtype, _ in outputs.values()],
        in_specs=[anywhere] * len(inputs),
        out_specs=[spec for _, _, spec in outputs.values()],
        scratch_shapes=[pltpu.VMEM(shape, dtype) for shape, dtype in scratch.values()]
        + [pltpu.SemaphoreType.DMA((len(inputs),))] * 2,
        compiler_params=pltpu.CompilerParams(vmem_limit_bytes=64 * 2**20 - 2**16),
        name="results",
    )(*inputs.values())
    return types.SimpleNamespace(**dict(zip(outputs, results)))


def rope_tables(first, count):
    angles = rope_angles(first, count)
    cosine = jnp.concatenate([jnp.cos(angles), jnp.cos(angles)], axis=-1)
    sine = jnp.concatenate([jnp.sin(angles), jnp.sin(angles)], axis=-1)
    return (cosine[:, None, :], sine[:, None, :])


def rotate(value, cosine, sine):
    half = value.shape[-1] // 2
    turned = jnp.concatenate([-value[..., half:], value[..., :half]], axis=-1)
    return value * cosine + turned * sine


def rotate_back(grad, cosine, sine):
    half = grad.shape[-1] // 2
    scaled = grad * sine
    return grad * cosine + jnp.concatenate([scaled[..., half:], -scaled[..., :half]], axis=-1)


def contract_last(left, right):
    return lax.dot_general(
        left, right, (((1,), (1,)), ((), ())), preferred_element_type=jnp.float32
    )


def contract_first(left, right):
    return lax.dot_general(
        left, right, (((0,), (0,)), ((), ())), preferred_element_type=jnp.float32
    )


def block_rows(rows):
    size = min(rows, 512)
    while rows % size:
        size -= 1
    return size


def over_blocks(state, pieces, update):
    rows = pieces[0].shape[0]
    size = block_rows(rows)
    count = rows // size
    stacked = tuple((piece.reshape((count, size) + piece.shape[1:]) for piece in pieces))
    offsets = size * jnp.arange(count, dtype=jnp.int32)

    def step(current, item):
        block = item[:-1]
        offset = item[-1]
        current = update(current, block, offset)
        return (current, None)

    final, unused = lax.scan(step, state, stacked + (offsets,))
    return final


def general(
    hidden_in,
    segments,
    attention_gain,
    query_gain,
    key_gain,
    query_weight,
    key_weight,
    value_weight,
    out_weight,
    feedforward_gain,
    gate_weight,
    up_weight,
    down_weight,
    cotangent,
):
    tokens = hidden_in.shape[2]
    groups = HQ // HK
    scale = HD ** (-0.5)
    first = lax.axis_index("ctx") * tokens
    length = lax.axis_size("ctx") * tokens
    query_pos = first + jnp.arange(tokens, dtype=jnp.int32)
    cosine, sine = rope_tables(first, tokens)
    sources = (
        query_weight,
        key_weight,
        value_weight,
        gate_weight,
        up_weight,
        out_weight.T,
        down_weight.T,
    )
    whole = lax.all_gather(jnp.concatenate(sources, axis=1), ("dp", "ctx"), axis=0, tiled=True)
    parts = []
    edge = 0
    for source in sources:
        parts.append(whole[:, edge : edge + source.shape[1]])
        edge = edge + source.shape[1]
    whole_query, whole_key, whole_value, whole_gate, whole_up, whole_out, whole_down = parts
    gain_in, gain_query, gain_key, gain_feed = (
        lax.all_gather(gain, ("dp", "ctx"), axis=0, tiled=True)
        for gain in (attention_gain, query_gain, key_gain, feedforward_gain)
    )
    grad_attention_gain = jnp.zeros((D,), jnp.float32)
    grad_feed_gain = jnp.zeros((D,), jnp.float32)
    grad_query_gain = jnp.zeros((HD,), jnp.float32)
    grad_key_gain = jnp.zeros((HD,), jnp.float32)
    outputs = []
    input_grads = []
    stored = []
    for batch in range(MB):
        hidden = hidden_in[batch, 0].astype(jnp.float32)
        query_seg = segments[batch, 0]
        grad_out = cotangent[batch, 0]
        normed = normalize(hidden)
        scaled_in = (normed * gain_in.astype(jnp.float32)).astype(jnp.bfloat16)
        query_heads = jnp.dot(scaled_in, whole_query, preferred_element_type=jnp.float32).reshape(
            tokens, HQ, HD
        )
        key_heads = jnp.dot(scaled_in, whole_key, preferred_element_type=jnp.float32).reshape(
            tokens, HK, HD
        )
        values = jnp.dot(scaled_in, whole_value, preferred_element_type=jnp.float32).astype(
            jnp.bfloat16
        )
        query_norm = normalize(query_heads)
        key_norm = normalize(key_heads)
        query_scale = gain_query.astype(jnp.float32)
        key_scale = gain_key.astype(jnp.float32)
        queries = rotate(query_norm * query_scale, cosine, sine).astype(jnp.bfloat16)
        keys_low = rotate(key_norm * key_scale, cosine, sine).astype(jnp.bfloat16)
        grouped = queries.reshape(tokens, HK, groups, HD)
        keys_flat = keys_low.reshape(tokens, HK * HD)

        def key_scores(keys, key_seg, offset):
            rows = keys.shape[0]
            shaped = keys.reshape(rows, HK, HD)
            raw = (
                jnp.einsum("qkgd,skd->kgqs", grouped, shaped, preferred_element_type=jnp.float32)
                * scale
            )
            key_pos = offset + jnp.arange(rows, dtype=jnp.int32)
            visible = (key_pos[None, :] <= query_pos[:, None]) & (
                key_seg[None, :] == query_seg[:, None]
            )
            return (jnp.where(visible, raw, MASKED), visible, shaped)

        def fold_with(update, state, pieces):
            return over_blocks(state, pieces, update)

        def add_lse(state, block, offset):
            keys, key_seg = block
            masked, visible, shaped = key_scores(keys, key_seg, offset)
            top, total = state
            new_top = jnp.maximum(top, jnp.max(masked, axis=-1))
            terms = jnp.where(visible, jnp.exp(masked - new_top[..., None]), 0.0)
            return (new_top, total * jnp.exp(top - new_top) + jnp.sum(terms, axis=-1))

        start_state = (
            jnp.full((HK, groups, tokens), MASKED, jnp.float32),
            jnp.zeros((HK, groups, tokens), jnp.float32),
        )
        top, total = fold_with(
            add_lse,
            start_state,
            (
                lax.all_gather(keys_flat, "ctx", axis=0, tiled=True),
                lax.all_gather(query_seg, "ctx", axis=0, tiled=True),
            ),
        )
        lse = top + jnp.log(total)

        def add_mixed(state, block, offset):
            keys, values_block, key_seg = block
            masked, visible, shaped = key_scores(keys, key_seg, offset)
            probs = jnp.exp(masked - lse[..., None]).astype(jnp.bfloat16)
            value_heads = values_block.reshape(values_block.shape[0], HK, HD)
            return state + jnp.einsum(
                "kgqs,skd->qkgd", probs, value_heads, preferred_element_type=jnp.float32
            )

        mixed = fold_with(
            add_mixed,
            jnp.zeros((tokens, HK, groups, HD), jnp.float32),
            (
                lax.all_gather(keys_flat, "ctx", axis=0, tiled=True),
                lax.all_gather(values, "ctx", axis=0, tiled=True),
                lax.all_gather(query_seg, "ctx", axis=0, tiled=True),
            ),
        )
        mixed_low = mixed.reshape(tokens, HQ * HD).astype(jnp.bfloat16)
        residual = hidden + contract_last(mixed_low, whole_out)
        feed_normed = normalize(residual)
        feed_scale = gain_feed.astype(jnp.float32)
        ff_in = (feed_normed * feed_scale).astype(jnp.bfloat16)
        gate = jnp.dot(ff_in, whole_gate, preferred_element_type=jnp.float32)
        up_part = jnp.dot(ff_in, whole_up, preferred_element_type=jnp.float32)
        sigmoid = jax.nn.sigmoid(gate)
        swish = gate * sigmoid
        hidden_low = (swish * up_part).astype(jnp.bfloat16)
        block_out = residual + contract_last(hidden_low, whole_down)
        outputs.append(block_out.astype(jnp.bfloat16))
        grad_hidden = jnp.dot(grad_out, whole_down, preferred_element_type=jnp.float32)
        grad_gate = (grad_hidden * up_part * (sigmoid * (1.0 + gate * (1.0 - sigmoid)))).astype(
            jnp.bfloat16
        )
        grad_up = (grad_hidden * swish).astype(jnp.bfloat16)
        grad_feed_in = contract_last(grad_gate, whole_gate) + contract_last(grad_up, whole_up)
        grad_feed_gain = grad_feed_gain + jnp.sum(grad_feed_in * feed_normed, axis=0)
        grad_residual = grad_out.astype(jnp.float32) + norm_back(
            residual, grad_feed_in * gain_feed.astype(jnp.float32)
        )
        grad_proj = grad_residual.astype(jnp.bfloat16)
        grad_mixed = (
            jnp.dot(grad_proj, whole_out, preferred_element_type=jnp.float32).astype(jnp.bfloat16).reshape(tokens, HK, groups, HD)
        )
        delta = jnp.transpose(jnp.sum(grad_mixed.astype(jnp.float32) * mixed, axis=-1), (1, 2, 0))

        def add_grads(state, block, offset):
            grad_query, grad_keys, grad_values = state
            keys, values_block, key_seg = block
            masked, visible, shaped = key_scores(keys, key_seg, offset)
            rows = keys.shape[0]
            probs = jnp.exp(masked - lse[..., None])
            probs_low = probs.astype(jnp.bfloat16)
            value_heads = values_block.reshape(rows, HK, HD)
            grad_probs = jnp.einsum(
                "qkgd,skd->kgqs", grad_mixed, value_heads, preferred_element_type=jnp.float32
            )
            grad_scores = (probs * (grad_probs - delta[..., None])).astype(jnp.bfloat16)
            grad_query = (
                grad_query
                + jnp.einsum(
                    "kgqs,skd->qkgd", grad_scores, shaped, preferred_element_type=jnp.float32
                )
                * scale
            )
            key_part = (
                jnp.einsum(
                    "kgqs,qkgd->skd", grad_scores, grouped, preferred_element_type=jnp.float32
                )
                * scale
            )
            value_part = jnp.einsum(
                "kgqs,qkgd->skd", probs_low, grad_mixed, preferred_element_type=jnp.float32
            )
            old_keys = lax.dynamic_slice_in_dim(grad_keys, offset, rows, 0)
            grad_keys = lax.dynamic_update_slice_in_dim(
                grad_keys, old_keys + key_part.reshape(rows, HK * HD), offset, 0
            )
            old_values = lax.dynamic_slice_in_dim(grad_values, offset, rows, 0)
            grad_values = lax.dynamic_update_slice_in_dim(
                grad_values, old_values + value_part.reshape(rows, HK * HD), offset, 0
            )
            return (grad_query, grad_keys, grad_values)

        back_state = (
            jnp.zeros((tokens, HK, groups, HD), jnp.float32),
            jnp.zeros((length, HK * HD), jnp.float32),
            jnp.zeros((length, HK * HD), jnp.float32),
        )
        grad_query, grad_keys_all, grad_values_all = fold_with(
            add_grads,
            back_state,
            (
                lax.all_gather(keys_flat, "ctx", axis=0, tiled=True),
                lax.all_gather(values, "ctx", axis=0, tiled=True),
                lax.all_gather(query_seg, "ctx", axis=0, tiled=True),
            ),
        )
        grad_keys_own, grad_values_own = (
            lax.psum_scatter(
                grad_keys_all.astype(jnp.bfloat16), "ctx", scatter_dimension=0, tiled=True
            ).astype(jnp.float32),
            lax.psum_scatter(
                grad_values_all.astype(jnp.bfloat16), "ctx", scatter_dimension=0, tiled=True
            ).astype(jnp.float32),
        )
        turned_query = rotate_back(grad_query.reshape(tokens, HQ, HD), cosine, sine)
        grad_query_gain = grad_query_gain + jnp.sum(turned_query * query_norm, axis=(0, 1))
        grad_query_low = (
            norm_back(query_heads, turned_query * gain_query.astype(jnp.float32))
            .reshape(tokens, HQ * HD)
            .astype(jnp.bfloat16)
        )
        turned_key = rotate_back(grad_keys_own.reshape(tokens, HK, HD), cosine, sine)
        grad_key_gain = grad_key_gain + jnp.sum(turned_key * key_norm, axis=(0, 1))
        grad_key_low = (
            norm_back(key_heads, turned_key * gain_key.astype(jnp.float32))
            .reshape(tokens, HK * HD)
            .astype(jnp.bfloat16)
        )
        grad_value_low = grad_values_own.astype(jnp.bfloat16)
        grad_scaled_in = (
            contract_last(grad_query_low, whole_query)
            + contract_last(grad_key_low, whole_key)
            + contract_last(grad_value_low, whole_value)
        )
        grad_attention_gain = grad_attention_gain + jnp.sum(grad_scaled_in * normed, axis=0)
        input_grads.append(
            grad_residual + norm_back(hidden, grad_scaled_in * gain_in.astype(jnp.float32))
        )
        stored.append(
            (
                scaled_in,
                grad_query_low,
                grad_key_low,
                grad_value_low,
                ff_in,
                grad_gate,
                grad_up,
                grad_proj,
                mixed_low,
                grad_out,
                hidden_low,
            )
        )
    columns = [jnp.concatenate([entry[index] for entry in stored], axis=0) for index in range(11)]
    (
        all_in,
        all_query,
        all_key,
        all_value,
        all_feed,
        all_gate,
        all_up,
        all_proj,
        all_mixed,
        all_out,
        all_hidden,
    ) = columns
    rows = query_weight.shape[0]
    head_rows = query_gain.shape[0]
    count = lax.axis_size(("dp", "ctx")) * rows
    row_ids = jnp.arange(count, dtype=jnp.int32)
    local = row_ids % rows
    place = jnp.clip(row_ids // rows * head_rows + local, 0, HD - 1)
    owned = local < head_rows
    gains = jnp.stack(
        [
            grad_attention_gain,
            grad_feed_gain,
            jnp.where(owned, jnp.take(grad_query_gain, place), 0.0),
            jnp.where(owned, jnp.take(grad_key_gain, place), 0.0),
        ],
        axis=1,
    )
    summed = lax.psum_scatter(
        jnp.concatenate(
            [
                contract_first(all_in, all_query).astype(BF),
                contract_first(all_in, all_key).astype(BF),
                contract_first(all_in, all_value).astype(BF),
                contract_first(all_feed, all_gate).astype(BF),
                contract_first(all_feed, all_up).astype(BF),
                contract_first(all_proj, all_mixed).astype(BF),
                contract_first(all_out, all_hidden).astype(BF),
                gains.astype(BF),
                jnp.zeros((count, 124), BF),
            ],
            axis=1,
        ),
        ("dp", "ctx"),
        scatter_dimension=0,
        tiled=True,
    ).astype(F32)
    widths = [HQ * HD, HK * HD, HK * HD, FF, FF, HQ * HD, FF, 128]
    pieces = []
    edge = 0
    for width in widths:
        pieces.append(summed[:, edge : edge + width])
        edge = edge + width
    gain_block = pieces[7]
    block_out = jnp.stack(outputs)[:, None]
    input_grad = jnp.stack(input_grads)[:, None]
    return (
        block_out,
        input_grad,
        gain_block[:, 0],
        gain_block[:head_rows, 2],
        gain_block[:head_rows, 3],
        pieces[0],
        pieces[1],
        pieces[2],
        pieces[5].T,
        gain_block[:, 1],
        pieces[3],
        pieces[4],
        pieces[6].T,
    )


def solution(mesh):
    shape = dict(mesh.shape)
    chips_hold_sequences = shape["dp"] == 4 and shape["ctx"] == 8

    def step(*arrays):
        if chips_hold_sequences and arrays[0].shape[2] == 64:
            return fused(*arrays)
        return general(*arrays)

    return jax.shard_map(
        step,
        mesh=mesh,
        in_specs=(
            P(None, "dp", "ctx", None),
            P(None, "dp", "ctx"),
            P(("dp", "ctx")),
            P(("dp", "ctx")),
            P(("dp", "ctx")),
            P(("dp", "ctx"), None),
            P(("dp", "ctx"), None),
            P(("dp", "ctx"), None),
            P(None, ("dp", "ctx")),
            P(("dp", "ctx")),
            P(("dp", "ctx"), None),
            P(("dp", "ctx"), None),
            P(None, ("dp", "ctx")),
            P(None, "dp", "ctx", None),
        ),
        out_specs=(
            P(None, "dp", "ctx", None),
            P(None, "dp", "ctx", None),
            P(("dp", "ctx")),
            P(("dp", "ctx")),
            P(("dp", "ctx")),
            P(("dp", "ctx"), None),
            P(("dp", "ctx"), None),
            P(("dp", "ctx"), None),
            P(None, ("dp", "ctx")),
            P(("dp", "ctx")),
            P(("dp", "ctx"), None),
            P(("dp", "ctx"), None),
            P(None, ("dp", "ctx")),
        ),
        check_vma=False,
    )
```

```python
import functools
import types

import jax
import jax.numpy as jnp
import numpy as np
from jax import lax
from jax.experimental import pallas as pl
from jax.experimental.pallas import tpu as pltpu
from jax.sharding import PartitionSpec as P

D = 1024
HQ = 16
HK = 8
HD = 128
FF = 3072
MB = 4

NORM_EPS = 1e-06
ROPE_BASE = 1000000.0
MASKED = -1e30
SCALE = HD ** (-0.5)
BF = jnp.bfloat16
F32 = jnp.float32
MESH = pl.DeviceIdType.MESH


def normalize(value):
    return value * lax.rsqrt(jnp.mean(value * value, axis=-1, keepdims=True) + NORM_EPS)


def norm_back(value, grad):
    scale = lax.rsqrt(jnp.mean(value * value, axis=-1, keepdims=True) + NORM_EPS)
    return scale * grad - value * (scale * scale * scale) * jnp.mean(
        grad * value, axis=-1, keepdims=True
    )


def rope_angles(first, count):
    positions = (first + jnp.arange(count, dtype=jnp.int32)).astype(F32)
    frequency = ROPE_BASE ** (-(jnp.arange(HD // 2, dtype=F32) * 2.0) / HD)
    return positions[:, None] * frequency[None, :]


KEYS = HK * HD // 2
WIDTHS = dict(
    k=KEYS + 128,
    v=KEYS,
    q=HQ * HD // 2,
    o=HQ * HD // 2,
    g=FF // 4,
    u=FF // 4,
    d=FF // 4,
)
ORDER = tuple(WIDTHS)
FEED = ("g", "u", "d")
PIECES = dict(k=(256, 384), v=(512,), q=(512, 512), o=(512, 512), g=(768,), u=(768,), d=(384, 384))
X_FIRST = (3,)
SUM_Y = dict(k=256, v=256, q=512, o=128)
HALF_HQ, HALF_HK = HQ // 2, HK // 2


def split_columns(name):
    return SUM_Y[name], WIDTHS[name] - SUM_Y[name]


def dot(left, right):
    return jnp.dot(left, right, preferred_element_type=F32)


def dot_nt(left, right):
    return lax.dot_general(left, right, (((1,), (1,)), ((), ())), preferred_element_type=F32)


def dot_tn(left, right):
    return lax.dot_general(left, right, (((0,), (0,)), ((), ())), preferred_element_type=F32)


class Semaphores:
    def __init__(self):
        self.count = 0

    def take(self, number=1):
        first = self.count
        self.count += number
        return first


def layer_kernel(names, tokens, *refs):
    at = types.SimpleNamespace(**dict(zip(names, refs)))
    sends, recvs = at.sends, at.recvs
    places = Semaphores()
    dp, ctx = lax.axis_index("dp"), lax.axis_index("ctx")
    x, c = lax.div(dp, 2), lax.rem(dp, 2)
    z, y = lax.div(ctx, 2), lax.rem(ctx, 2)
    ox, oc, oy = 1 - x, 1 - c, 1 - y
    sibling = (2 * x + oc, ctx)
    x_next = (2 * ox + c, ctx)
    x_cross = (2 * ox + oc, ctx)
    y_next = (dp, 2 * z + oy)
    length = 8 * tokens
    own_rows = 4 * tokens
    half = length // 2

    def z_at(step):
        return lax.rem(z + step, 4)

    def z_device(step):
        return (dp, 2 * z_at(step) + y)

    def remote(src, dst, place, device, recv_place=None):
        return pltpu.make_async_remote_copy(
            src_ref=src,
            dst_ref=dst,
            send_sem=sends.at[place],
            recv_sem=recvs.at[place if recv_place is None else recv_place],
            device_id=device,
            device_id_type=MESH,
        )

    def arrived(region, place, device):
        remote(region, region, place, device).wait_recv()

    barrier = pltpu.get_barrier_semaphore()
    me = c * 8 + ctx
    for other in range(1, 16):
        there = lax.rem(me + other, 16)
        pl.semaphore_signal(
            barrier, inc=1, device_id=(2 * x + lax.div(there, 8), lax.rem(there, 8)), device_id_type=MESH
        )
    pl.semaphore_signal(barrier, inc=1, device_id=x_next, device_id_type=MESH)
    pl.semaphore_signal(barrier, inc=1, device_id=x_cross, device_id_type=MESH)
    pl.semaphore_wait(barrier, 17)

    weight = {n: getattr(at, "w_" + n) for n in ORDER}
    shard = {n: getattr(at, "in_" + n) for n in ORDER}
    s0 = {n: places.take(3 if n in FEED else 1) for n in ORDER}
    lc = {n: places.take() for n in ORDER}
    pieces = []
    for n in ORDER:
        start = 0
        for size in PIECES[n]:
            pieces.append((n, pl.ds(start, size), places.take(4), places.take(), None if n in FEED else places.take()))
            start += size
    gather_sends = {n: [] for n in ORDER}

    def part(name, xx, cc):
        width = KEYS if name == "k" else WIDTHS[name]
        which = 2 * xx + cc if name in FEED else cc
        return shard[name].at[:, pl.ds(pl.multiple_of(which * width, width), width)]

    def keys_at(ref):
        return ref.at[:, pl.ds(0, KEYS)]

    def local(name):
        if name == "k":
            return pltpu.make_async_copy(part(name, x, c), keys_at(weight[name].at[x, c, z, y]), recvs.at[lc[name]])
        return pltpu.make_async_copy(part(name, x, c), weight[name].at[x, c, z, y], recvs.at[lc[name]])

    def begin(name, copy):
        copy.start()
        gather_sends[name].append(copy)

    extra_place = places.take()

    def gather_extra():
        rows = at.share_rows
        rows[...] = jnp.zeros_like(rows)
        for i, gain in enumerate((at.attention_gain, at.feedforward_gain, at.query_gain, at.key_gain)):
            rows[i : i + 1, : gain.shape[1]] = gain[...].astype(F32)
        columns = rows[...].T[: at.extra.shape[0]].astype(BF)
        at.extra[...] = columns
        weight["k"][x, c, z, y, :, KEYS:] = columns
        here = weight["k"].at[x, c, z, y, :, pl.ds(KEYS, 128)]
        begin("k", remote(at.extra, here, extra_place, sibling))

    def gather_core(name):
        here = weight[name].at[x, c, z, y]
        begin(name, remote(part(name, x, oc), keys_at(here) if name == "k" else here, s0[name], sibling))
        if name in FEED:
            begin(name, remote(part(name, ox, c), here, s0[name] + 1, x_next))
            begin(name, remote(part(name, ox, oc), here, s0[name] + 2, x_cross))
        local(name).start()

    def gather_core_done(name):
        w = weight[name]
        local(name).wait()
        if name == "k":
            arrived(keys_at(w.at[x, oc, z, y]), s0[name], sibling)
        else:
            arrived(w.at[x, oc, z, y], s0[name], sibling)
        if name in FEED:
            arrived(w.at[ox, c, z, y], s0[name] + 1, x_next)
            arrived(w.at[ox, oc, z, y], s0[name] + 2, x_cross)

    middle = (z == 1) | (z == 2)
    far = jnp.where(z == 1, 3, 0)

    def z_block(piece, zz):
        name, columns = piece[:2]
        w = weight[name]
        return w.at[:, :, zz, y, :, columns] if name in FEED else w.at[x, :, zz, y, :, columns]

    def z_copies(piece):
        block = z_block(piece, z)
        for there in range(4):
            distance = jnp.abs(there - z)
            sending = (distance == 1) | (distance == 2)
            yield sending, lambda there=there: remote(
                block, block, piece[2] + there, (dp, 2 * there + y), piece[2] + z
            )

    def z_forward(piece):
        block = z_block(piece, far)
        return remote(block, block, piece[2] + z, (dp, 2 * (3 - far) + y), piece[2] + far)

    def gather_z(number):
        piece = pieces[number]
        if piece[1].start == 0:
            gather_core_done(piece[0])
        if number == 1:
            arrived(weight["k"].at[x, oc, z, y, :, pl.ds(KEYS, 128)], extra_place, sibling)
        for sending, copy in z_copies(piece):
            pl.when(sending)(lambda copy=copy: copy().start())

    def gather_two(number):
        piece = pieces[number]
        name, columns, sem, y_sem, _ = piece
        w = weight[name]

        @pl.when(middle)
        def _():
            arrived(z_block(piece, far), sem + far, (dp, 2 * far + y))
            z_forward(piece).start()

        for source in range(4):
            waiting = (z != source) & jnp.logical_not(middle & (far == source))
            pl.when(waiting)(
                lambda source=source: arrived(z_block(piece, source), sem + source, (dp, 2 * source + y))
            )
        block = w.at[:, :, :, y, :, columns] if name in FEED else w.at[x, :, :, y, :, columns]
        begin(name, remote(block, block, y_sem, x_next if number in X_FIRST else y_next))

    def gather_three(number):
        name, columns, _, y_sem, x_sem = pieces[number]
        w = weight[name]
        if number in X_FIRST:
            arrived(w.at[ox, :, :, y, :, columns], y_sem, x_next)
            block = w.at[:, :, :, y, :, columns]
            begin(name, remote(block, block, x_sem, y_next))
            return
        arrived(w.at[x, :, :, oy, :, columns], y_sem, y_next)
        block = w.at[x, :, :, :, :, columns]
        begin(name, remote(block, block, x_sem, x_next))

    def gather_done(number):
        name, columns, _, y_sem, x_sem = pieces[number]
        w = weight[name]
        if name in FEED:
            arrived(w.at[:, :, :, oy, :, columns], y_sem, y_next)
        elif number in X_FIRST:
            arrived(w.at[:, :, :, oy, :, columns], x_sem, y_next)
        else:
            arrived(w.at[ox, :, :, :, :, columns], x_sem, x_next)

    def gather_sent(name):
        for copy in gather_sends[name]:
            copy.wait_send()
        for piece in pieces:
            if piece[0] == name:
                for sending, copy in z_copies(piece):
                    pl.when(sending)(lambda copy=copy: copy().wait_send())
                pl.when(middle)(lambda piece=piece: z_forward(piece).wait_send())

    slot = 2 * lax.rem(z, 2) + y
    target_core = lax.div(z, 2)

    class Reshard:
        def __init__(self, source, landing):
            self.source, self.landing = source, landing
            self.place, self.recv, self.own = places.take(4), places.take(4), places.take()

        def device(self, m):
            return (2 * x + target_core, 2 * m + c)

        def keeps(self, m):
            return (target_core == c) & (z == m) & (y == c)

        def copy(self, m):
            return remote(
                self.source.at[m], self.landing(target_core, slot), self.place + m, self.device(m), self.recv + slot
            )

        def keep(self, m):
            return pltpu.make_async_copy(
                self.source.at[m], self.landing(target_core, slot), recvs.at[self.own]
            )

        def start(self):
            for m in range(MB):
                pl.when(jnp.logical_not(self.keeps(m)))(lambda m=m: self.copy(m).start())
                pl.when(self.keeps(m))(lambda m=m: self.keep(m).start())

        def wait(self):
            for j in range(4):
                mine = (y == c) & (4 * c + j == ctx)
                region = self.landing(c, j)
                device = (2 * x + y, 4 * c + j)
                pl.when(jnp.logical_not(mine))(
                    lambda j=j, region=region, device=device: arrived(region, self.recv + j, device)
                )
                pl.when(mine)(
                    lambda region=region: pltpu.make_async_copy(
                        region, region, recvs.at[self.own]
                    ).wait()
                )

        def sent(self):
            for m in range(MB):
                pl.when(jnp.logical_not(self.keeps(m)))(lambda m=m: self.copy(m).wait_send())

    class Return:
        def __init__(self, source, landing):
            self.source, self.landing = source, landing
            self.place, self.recv, self.own = places.take(4), places.take(4), places.take()

        def keeps(self, j):
            return (y == c) & (4 * c + j == ctx)

        def copy(self, j):
            return remote(
                self.source.at[j], self.landing.at[z], self.place + j, (2 * x + y, 4 * c + j), self.recv + z
            )

        def keep(self, j):
            return pltpu.make_async_copy(
                self.source.at[j], self.landing.at[z], recvs.at[self.own]
            )

        def start(self, j):
            pl.when(jnp.logical_not(self.keeps(j)))(lambda: self.copy(j).start())
            pl.when(self.keeps(j))(lambda: self.keep(j).start())

        def finish(self):
            for j in range(4):
                pl.when(jnp.logical_not(self.keeps(j)))(lambda j=j: self.copy(j).wait_send())
                pl.when(self.keeps(j))(lambda j=j: self.keep(j).wait())
            for m in range(MB):
                mine = (target_core == c) & (z == m) & (y == c)
                device = (2 * x + target_core, 2 * m + c)
                pl.when(jnp.logical_not(mine))(
                    lambda m=m, device=device: arrived(self.landing.at[m], self.recv + m, device)
                )

    hidden_own, cot_all = at.hidden_own, at.cot_all
    hidden_move = Reshard(at.hidden_in, lambda core, j: hidden_own.at[j])
    number_move = Reshard(at.number_out, lambda core, j: at.number_own.at[j])
    cot_move = Reshard(at.cotangent, lambda core, j: cot_all.at[4 * (2 * x + core) + j])
    out_move = Return(at.out_own, at.block_out)
    grad_move = Return(at.grad_own, at.input_grad)
    class Swap:
        def __init__(self, source, there, here):
            self.place = places.take()
            self.out = remote(source, there, self.place, sibling)
            self.here = here

        def start(self):
            self.out.start()

        def wait(self):
            self.out.wait_send()
            arrived(self.here, self.place, sibling)

    def swap_rows(ref):
        mine, theirs = ref.at[pl.ds(own_at, own_rows)], ref.at[pl.ds(other_at, own_rows)]
        return Swap(mine, mine, theirs)

    own_at = pl.multiple_of(c * own_rows, own_rows)
    other_at = pl.multiple_of(oc * own_rows, own_rows)

    class Spread:
        def __init__(self, block):
            self.block = block
            self.place = places.take(3)

        def start(self):
            own = self.block(x, c)
            self.near = remote(own, own, self.place, sibling)
            self.across = remote(own, own, self.place + 1, x_next)
            self.near.start()
            self.across.start()

        def near_wait(self):
            arrived(self.block(x, oc), self.place, sibling)

        def pass_on(self):
            arrived(self.block(ox, c), self.place + 1, x_next)
            block = self.block(ox, c)
            self.far = remote(block, block, self.place + 2, sibling)
            self.far.start()

        def far_wait(self):
            arrived(self.block(ox, oc), self.place + 2, sibling)

        def sent(self):
            for copy in (self.near, self.across, self.far):
                copy.wait_send()

    r1 = {n: places.take(1 if n in FEED else 2) for n in ORDER}
    r2 = {n: places.take(0 if n in FEED else 2) for n in ORDER}
    r3 = {n: places.take(4) for n in ORDER}
    r4 = {n: places.take(3 if n in FEED else 1) for n in ORDER}
    sum_sends = []
    grads = dict(weight, d=at.grad_d)

    def send(copy):
        copy.start()
        sum_sends.append(copy)

    def sum_block(name, zz):
        w = grads[name]
        return w.at[:, :, zz, y] if name in FEED else w.at[x, :, zz, y]

    end = jnp.logical_not(middle)
    neighbour = jnp.where(z == 0, 1, 2)

    def sum_z_copies(name):
        landing = getattr(at, "r3_" + name)
        for there in range(4):
            distance = jnp.abs(there - z)
            sending = (distance == 1) | ((distance == 2) & end)
            yield sending, lambda there=there: remote(
                sum_block(name, there), landing.at[z], r3[name] + there, (dp, 2 * there + y), r3[name] + z
            )

        yield end, lambda: remote(
            sum_block(name, 3 - z), landing.at[neighbour], r3[name] + z, (dp, 2 * neighbour + y), r3[name] + neighbour
        )

    def sum_z_late(name):
        landing = getattr(at, "r3_" + name)
        return remote(sum_block(name, far), landing.at[z], r3[name] + far, (dp, 2 * far + y), r3[name] + z)

    def sum_z(name):
        for sending, copy in sum_z_copies(name):
            pl.when(sending)(lambda copy=copy: copy().start())

    def sum_z_pass(name):
        landing, w = getattr(at, "r3_" + name), grads[name]

        @pl.when(middle)
        def _():
            arrived(landing.at[z], r3[name] + z, (dp, 2 * (3 - far) + y))
            if name in FEED:
                for xx in range(2):
                    for cc in range(2):
                        w[xx, cc, far, y] += landing[z, xx, cc]
            else:
                for cc in range(2):
                    w[x, cc, far, y] += landing[z, cc]
            sum_z_late(name).start()

    def sum_one(name):
        w = grads[name]
        if name in FEED:
            send(remote(w.at[:, :, :, oy], getattr(at, "r1a_" + name), r1[name], y_next))
            return
        first, second = split_columns(name)
        send(remote(w.at[:, :, :, oy, :, pl.ds(0, first)], getattr(at, "r1a_" + name), r1[name], y_next))
        if second:
            send(remote(w.at[ox, :, :, :, :, pl.ds(first, second)], getattr(at, "r1b_" + name), r1[name] + 1, x_next))

    def sum_two(name):
        w = grads[name]
        arrived(getattr(at, "r1a_" + name), r1[name], y_next)
        first, second = (WIDTHS[name], 0) if name in FEED else split_columns(name)

        @pl.loop(0, 16)
        def _(i):
            xx, cc, zz = lax.div(i, 8), lax.rem(lax.div(i, 4), 2), lax.rem(i, 4)
            w[xx, cc, zz, y, :, pl.ds(0, first)] += getattr(at, "r1a_" + name)[xx, cc, zz]

        if name in FEED:
            sum_z(name)
            return
        send(remote(w.at[ox, :, :, y, :, pl.ds(0, first)], getattr(at, "r2a_" + name), r2[name], x_next))
        if second:
            arrived(getattr(at, "r1b_" + name), r1[name] + 1, x_next)

            @pl.loop(0, 16)
            def _(i):
                cc, zz, yy = lax.div(i, 8), lax.rem(lax.div(i, 2), 4), lax.rem(i, 2)
                w[x, cc, zz, yy, :, pl.ds(first, second)] += getattr(at, "r1b_" + name)[cc, zz, yy]

            send(remote(w.at[x, :, :, oy, :, pl.ds(first, second)], getattr(at, "r2b_" + name), r2[name] + 1, y_next))

    def sum_three(name):
        w = grads[name]
        first, second = split_columns(name)
        arrived(getattr(at, "r2a_" + name), r2[name], x_next)
        if second:
            arrived(getattr(at, "r2b_" + name), r2[name] + 1, y_next)

        @pl.loop(0, 8)
        def _(i):
            cc, zz = lax.div(i, 4), lax.rem(i, 4)
            w[x, cc, zz, y, :, pl.ds(0, first)] += getattr(at, "r2a_" + name)[cc, zz]
            if second:
                w[x, cc, zz, y, :, pl.ds(first, second)] += getattr(at, "r2b_" + name)[cc, zz]

        sum_z(name)

    def sum_four(name):
        w, landed = grads[name], getattr(at, "r3_" + name)
        for source in range(4):
            coming = (z != source) & (jnp.abs(source - z) != 3)
            pl.when(coming)(
                lambda source=source: arrived(landed.at[source], r3[name] + source, (dp, 2 * source + y))
            )

        def total(*place):
            mine = w[(*place, z, y)] if name in FEED else w[(x, *place, z, y)]
            value = mine.astype(F32)
            value = value + landed[(jnp.where(z == 0, 1, z - 1), *place)].astype(F32)
            value = value + landed[(jnp.where(z == 0, 2, jnp.where(z == 3, 1, z + 1)), *place)].astype(F32)
            third = landed[(far, *place)].astype(F32)
            return jnp.where(middle, value + third, value)

        width = WIDTHS[name]
        staged, result = getattr(at, "r4_" + name), getattr(at, "out_" + name)
        if name in FEED:
            columns = pl.ds(pl.multiple_of(dp * width, width), width)
            for i, (xx, cc, device) in enumerate(((ox, oc, x_cross), (ox, c, x_next), (x, oc, sibling))):
                staged[i] = total(xx, cc).astype(BF)
                send(remote(staged.at[i], getattr(at, "r5_" + name).at[i], r4[name] + i, device))
            result[:, columns] = total(x, c)
            return
        staged[...] = total(oc)
        columns = pl.ds(pl.multiple_of(c * width, width), width)
        send(remote(staged, result.at[:, columns], r4[name], sibling))
        result[:, columns] = total(c)

    def sum_done(name):
        width = WIDTHS[name]
        if name in FEED:
            for i, (xx, cc, device) in enumerate(((ox, oc, x_cross), (ox, c, x_next), (x, oc, sibling))):
                columns = pl.ds(pl.multiple_of((2 * xx + cc) * width, width), width)
                arrived(getattr(at, "r5_" + name).at[i], r4[name] + i, device)
                getattr(at, "out_" + name)[:, columns] = getattr(at, "r5_" + name)[i].astype(F32)
        else:
            columns = pl.ds(pl.multiple_of(oc * width, width), width)
            arrived(getattr(at, "out_" + name).at[:, columns], r4[name], sibling)

    gains, head_gains = at.gains, at.head_gains
    scaled, ff_in, grad_proj = at.scaled, at.ff_in, at.grad_proj
    residual, grad_residual = at.residual, at.grad_residual
    acc_own = at.acc_own
    scaled_swap, proj_swap = swap_rows(scaled), swap_rows(grad_proj)
    ff_spread = Spread(lambda xx, cc: ff_in.at[2 * xx + cc])
    cot_spread = Spread(lambda xx, cc: cot_all.at[pl.ds(4 * (2 * xx + cc), 4)])
    partials = [Swap(at.partial_out.at[i], at.partial_in.at[i], at.partial_in.at[i]) for i in range(2)]
    feed_near = [
        [Swap(at.near_out.at[i, k], at.near_in.at[i, k], at.near_in.at[i, k]) for k in range(2)] for i in range(2)
    ]
    feed_cross = []
    for i in range(2):
        place = places.take()
        feed_cross.append((remote(at.cross_out.at[i], at.cross_in.at[i], place, x_next), place))

    def selector():
        row = lax.broadcasted_iota(jnp.int32, (D, HD), 0)
        column = lax.broadcasted_iota(jnp.int32, (D, HD), 1)
        local_row = row & 31
        hit = ((row >> 5) * 4 + local_row == column) & (local_row < 4)
        return jnp.where(hit, 1.0, 0.0).astype(BF)

    def prepare_gains():
        columns = weight["k"][:, :, :, :, :, KEYS:].reshape(D, 128).astype(F32)
        for i in range(8):
            gains[:, i * 128 : (i + 1) * 128] = columns[i * 128 : (i + 1) * 128].T[:8]
        head_gains[...] = dot(gains[...].astype(BF), selector())

    def prepare_numbers():
        for m in range(MB):
            at.share_rows[:1, :tokens] = at.segments[m].astype(F32)
            at.number_out[m] = jnp.broadcast_to(at.share_rows[:1], (128, 128)).T[:tokens].astype(BF)

    def prepare_mask():
        def number(i):
            return scaled[i * 128 : (i + 1) * 128, D:].astype(F32)

        for j in range(4):
            key = number(j).T
            for i in range(4):
                place = slice(i * 128, (i + 1) * 128), slice(j * 128, (j + 1) * 128)
                if j > i:
                    at.bias[place] = jnp.full((128, 128), MASKED, F32)
                    continue
                seen = number(i) == key
                if i == j:
                    seen = seen & (
                        lax.broadcasted_iota(jnp.int32, (128, 128), 1)
                        <= lax.broadcasted_iota(jnp.int32, (128, 128), 0)
                    )
                at.bias[place] = jnp.where(seen, 0.0, MASKED)

    def own_block(j):
        return pl.ds(pl.multiple_of(c * own_rows + j * tokens, tokens), tokens)

    def here_block(j):
        return pl.ds(pl.multiple_of(j * tokens, tokens), tokens)

    def scale_input():
        @pl.loop(0, 4)
        def _(j):
            value = normalize(hidden_own[j].astype(F32)) * gains[0:1]
            scaled[own_block(j), :D] = value.astype(BF)
            scaled[own_block(j), D:] = at.number_own[j]

    def columns_of(name, t, size=256):
        return weight[name][:, :, :, :, :, pl.ds(pl.multiple_of(t * size, size), size)].reshape(D, size)

    def rows_of(name, t):
        if name == "k":
            return weight[name][lax.div(t, 2), lax.rem(t, 2), :, :, :, :KEYS].reshape(D // 4, KEYS)
        return weight[name][lax.div(t, 2), lax.rem(t, 2)].reshape(D // 4, WIDTHS[name])

    cosine, sine = at.cosine, at.sine

    def turn(value):
        return value * cosine[...] + pltpu.roll(value, HD // 2, 1) * sine[...]

    def project_heads(name, count, gain, kept, turned):
        @pl.loop(0, count // 2)
        def _(t):
            both = dot(scaled[:, :D], columns_of(name, t))
            for i in range(2):
                value = both[:, i * HD : (i + 1) * HD]
                kept[2 * t + i] = value
                turned[2 * t + i] = turn(normalize(value) * gain).astype(BF)

    def project_values():
        @pl.loop(0, WIDTHS["v"] // 256)
        def _(t):
            both = dot(scaled[:, :D], columns_of("v", t))
            for i in range(2):
                at.values[2 * t + i] = both[:, i * HD : (i + 1) * HD].astype(BF)

    def probabilities(head, pair, block):
        rows = slice(block * half, (block + 1) * half)
        seen = slice(0, (block + 1) * half)
        scores = dot_nt(at.queries[head, rows], at.keys[pair, seen]) * SCALE + at.bias[rows, seen]
        terms = jnp.exp(scores - jnp.max(scores, axis=-1, keepdims=True))
        return terms * (1.0 / jnp.sum(terms, axis=-1, keepdims=True))

    def attend(first, last):
        @pl.loop(first, last)
        def _(head):
            pair = lax.div(head, 2)
            for block in range(2):
                seen = slice(0, (block + 1) * half)
                low = probabilities(head, pair, block).astype(BF)
                at.mixed[
                    block * half : (block + 1) * half, pl.ds(pl.multiple_of(head * HD, HD), HD)
                ] = dot(low, at.values[pair, seen]).astype(BF)

    def column_quarters(body):
        @pl.loop(0, 4)
        def _(t):
            body(t, pl.ds(pl.multiple_of(t * (D // 4), D // 4), D // 4))

    def partial_product(index, terms):
        def rows_times(first, t):
            return sum(dot_nt(left(pl.ds(first, own_rows)), rows_of(name, t)) for left, name in terms)

        def theirs(t, columns):
            at.partial_out[index, :, columns] = rows_times(other_at, t).astype(BF)

        def mine(t, columns):
            acc_own[:, columns] = rows_times(own_at, t)

        column_quarters(theirs)
        partials[index].start()
        column_quarters(mine)

    def own_sum(index, j):
        return acc_own[here_block(j)] + at.partial_in[index, here_block(j)].astype(F32)

    def feed_product(index, terms):
        acc = at.acc_feed if index == 0 else acc_own

        def rows_times(xx, cc, t):
            first = pl.multiple_of((2 * xx + cc) * own_rows, own_rows)
            return sum(dot_nt(left[pl.ds(first, own_rows)], rows_of(name, t)) for left, name in terms)

        def give(k, xx):
            def body(t, columns):
                at.near_out[index, k, :, columns] = rows_times(xx, oc, t).astype(BF)

            column_quarters(body)
            feed_near[index][k].start()

        def keep(xx):
            def body(t, columns):
                acc[:, columns] = rows_times(xx, c, t)

            column_quarters(body)

        give(0, ox)
        keep(ox)
        feed_near[index][0].wait()
        near = at.near_in

        @pl.loop(0, 4)
        def _(j):
            rows = here_block(j)
            at.cross_out[index, rows] = (acc[rows] + near[index, 0, rows].astype(F32)).astype(BF)

        if index == 1:
            feed_cross[index][0].start()
        give(1, x)
        keep(x)

    def feed_wait(index):
        feed_near[index][1].wait()
        copy, place = feed_cross[index]
        copy.wait_send()
        arrived(at.cross_in.at[index], place, x_next)

    def feed_sum(index, j):
        rows = here_block(j)
        acc = at.acc_feed if index == 0 else acc_own
        return acc[rows] + at.near_in[index, 1, rows].astype(F32) + at.cross_in[index, rows].astype(F32)

    def add_residual():
        @pl.loop(0, 4)
        def _(j):
            value = hidden_own[j].astype(F32) + own_sum(0, j)
            residual[here_block(j)] = value
            ff_in[2 * x + c, here_block(j)] = (normalize(value) * gains[1:2]).astype(BF)

    gate_part, up_part, hidden_low = at.gate_part, at.up_part, at.hidden_low

    def chip_rows(xx):
        return pl.ds(pl.multiple_of(xx * length, length), length)

    def feed_forward(xx):
        rows = chip_rows(xx)

        @pl.loop(0, WIDTHS["g"] // 256)
        def _(t):
            columns = pl.ds(pl.multiple_of(t * 256, 256), 256)
            left = ff_in[pl.ds(2 * xx, 2)].reshape(length, D)
            gate = dot(left, columns_of("g", t))
            up = dot(left, columns_of("u", t))
            sigmoid = 1.0 / (1.0 + jnp.exp(-gate))
            swish = gate * sigmoid
            hidden_low[rows, columns] = (swish * up).astype(BF)
            up_part[rows, columns] = swish.astype(BF)
            gate_part[rows, columns] = (up * sigmoid * (1.0 + gate * (1.0 - sigmoid))).astype(BF)

    def write_out():
        @pl.loop(0, 4)
        def _(j):
            at.out_own[j] = (residual[here_block(j)] + feed_sum(0, j)).astype(BF)

        for j in range(4):
            out_move.start(j)

    def grad_hidden():
        @pl.loop(0, 2 * (WIDTHS["d"] // 256))
        def _(i):
            xx, t = lax.div(i, 3), lax.rem(i, 3)
            rows, columns = chip_rows(xx), pl.ds(pl.multiple_of(t * 256, 256), 256)
            grad = dot(cot_all[pl.ds(8 * xx, 8)].reshape(length, D), columns_of("d", t))
            gate_part[rows, columns] = (grad * gate_part[rows, columns].astype(F32)).astype(BF)
            up_part[rows, columns] = (grad * up_part[rows, columns].astype(F32)).astype(BF)

    turned_rows = at.turned_rows

    def transpose_rows(load, count):
        @pl.loop(0, D // 128)
        def _(t):
            place = pl.ds(pl.multiple_of(t * 128, 128), 128)
            turned_rows[place, :count] = load(place).reshape(count, 128).T

    def weight_grad(name, right, count):
        if name != "d":
            gather_sent(name)

        @pl.loop(0, (KEYS if name == "k" else WIDTHS[name]) // 256)
        def _(t):
            columns = pl.ds(pl.multiple_of(t * 256, 256), 256)
            grad = dot(turned_rows[:, :count], right(columns))
            grads[name][:, :, :, :, :, columns] = grad.astype(BF).reshape(2, 2, 4, 2, 32, 256)

    grad_gains = at.grad_gains

    def back_residual():
        grad_gains[...] = jnp.zeros_like(grad_gains)

        @pl.loop(0, 4)
        def _(j):
            value = residual[here_block(j)]
            grad = feed_sum(1, j)
            scale = lax.rsqrt(jnp.mean(value * value, axis=-1, keepdims=True) + NORM_EPS)
            grad_gains[1:2] += jnp.sum(grad * (value * scale), axis=0, keepdims=True)
            total = cot_all[4 * (2 * x + c) + j].astype(F32) + norm_back(value, grad * gains[1:2])
            grad_residual[here_block(j)] = total
            grad_proj[own_block(j)] = total.astype(BF)

    grad_mixed, grad_heads = ff_in, cot_all

    def back_mixed():
        @pl.loop(0, WIDTHS["o"] // 256)
        def _(t):
            columns = pl.ds(pl.multiple_of(t * 256, 256), 256)
            grad = dot(grad_proj[...], columns_of("o", t)).astype(BF)
            grad_mixed[:2, :, columns] = grad.reshape(2, half, 256)

    def put_heads(first, columns, value):
        grad_heads[first : first + 8, :, columns] = value.astype(BF).reshape(8, tokens, HD)

    def head_columns(first, columns):
        return grad_heads[first : first + 8, :, columns].reshape(length, columns.size)

    def head_rows(first, rows, start, width):
        block = first + lax.div(rows.start, tokens)
        return grad_heads[pl.ds(block, 4), :, start : start + width].reshape(own_rows, width)

    grad_head_gains = at.grad_head_gains

    def turn_back(value):
        return value * cosine[...] - pltpu.roll(value, HD // 2, 1) * sine[...]

    def back_head(value, grad, row, first, columns):
        scale = lax.rsqrt(jnp.mean(value * value, axis=-1, keepdims=True) + NORM_EPS)
        turned = turn_back(grad)
        grad_head_gains[row : row + 1] += jnp.sum(turned * (value * scale), axis=0, keepdims=True)
        put_heads(first, columns, norm_back(value, turned * head_gains[row : row + 1]))

    grad_key, grad_value, grad_query = at.grad_key, at.grad_value, at.grad_query

    def back_attend(first, last):
        if first == 0:
            grad_head_gains[...] = jnp.zeros_like(grad_head_gains)

        @pl.loop(first, last)
        def _(pair):
            for i in range(2):
                head = 2 * pair + i
                lanes = pl.ds(pl.multiple_of(head * HD, HD), HD)
                for block in (1, 0):
                    rows = slice(block * half, (block + 1) * half)
                    seen = slice(0, (block + 1) * half)
                    probs = probabilities(head, pair, block)
                    grad_out = grad_mixed[block, :, lanes]
                    grad_probs = dot_nt(grad_out, at.values[pair, seen])
                    delta = jnp.sum(probs * grad_probs, axis=-1, keepdims=True)
                    grad_scores = (probs * (grad_probs - delta)).astype(BF)
                    grad_query[rows] = dot(grad_scores, at.keys[pair, seen]) * SCALE
                    key_part = dot_tn(grad_scores, at.queries[head, rows]) * SCALE
                    value_part = dot_tn(probs.astype(BF), grad_out)
                    if i == 0 and block == 1:
                        grad_key[...] = key_part
                        grad_value[...] = value_part
                    else:
                        grad_key[seen] += key_part
                        grad_value[seen] += value_part
                back_head(at.query_acc[head], grad_query[...], 2, 0, lanes)
            lanes = pl.ds(pl.multiple_of(pair * HD, HD), HD)
            back_head(at.key_acc[pair], grad_key[...], 3, 8, lanes)
            put_heads(8, pl.ds(pl.multiple_of(KEYS + pair * HD, HD), HD), grad_value[...])

    def back_input():
        @pl.loop(0, 4)
        def _(j):
            value = hidden_own[j].astype(F32)
            grad = own_sum(1, j)
            scale = lax.rsqrt(jnp.mean(value * value, axis=-1, keepdims=True) + NORM_EPS)
            grad_gains[0:1] += jnp.sum(grad * (value * scale), axis=0, keepdims=True)
            at.grad_own[j] = (
                grad_residual[here_block(j)] + norm_back(value, grad * gains[0:1])
            ).astype(BF)

        for j in range(4):
            grad_move.start(j)

    def gain_grads():
        grad_gains[...] += dot_nt(grad_head_gains[...].astype(BF), selector())
        for i in range(8):
            block = jnp.concatenate(
                [grad_gains[:, i * 128 : (i + 1) * 128], jnp.zeros((120, 128), F32)], axis=0
            ).T
            weight["k"][i // 4, (i // 2) % 2, 2 * (i % 2) : 2 * (i % 2) + 2, :, :, KEYS:] = block.astype(BF).reshape(
                2, 2, 32, 128
            )

    gather_core("k")
    gather_extra()
    gather_z(0)
    gather_core("v")
    gather_z(1)
    for name in ("q", "o", *FEED):
        gather_core(name)
    prepare_numbers()
    gather_two(0)
    gather_z(2)
    gather_two(1)
    gather_three(0)
    gather_z(3)
    gather_two(2)
    gather_three(1)
    gather_z(4)
    hidden_move.start()
    number_move.start()
    gather_two(3)
    gather_three(2)
    gather_z(5)
    gather_two(4)
    gather_z(6)
    gather_done(0)
    gather_done(1)
    gather_three(3)
    prepare_gains()
    gather_two(5)
    gather_z(7)
    hidden_move.wait()
    number_move.wait()
    scale_input()
    scaled_swap.start()
    gather_two(6)
    gather_z(8)
    scaled_swap.wait()
    prepare_mask()
    project_heads("k", HALF_HK, head_gains[3:4], at.key_acc, at.keys)
    gather_done(2)
    gather_three(4)
    project_values()
    gather_two(7)
    gather_z(9)
    gather_done(3)
    gather_three(5)
    gather_done(4)
    gather_three(6)
    project_heads("q", HALF_HQ, head_gains[2:3], at.query_acc, at.queries)
    gather_two(8)
    gather_z(10)
    cot_move.start()
    attend(0, 4)
    gather_two(9)
    attend(4, 8)
    gather_done(5)
    gather_done(6)
    partial_product(0, [(lambda rows: at.mixed[rows], "o")])
    partials[0].wait()
    add_residual()
    ff_spread.start()
    gather_two(10)
    cot_move.wait()
    cot_spread.start()
    gather_done(7)
    gather_done(8)
    ff_spread.near_wait()
    feed_forward(x)
    ff_spread.pass_on()
    ff_spread.far_wait()
    feed_forward(ox)
    cot_spread.pass_on()
    cot_spread.near_wait()
    cot_spread.far_wait()
    transpose_rows(lambda columns: cot_all[:, :, columns], 2 * length)

    weight_grad("d", lambda columns: hidden_low[:, columns], 2 * length)
    sum_one("d")
    gather_done(9)
    gather_done(10)
    grad_hidden()
    feed_product(1, [(gate_part, "g"), (up_part, "u")])
    transpose_rows(lambda columns: ff_in[:, :, columns], 2 * length)
    weight_grad("g", lambda columns: gate_part[:, columns], 2 * length)
    sum_one("g")
    weight_grad("u", lambda columns: up_part[:, columns], 2 * length)
    feed_wait(1)
    back_residual()
    proj_swap.start()
    ff_spread.sent()
    cot_spread.sent()
    sum_two("d")
    proj_swap.wait()
    back_mixed()
    transpose_rows(lambda columns: grad_proj[:, columns], length)
    weight_grad("o", lambda columns: at.mixed[:, columns], length)
    sum_one("o")
    sum_one("u")
    back_attend(0, 2)
    sum_two("g")
    sum_z_pass("d")
    back_attend(2, 4)
    partial_product(
        1,
        [
            (lambda rows: head_rows(0, rows, 0, WIDTHS["q"]), "q"),
            (lambda rows: head_rows(8, rows, 0, KEYS), "k"),
            (lambda rows: head_rows(8, rows, KEYS, KEYS), "v"),
        ],
    )
    transpose_rows(lambda columns: scaled[:, columns], length)
    weight_grad("q", lambda columns: head_columns(0, columns), length)
    sum_one("q")
    sum_two("o")
    weight_grad("v", lambda columns: head_columns(8, pl.ds(columns.start + KEYS, 256)), length)
    weight_grad("k", lambda columns: head_columns(8, columns), length)
    sum_two("u")
    sum_one("v")
    feed_product(0, [(hidden_low, "d")])
    feed_cross[0][0].start()
    partials[1].wait()
    back_input()
    gain_grads()
    sum_z_pass("g")
    sum_four("d")
    sum_three("o")
    sum_z_pass("u")
    sum_four("g")
    sum_two("q")
    sum_one("k")
    sum_z_pass("o")
    sum_four("u")
    feed_wait(0)
    write_out()
    sum_three("q")
    sum_two("v")
    sum_z_pass("q")
    sum_four("o")
    sum_three("v")
    sum_two("k")
    sum_z_pass("v")
    sum_four("q")
    sum_three("k")
    sum_four("v")
    sum_z_pass("k")
    sum_four("k")
    for name in ("d", "g", "u", "o", "q", "v", "k"):
        sum_done(name)
    for copy in sum_sends:
        copy.wait_send()
    for name in ORDER:
        for sending, copy in sum_z_copies(name):
            pl.when(sending)(lambda copy=copy: copy().wait_send())
        pl.when(middle)(lambda name=name: sum_z_late(name).wait_send())
    gather_sent("d")
    hidden_move.sent()
    number_move.sent()
    cot_move.sent()
    out_move.finish()
    grad_move.finish()
    assert places.count == SEMAPHORES, places.count


SEMAPHORES = 204


def fused(
    hidden_in,
    segments,
    attention_gain,
    query_gain,
    key_gain,
    query_weight,
    key_weight,
    value_weight,
    out_weight,
    feedforward_gain,
    gate_weight,
    up_weight,
    down_weight,
    cotangent,
):
    tokens = hidden_in.shape[2]
    length = 8 * tokens
    rows = query_weight.shape[0]
    heads = query_gain.shape[0]
    positions = np.arange(length, dtype=np.float32)
    frequency = (ROPE_BASE ** (-(np.arange(HD // 2, dtype=np.float32) * 2.0) / HD)).astype(np.float32)
    angles = (positions[:, None] * frequency[None, :]).astype(np.float64)
    cosine = np.concatenate([np.cos(angles), np.cos(angles)], axis=-1).astype(np.float32)
    sine = np.concatenate([-np.sin(angles), np.sin(angles)], axis=-1).astype(np.float32)

    vmem, anywhere = pl.BlockSpec(memory_space=pltpu.VMEM), pl.BlockSpec(memory_space=pl.ANY)
    inputs = dict(
        hidden_in=(hidden_in[:, 0], anywhere),
        cotangent=(cotangent[:, 0], anywhere),
        segments=(segments, vmem),
        cosine=(jnp.asarray(cosine), vmem),
        sine=(jnp.asarray(sine), vmem),
        attention_gain=(attention_gain[None], vmem),
        feedforward_gain=(feedforward_gain[None], vmem),
        query_gain=(query_gain[None], vmem),
        key_gain=(key_gain[None], vmem),
        in_k=(key_weight, anywhere),
        in_v=(value_weight, anywhere),
        in_q=(query_weight, anywhere),
        in_o=(out_weight.T, anywhere),
        in_g=(gate_weight, anywhere),
        in_u=(up_weight, anywhere),
        in_d=(down_weight.T, anywhere),
    )
    block = (MB, tokens, D)
    outputs = dict(block_out=(block, BF, anywhere), input_grad=(block, BF, anywhere))
    for name, width in WIDTHS.items():
        outputs["out_" + name] = ((rows, width * (4 if name in FEED else 2)), F32, vmem)
    own = 4 * tokens
    scratch = dict(
        share_rows=((128, 128), F32),
        extra=((rows, 128), BF),
        number_out=((MB, tokens, 128), BF),
        number_own=((4, tokens, 128), BF),
        hidden_own=((4, tokens, D), BF),
        cot_all=((16, tokens, D), BF),
        gains=((8, D), F32),
        head_gains=((8, HD), F32),
        grad_gains=((8, D), F32),
        grad_head_gains=((8, HD), F32),
        bias=((length, length), F32),
        scaled=((length, D + 128), BF),
        query_acc=((HALF_HQ, length, HD), F32),
        key_acc=((HALF_HK, length, HD), F32),
        queries=((HALF_HQ, length, HD), BF),
        keys=((HALF_HK, length, HD), BF),
        values=((HALF_HK, length, HD), BF),
        mixed=((length, HALF_HQ * HD), BF),
        acc_own=((own, D), F32),
        acc_feed=((own, D), F32),
        partial_out=((2, own, D), BF),
        partial_in=((2, own, D), BF),
        near_out=((2, 2, own, D), BF),
        near_in=((2, 2, own, D), BF),
        cross_out=((2, own, D), BF),
        cross_in=((2, own, D), BF),
        residual=((own, D), F32),
        grad_residual=((own, D), F32),
        ff_in=((4, own, D), BF),
        gate_part=((2 * length, FF // 4), BF),
        up_part=((2 * length, FF // 4), BF),
        hidden_low=((2 * length, FF // 4), BF),
        grad_d=((2, 2, 4, 2, rows, FF // 4), BF),
        grad_proj=((length, D), BF),
        grad_key=((length, HD), F32),
        grad_value=((length, HD), F32),
        grad_query=((length, HD), F32),
        turned_rows=((D, 2 * length), BF),
        out_own=((4, tokens, D), BF),
        grad_own=((4, tokens, D), BF),
    )
    for name, width in WIDTHS.items():
        scratch["w_" + name] = ((2, 2, 4, 2, rows, width), BF)
        if name in FEED:
            scratch["r1a_" + name] = ((2, 2, 4, rows, width), BF)
            scratch["r3_" + name] = ((4, 2, 2, rows, width), BF)
            scratch["r4_" + name] = ((3, rows, width), BF)
            scratch["r5_" + name] = ((3, rows, width), BF)
            continue
        first, second = split_columns(name)
        scratch["r1a_" + name] = ((2, 2, 4, rows, first), BF)
        scratch["r2a_" + name] = ((2, 4, rows, first), BF)
        if second:
            scratch["r1b_" + name] = ((2, 4, 2, rows, second), BF)
            scratch["r2b_" + name] = ((2, 4, rows, second), BF)
        scratch["r3_" + name] = ((4, 2, rows, width), BF)
        scratch["r4_" + name] = ((rows, width), F32)
    names = (*inputs, *outputs, *scratch, "sends", "recvs")
    results = pl.pallas_call(
        functools.partial(layer_kernel, names, tokens),
        out_shape=[jax.ShapeDtypeStruct(shape, dtype) for shape, dtype, _ in outputs.values()],
        in_specs=[spec for _, spec in inputs.values()],
        out_specs=[spec for _, _, spec in outputs.values()],
        scratch_shapes=[pltpu.VMEM(shape, dtype) for shape, dtype in scratch.values()]
        + [pltpu.SemaphoreType.DMA((SEMAPHORES,))] * 2,
        compiler_params=pltpu.CompilerParams(
            collective_id=0, has_side_effects=True, vmem_limit_bytes=64 * 2**20 - 2**16
        ),
        name="layer",
    )(*(value for value, _ in inputs.values()))
    got = finish(types.SimpleNamespace(**dict(zip(outputs, results))), rows, heads)
    return (
        got.block_out[:, None],
        got.input_grad[:, None],
        got.attention_gain[0],
        got.query_gain[0],
        got.key_gain[0],
        got.out_q,
        got.out_k,
        got.out_v,
        got.out_o.T,
        got.feedforward_gain[0],
        got.out_g,
        got.out_u,
        got.out_d.T,
    )


def finish_kernel(names, heads, *refs):
    at = types.SimpleNamespace(**dict(zip(names, refs)))
    moved = [n[4:] for n in names if n.startswith("got_")]
    brought = [
        pltpu.make_async_copy(getattr(at, "got_" + n), getattr(at, "here_" + n), at.brought.at[i])
        for i, n in enumerate(moved)
    ]
    for copy in brought:
        copy.start()
    taken = []

    def take(name, source):
        copy = pltpu.make_async_copy(source, getattr(at, name), at.taken.at[len(taken)])
        copy.start()
        taken.append(copy)

    def ready(name):
        brought[moved.index(name)].wait()
        return getattr(at, "here_" + name)

    value = ready("input_grad")
    for m in range(MB):
        at.wide_grad[m] = value[m].astype(F32)
    take("input_grad", at.wide_grad)
    for name in moved:
        if name not in ("input_grad", "out_k"):
            take(name, ready(name))
    value = ready("out_k")
    at.keys[:, :KEYS] = value[:, :KEYS]
    at.keys[:, KEYS:] = value[:, KEYS + 128 : 2 * KEYS + 128]
    take("out_k", at.keys)
    gains = value[:, KEYS : KEYS + 128] + value[:, 2 * KEYS + 128 :]
    blank = jnp.zeros((128 - gains.shape[0], 128), F32)
    turned = jnp.concatenate([gains, blank], axis=0).T
    at.attention_gain[...] = turned[0:1, : gains.shape[0]]
    at.feedforward_gain[...] = turned[1:2, : gains.shape[0]]
    at.query_gain[...] = turned[2:3, :heads]
    at.key_gain[...] = turned[3:4, :heads]
    for copy in taken:
        copy.wait()


def finish(got, rows, heads):
    vmem, anywhere = pl.BlockSpec(memory_space=pltpu.VMEM), pl.BlockSpec(memory_space=pl.ANY)
    inputs = vars(got)
    outputs = {n: (v.shape, v.dtype, anywhere) for n, v in inputs.items()}
    outputs.update(
        input_grad=(got.input_grad.shape, F32, anywhere),
        out_k=((rows, 2 * KEYS), F32, anywhere),
        attention_gain=((1, rows), F32, vmem),
        feedforward_gain=((1, rows), F32, vmem),
        query_gain=((1, heads), F32, vmem),
        key_gain=((1, heads), F32, vmem),
    )
    scratch = {"here_" + n: (v.shape, v.dtype) for n, v in inputs.items()}
    scratch.update(wide_grad=(got.input_grad.shape, F32), keys=((rows, 2 * KEYS), F32))
    names = (*("got_" + n for n in inputs), *outputs, *scratch, "brought", "taken")
    results = pl.pallas_call(
        functools.partial(finish_kernel, names, heads),
        out_shape=[jax.ShapeDtypeStruct(shape, dtype) for shape, dtype, _ in outputs.values()],
        in_specs=[anywhere] * len(inputs),
        out_specs=[spec for _, _, spec in outputs.values()],
        scratch_shapes=[pltpu.VMEM(shape, dtype) for shape, dtype in scratch.values()]
        + [pltpu.SemaphoreType.DMA((len(inputs),))] * 2,
        compiler_params=pltpu.CompilerParams(vmem_limit_bytes=64 * 2**20 - 2**16),
        name="results",
    )(*inputs.values())
    return types.SimpleNamespace(**dict(zip(outputs, results)))


def rope_tables(first, count):
    angles = rope_angles(first, count)
    cosine = jnp.concatenate([jnp.cos(angles), jnp.cos(angles)], axis=-1)
    sine = jnp.concatenate([jnp.sin(angles), jnp.sin(angles)], axis=-1)
    return (cosine[:, None, :], sine[:, None, :])


def rotate(value, cosine, sine):
    half = value.shape[-1] // 2
    turned = jnp.concatenate([-value[..., half:], value[..., :half]], axis=-1)
    return value * cosine + turned * sine


def rotate_back(grad, cosine, sine):
    half = grad.shape[-1] // 2
    scaled = grad * sine
    return grad * cosine + jnp.concatenate([scaled[..., half:], -scaled[..., :half]], axis=-1)


def contract_last(left, right):
    return lax.dot_general(
        left, right, (((1,), (1,)), ((), ())), preferred_element_type=jnp.float32
    )


def contract_first(left, right):
    return lax.dot_general(
        left, right, (((0,), (0,)), ((), ())), preferred_element_type=jnp.float32
    )


def block_rows(rows):
    size = min(rows, 512)
    while rows % size:
        size -= 1
    return size


def over_blocks(state, pieces, update):
    rows = pieces[0].shape[0]
    size = block_rows(rows)
    count = rows // size
    stacked = tuple((piece.reshape((count, size) + piece.shape[1:]) for piece in pieces))
    offsets = size * jnp.arange(count, dtype=jnp.int32)

    def step(current, item):
        block = item[:-1]
        offset = item[-1]
        current = update(current, block, offset)
        return (current, None)

    final, unused = lax.scan(step, state, stacked + (offsets,))
    return final


def general(
    hidden_in,
    segments,
    attention_gain,
    query_gain,
    key_gain,
    query_weight,
    key_weight,
    value_weight,
    out_weight,
    feedforward_gain,
    gate_weight,
    up_weight,
    down_weight,
    cotangent,
):
    tokens = hidden_in.shape[2]
    groups = HQ // HK
    scale = HD ** (-0.5)
    first = lax.axis_index("ctx") * tokens
    length = lax.axis_size("ctx") * tokens
    query_pos = first + jnp.arange(tokens, dtype=jnp.int32)
    cosine, sine = rope_tables(first, tokens)
    sources = (
        query_weight,
        key_weight,
        value_weight,
        gate_weight,
        up_weight,
        out_weight.T,
        down_weight.T,
    )
    whole = lax.all_gather(jnp.concatenate(sources, axis=1), ("dp", "ctx"), axis=0, tiled=True)
    parts = []
    edge = 0
    for source in sources:
        parts.append(whole[:, edge : edge + source.shape[1]])
        edge = edge + source.shape[1]
    whole_query, whole_key, whole_value, whole_gate, whole_up, whole_out, whole_down = parts
    gain_in, gain_query, gain_key, gain_feed = (
        lax.all_gather(gain, ("dp", "ctx"), axis=0, tiled=True)
        for gain in (attention_gain, query_gain, key_gain, feedforward_gain)
    )
    grad_attention_gain = jnp.zeros((D,), jnp.float32)
    grad_feed_gain = jnp.zeros((D,), jnp.float32)
    grad_query_gain = jnp.zeros((HD,), jnp.float32)
    grad_key_gain = jnp.zeros((HD,), jnp.float32)
    outputs = []
    input_grads = []
    stored = []
    for batch in range(MB):
        hidden = hidden_in[batch, 0].astype(jnp.float32)
        query_seg = segments[batch, 0]
        grad_out = cotangent[batch, 0]
        normed = normalize(hidden)
        scaled_in = (normed * gain_in.astype(jnp.float32)).astype(jnp.bfloat16)
        query_heads = jnp.dot(scaled_in, whole_query, preferred_element_type=jnp.float32).reshape(
            tokens, HQ, HD
        )
        key_heads = jnp.dot(scaled_in, whole_key, preferred_element_type=jnp.float32).reshape(
            tokens, HK, HD
        )
        values = jnp.dot(scaled_in, whole_value, preferred_element_type=jnp.float32).astype(
            jnp.bfloat16
        )
        query_norm = normalize(query_heads)
        key_norm = normalize(key_heads)
        query_scale = gain_query.astype(jnp.float32)
        key_scale = gain_key.astype(jnp.float32)
        queries = rotate(query_norm * query_scale, cosine, sine).astype(jnp.bfloat16)
        keys_low = rotate(key_norm * key_scale, cosine, sine).astype(jnp.bfloat16)
        grouped = queries.reshape(tokens, HK, groups, HD)
        keys_flat = keys_low.reshape(tokens, HK * HD)

        def key_scores(keys, key_seg, offset):
            rows = keys.shape[0]
            shaped = keys.reshape(rows, HK, HD)
            raw = (
                jnp.einsum("qkgd,skd->kgqs", grouped, shaped, preferred_element_type=jnp.float32)
                * scale
            )
            key_pos = offset + jnp.arange(rows, dtype=jnp.int32)
            visible = (key_pos[None, :] <= query_pos[:, None]) & (
                key_seg[None, :] == query_seg[:, None]
            )
            return (jnp.where(visible, raw, MASKED), visible, shaped)

        def fold_with(update, state, pieces):
            return over_blocks(state, pieces, update)

        def add_lse(state, block, offset):
            keys, key_seg = block
            masked, visible, shaped = key_scores(keys, key_seg, offset)
            top, total = state
            new_top = jnp.maximum(top, jnp.max(masked, axis=-1))
            terms = jnp.where(visible, jnp.exp(masked - new_top[..., None]), 0.0)
            return (new_top, total * jnp.exp(top - new_top) + jnp.sum(terms, axis=-1))

        start_state = (
            jnp.full((HK, groups, tokens), MASKED, jnp.float32),
            jnp.zeros((HK, groups, tokens), jnp.float32),
        )
        top, total = fold_with(
            add_lse,
            start_state,
            (
                lax.all_gather(keys_flat, "ctx", axis=0, tiled=True),
                lax.all_gather(query_seg, "ctx", axis=0, tiled=True),
            ),
        )
        lse = top + jnp.log(total)

        def add_mixed(state, block, offset):
            keys, values_block, key_seg = block
            masked, visible, shaped = key_scores(keys, key_seg, offset)
            probs = jnp.exp(masked - lse[..., None]).astype(jnp.bfloat16)
            value_heads = values_block.reshape(values_block.shape[0], HK, HD)
            return state + jnp.einsum(
                "kgqs,skd->qkgd", probs, value_heads, preferred_element_type=jnp.float32
            )

        mixed = fold_with(
            add_mixed,
            jnp.zeros((tokens, HK, groups, HD), jnp.float32),
            (
                lax.all_gather(keys_flat, "ctx", axis=0, tiled=True),
                lax.all_gather(values, "ctx", axis=0, tiled=True),
                lax.all_gather(query_seg, "ctx", axis=0, tiled=True),
            ),
        )
        mixed_low = mixed.reshape(tokens, HQ * HD).astype(jnp.bfloat16)
        residual = hidden + contract_last(mixed_low, whole_out)
        feed_normed = normalize(residual)
        feed_scale = gain_feed.astype(jnp.float32)
        ff_in = (feed_normed * feed_scale).astype(jnp.bfloat16)
        gate = jnp.dot(ff_in, whole_gate, preferred_element_type=jnp.float32)
        up_part = jnp.dot(ff_in, whole_up, preferred_element_type=jnp.float32)
        sigmoid = jax.nn.sigmoid(gate)
        swish = gate * sigmoid
        hidden_low = (swish * up_part).astype(jnp.bfloat16)
        block_out = residual + contract_last(hidden_low, whole_down)
        outputs.append(block_out.astype(jnp.bfloat16))
        grad_hidden = jnp.dot(grad_out, whole_down, preferred_element_type=jnp.float32)
        grad_gate = (grad_hidden * up_part * (sigmoid * (1.0 + gate * (1.0 - sigmoid)))).astype(
            jnp.bfloat16
        )
        grad_up = (grad_hidden * swish).astype(jnp.bfloat16)
        grad_feed_in = contract_last(grad_gate, whole_gate) + contract_last(grad_up, whole_up)
        grad_feed_gain = grad_feed_gain + jnp.sum(grad_feed_in * feed_normed, axis=0)
        grad_residual = grad_out.astype(jnp.float32) + norm_back(
            residual, grad_feed_in * gain_feed.astype(jnp.float32)
        )
        grad_proj = grad_residual.astype(jnp.bfloat16)
        grad_mixed = (
            jnp.dot(grad_proj, whole_out, preferred_element_type=jnp.float32).astype(jnp.bfloat16).reshape(tokens, HK, groups, HD)
        )
        delta = jnp.transpose(jnp.sum(grad_mixed.astype(jnp.float32) * mixed, axis=-1), (1, 2, 0))

        def add_grads(state, block, offset):
            grad_query, grad_keys, grad_values = state
            keys, values_block, key_seg = block
            masked, visible, shaped = key_scores(keys, key_seg, offset)
            rows = keys.shape[0]
            probs = jnp.exp(masked - lse[..., None])
            probs_low = probs.astype(jnp.bfloat16)
            value_heads = values_block.reshape(rows, HK, HD)
            grad_probs = jnp.einsum(
                "qkgd,skd->kgqs", grad_mixed, value_heads, preferred_element_type=jnp.float32
            )
            grad_scores = (probs * (grad_probs - delta[..., None])).astype(jnp.bfloat16)
            grad_query = (
                grad_query
                + jnp.einsum(
                    "kgqs,skd->qkgd", grad_scores, shaped, preferred_element_type=jnp.float32
                )
                * scale
            )
            key_part = (
                jnp.einsum(
                    "kgqs,qkgd->skd", grad_scores, grouped, preferred_element_type=jnp.float32
                )
                * scale
            )
            value_part = jnp.einsum(
                "kgqs,qkgd->skd", probs_low, grad_mixed, preferred_element_type=jnp.float32
            )
            old_keys = lax.dynamic_slice_in_dim(grad_keys, offset, rows, 0)
            grad_keys = lax.dynamic_update_slice_in_dim(
                grad_keys, old_keys + key_part.reshape(rows, HK * HD), offset, 0
            )
            old_values = lax.dynamic_slice_in_dim(grad_values, offset, rows, 0)
            grad_values = lax.dynamic_update_slice_in_dim(
                grad_values, old_values + value_part.reshape(rows, HK * HD), offset, 0
            )
            return (grad_query, grad_keys, grad_values)

        back_state = (
            jnp.zeros((tokens, HK, groups, HD), jnp.float32),
            jnp.zeros((length, HK * HD), jnp.float32),
            jnp.zeros((length, HK * HD), jnp.float32),
        )
        grad_query, grad_keys_all, grad_values_all = fold_with(
            add_grads,
            back_state,
            (
                lax.all_gather(keys_flat, "ctx", axis=0, tiled=True),
                lax.all_gather(values, "ctx", axis=0, tiled=True),
                lax.all_gather(query_seg, "ctx", axis=0, tiled=True),
            ),
        )
        grad_keys_own, grad_values_own = (
            lax.psum_scatter(
                grad_keys_all.astype(jnp.bfloat16), "ctx", scatter_dimension=0, tiled=True
            ).astype(jnp.float32),
            lax.psum_scatter(
                grad_values_all.astype(jnp.bfloat16), "ctx", scatter_dimension=0, tiled=True
            ).astype(jnp.float32),
        )
        turned_query = rotate_back(grad_query.reshape(tokens, HQ, HD), cosine, sine)
        grad_query_gain = grad_query_gain + jnp.sum(turned_query * query_norm, axis=(0, 1))
        grad_query_low = (
            norm_back(query_heads, turned_query * gain_query.astype(jnp.float32))
            .reshape(tokens, HQ * HD)
            .astype(jnp.bfloat16)
        )
        turned_key = rotate_back(grad_keys_own.reshape(tokens, HK, HD), cosine, sine)
        grad_key_gain = grad_key_gain + jnp.sum(turned_key * key_norm, axis=(0, 1))
        grad_key_low = (
            norm_back(key_heads, turned_key * gain_key.astype(jnp.float32))
            .reshape(tokens, HK * HD)
            .astype(jnp.bfloat16)
        )
        grad_value_low = grad_values_own.astype(jnp.bfloat16)
        grad_scaled_in = (
            contract_last(grad_query_low, whole_query)
            + contract_last(grad_key_low, whole_key)
            + contract_last(grad_value_low, whole_value)
        )
        grad_attention_gain = grad_attention_gain + jnp.sum(grad_scaled_in * normed, axis=0)
        input_grads.append(
            grad_residual + norm_back(hidden, grad_scaled_in * gain_in.astype(jnp.float32))
        )
        stored.append(
            (
                scaled_in,
                grad_query_low,
                grad_key_low,
                grad_value_low,
                ff_in,
                grad_gate,
                grad_up,
                grad_proj,
                mixed_low,
                grad_out,
                hidden_low,
            )
        )
    columns = [jnp.concatenate([entry[index] for entry in stored], axis=0) for index in range(11)]
    (
        all_in,
        all_query,
        all_key,
        all_value,
        all_feed,
        all_gate,
        all_up,
        all_proj,
        all_mixed,
        all_out,
        all_hidden,
    ) = columns
    rows = query_weight.shape[0]
    head_rows = query_gain.shape[0]
    count = lax.axis_size(("dp", "ctx")) * rows
    row_ids = jnp.arange(count, dtype=jnp.int32)
    local = row_ids % rows
    place = jnp.clip(row_ids // rows * head_rows + local, 0, HD - 1)
    owned = local < head_rows
    gains = jnp.stack(
        [
            grad_attention_gain,
            grad_feed_gain,
            jnp.where(owned, jnp.take(grad_query_gain, place), 0.0),
            jnp.where(owned, jnp.take(grad_key_gain, place), 0.0),
        ],
        axis=1,
    )
    summed = lax.psum_scatter(
        jnp.concatenate(
            [
                contract_first(all_in, all_query).astype(BF),
                contract_first(all_in, all_key).astype(BF),
                contract_first(all_in, all_value).astype(BF),
                contract_first(all_feed, all_gate).astype(BF),
                contract_first(all_feed, all_up).astype(BF),
                contract_first(all_proj, all_mixed).astype(BF),
                contract_first(all_out, all_hidden).astype(BF),
                gains.astype(BF),
                jnp.zeros((count, 124), BF),
            ],
            axis=1,
        ),
        ("dp", "ctx"),
        scatter_dimension=0,
        tiled=True,
    ).astype(F32)
    widths = [HQ * HD, HK * HD, HK * HD, FF, FF, HQ * HD, FF, 128]
    pieces = []
    edge = 0
    for width in widths:
        pieces.append(summed[:, edge : edge + width])
        edge = edge + width
    gain_block = pieces[7]
    block_out = jnp.stack(outputs)[:, None]
    input_grad = jnp.stack(input_grads)[:, None]
    return (
        block_out,
        input_grad,
        gain_block[:, 0],
        gain_block[:head_rows, 2],
        gain_block[:head_rows, 3],
        pieces[0],
        pieces[1],
        pieces[2],
        pieces[5].T,
        gain_block[:, 1],
        pieces[3],
        pieces[4],
        pieces[6].T,
    )


def solution(mesh):
    shape = dict(mesh.shape)
    chips_hold_sequences = shape["dp"] == 4 and shape["ctx"] == 8

    def step(*arrays):
        if chips_hold_sequences and arrays[0].shape[2] == 64:
            return fused(*arrays)
        return general(*arrays)

    return jax.shard_map(
        step,
        mesh=mesh,
        in_specs=(
            P(None, "dp", "ctx", None),
            P(None, "dp", "ctx"),
            P(("dp", "ctx")),
            P(("dp", "ctx")),
            P(("dp", "ctx")),
            P(("dp", "ctx"), None),
            P(("dp", "ctx"), None),
            P(("dp", "ctx"), None),
            P(None, ("dp", "ctx")),
            P(("dp", "ctx")),
            P(("dp", "ctx"), None),
            P(("dp", "ctx"), None),
            P(None, ("dp", "ctx")),
            P(None, "dp", "ctx", None),
        ),
        out_specs=(
            P(None, "dp", "ctx", None),
            P(None, "dp", "ctx", None),
            P(("dp", "ctx")),
            P(("dp", "ctx")),
            P(("dp", "ctx")),
            P(("dp", "ctx"), None),
            P(("dp", "ctx"), None),
            P(("dp", "ctx"), None),
            P(None, ("dp", "ctx")),
            P(("dp", "ctx")),
            P(("dp", "ctx"), None),
            P(("dp", "ctx"), None),
            P(None, ("dp", "ctx")),
        ),
        check_vma=False,
    )
```
